512 devices in a mesh: pair: 64 (over z, x, y_lo), grp: 8 (over y_hi, core).
Axes of the slice: x: 4, y: 8 (y_hi: 4, y_lo: 2; y = y_hi * 2 + y_lo), z: 8, core: 2. Of those that a mesh axis runs over, the one named last changes fastest.
Arguments:
- c_occ: bfloat16 [768, 8], replicated, may hold values from -0.75 to 0.75
- c_vir: bfloat16 [768, 2048], replicated, may hold values from -0.125 to 0.125
- ints: bfloat16 [32, 2048, 4096], P('grp', 'pair'), may hold values from -4 to 4
- blocks: int32 [32, 2], P('grp'), may hold values from 0 to 11
- screen: int32 [32], P('grp'), may hold values 0 or 1
- eps_occ: float32 [8], replicated, may hold values from -1.5 to -0.4
- eps_vir: float32 [2048], replicated, may hold values from 0.3 to 3.2
Outputs:
- bmat: bfloat16 [8, 2048, 2048], P('grp', 'pair')
- pair_energy: float32 [8, 8], replicated
The draws below stay inside these ranges and needn't reach their ends.
All inputs are finite; a program needn't handle non-finite values. No bound on the sum of `screen` on one device may be relied on, other than what follows from the above.
Results may differ from the reference program's by a relative error of at most 0.001.
Values may be sent and summed in bfloat16 or wider, within the bound.
No kernel may reach another device: no remote copies, remote signals or barrier semaphores. Data moves between devices by JAX's collectives and lax.ppermute only.
A program may use at most 64 MiB of HBM per device.

```python
import math
import jax
import jax.numpy as jnp
from jax import lax

SHELL = 64
NSB = 12
VIR = 2048
NAUX = 2048
OCC = 8
NPB = 32
NBF = 768


def draw_eps_vir(key, part):
    key = jax.random.fold_in(key, 7)
    ramp = 0.3 + 2.7 * jnp.arange(VIR, dtype=jnp.float32) / float(VIR)
    noise = 0.2 * jax.random.uniform(key, (VIR,), jnp.float32)
    return ramp + noise


def draw_ints(key, part):
    key = jax.random.fold_in(key, 11)
    rank = max(NAUX // 8, 4)
    key_aux, key_block = jax.random.split(key)
    factor = jax.random.normal(key_aux, (NAUX, rank), jnp.float32)
    share = 0.75

    def one_block(index):
        block_key = jax.random.fold_in(key_block, index)
        key_load, key_spread, key_noise = jax.random.split(block_key, 3)
        loadings = jax.random.normal(key_load, (rank, SHELL * SHELL), jnp.float32)
        noise = jax.random.normal(key_noise, (NAUX, SHELL * SHELL), jnp.float32)
        spread = jnp.exp(jax.random.uniform(key_spread, (rank, 1), jnp.float32, math.log(0.3), math.log(3.0))) / math.sqrt(1.935)
        coherent = jnp.dot(factor, loadings * spread, precision=lax.Precision.HIGHEST) / math.sqrt(float(rank))
        values = math.sqrt(share) * coherent + math.sqrt(1.0 - share) * noise
        return jnp.clip(values, -4.0, 4.0).astype(jnp.bfloat16)
    return lax.map(one_block, jnp.arange(NPB, dtype=jnp.int32))


def set_ends(array, own_key, low, high):
    extent = array.shape
    index_at = [jax.random.randint(jax.random.fold_in(own_key, axis), (), 0, extent[axis]) for axis in range(len(extent))]
    array = array.at[tuple(index_at)].set(low)
    longest = extent.index(max(extent))
    index_at[longest] = (index_at[longest] + 1) % extent[longest]
    return array.at[tuple(index_at)].set(high)


def centred(stream_key, shape, deviation, bound, kind=jnp.bfloat16):
    result = deviation * jax.random.normal(stream_key, shape, jnp.float32)
    return jnp.clip(result, min=-bound, max=bound).astype(kind)


def setup_inputs(seed: int = 0) -> dict:
    key_of = jax.random.split(jax.random.key(seed), 8)
    c_occ = centred(key_of[0], (NBF, OCC), SHELL ** -0.5, 0.75)
    c_vir = centred(key_of[1], (NBF, VIR), (SHELL * NPB) ** -0.5, 0.125)
    ints = draw_ints(jax.random.fold_in(key_of[7], 71), 0)
    blocks = set_ends(jax.random.randint(key_of[3], (NPB, 2), 0, NSB), jax.random.fold_in(key_of[3], 1), 0, NSB - 1).astype(jnp.int32)
    screen = set_ends((jax.random.randint(key_of[4], (NPB,), 0, 3) < 2).astype(jnp.int32), jax.random.fold_in(key_of[4], 1), 0, 1)
    eps_occ = jnp.clip(jax.random.uniform(key_of[5], (OCC,), jnp.float32, -1.5, -0.4), -1.5, -0.4)
    eps_vir = draw_eps_vir(jax.random.fold_in(key_of[7], 71), 0)
    return dict(c_occ=c_occ, c_vir=c_vir, ints=ints, blocks=blocks, screen=screen, eps_occ=eps_occ, eps_vir=eps_vir)


def transform(c_occ, c_vir, ints, blocks, screen):
    def add_block(block_index, running):
        block_index = jnp.asarray(block_index).astype(jnp.int32)
        start_occ = (blocks[block_index, 0] * SHELL).astype(jnp.int32)
        start_vir = (blocks[block_index, 1] * SHELL).astype(jnp.int32)
        rows_occ = lax.dynamic_slice_in_dim(c_occ, start_occ, SHELL, 0).astype(jnp.float32)
        rows_vir = lax.dynamic_slice_in_dim(c_vir, start_vir, SHELL, 0).astype(jnp.float32)
        int_block = ints[block_index].astype(jnp.float32).reshape(NAUX, SHELL, SHELL)
        half_done = jnp.einsum('pmn,mi->ipn', int_block, rows_occ, precision=lax.Precision.HIGHEST)
        vir_done = jnp.einsum('ipn,na->ipa', half_done, rows_vir, precision=lax.Precision.HIGHEST)
        return running + screen[block_index].astype(jnp.float32) * vir_done

    return lax.fori_loop(0, NPB, add_block, jnp.zeros((OCC, NAUX, VIR), jnp.float32))


def reference(c_occ, c_vir, ints, blocks, screen, eps_occ, eps_vir):
    bmat = transform(c_occ, c_vir, ints, blocks, screen).astype(jnp.bfloat16)
    scale_factor = 1.0 / (float(VIR) * float(VIR) * float(NAUX))
    positions = jnp.arange(OCC, dtype=jnp.int32)

    def pair_row(first):
        def one_pair(second):
            amplitude = lax.dot_general(bmat[first], bmat[second], (((0,), (0,)), ((), ())), preferred_element_type=jnp.float32)
            denominators = eps_occ[first] + eps_occ[second] - eps_vir[:, None] - eps_vir[None, :]
            terms = amplitude * (2.0 * amplitude - amplitude.T) / denominators
            return jnp.sum(terms) * scale_factor

        return lax.map(one_pair, positions)

    pair_energy = lax.map(pair_row, positions)
    return bmat, pair_energy
```

```python
import jax
import jax.numpy as jnp
from jax import lax
from jax.sharding import Mesh, PartitionSpec as P

SHELL = 64
AXES = ("z", "x", "yl", "yh", "core")
PAIR = ("z", "x", "yl")
GRP = ("yh", "core")
TILES = 16
F32 = jnp.float32
BF16 = jnp.bfloat16


def split3(x):
    a = lax.reduce_precision(x, 8, 7)
    b = lax.reduce_precision(x - a, 8, 7)
    c = x - a - b
    return a.astype(BF16), b.astype(BF16), c.astype(BF16)


def half_transform(c_occ, ints, blocks, screen):
    nblk, rows, _ = ints.shape
    occ = c_occ.shape[1]
    coef = jnp.stack(
        [lax.dynamic_slice_in_dim(c_occ, blocks[b, 0] * SHELL, SHELL, 0) for b in range(nblk)]
    )
    coef = coef * screen.astype(BF16)[:, None, None]
    half = jnp.einsum(
        "bpmn,bmi->ibpn",
        ints.reshape(nblk, rows, SHELL, SHELL),
        coef,
        preferred_element_type=F32,
    )
    half = half.reshape(occ, nblk, rows // 2, 2 * SHELL).reshape(occ, -1, 128)
    where = jnp.broadcast_to(blocks[:, 1].astype(F32)[:, None, None], (nblk, 2, 128))
    where = jnp.broadcast_to(where.reshape(1, 2 * nblk, 128), (occ, 2 * nblk, 128))
    return jnp.concatenate([half, where], axis=1)


def transform(recv, c_vir, nblk, rows):
    sources = recv.shape[0]
    half = recv[:, : nblk * rows // 2].reshape(sources * nblk, rows, SHELL)
    shell = recv[:, nblk * rows // 2 :: 2, 0].reshape(sources * nblk)
    count = c_vir.shape[0] // SHELL
    onehot = (shell[None, :] == jnp.arange(count, dtype=F32)[:, None]).astype(F32)
    summed = jnp.einsum("nb,bpm->pnm", onehot, half, precision=lax.Precision.HIGHEST)
    summed = summed.reshape(rows, count * SHELL)
    terms = jnp.concatenate(split3(summed), axis=0)
    full = jnp.dot(terms, c_vir, preferred_element_type=F32)
    full = full[2 * rows :] + full[rows : 2 * rows] + full[:rows]
    return full.astype(BF16)


def outgoing(bmat):
    rows = bmat.shape[0]
    tiles = bmat.reshape(2, rows // 2, TILES, 128).transpose(2, 0, 1, 3)
    first = jnp.broadcast_to(tiles[:, None], (TILES, TILES, 2, rows // 2, 128))
    halves = bmat.reshape(2, 2, rows // 4, TILES, 2, 64).transpose(3, 4, 0, 2, 1, 5)
    halves = halves.reshape(TILES, 2, 2, rows // 4, 128)
    second = jnp.stack([jnp.roll(halves, -k, axis=0) for k in range(1, 9)], axis=1)
    second = second.reshape(TILES, TILES, 2, rows // 4, 128)
    return jnp.concatenate([first, second], axis=3).reshape(512, 3 * rows // 4, 128)


def energies(recv, eps_occ, eps_vir):
    occ = eps_occ.shape[0]
    rows = recv.shape[1] // 3
    recv = recv.reshape(-1, occ, 3 * rows, 128)
    chip = ((lax.axis_index("z") * 4 + lax.axis_index("x")) * 2 + lax.axis_index("yl")) * 4 + lax.axis_index("yh")
    tile, kind = chip // TILES, chip % TILES
    step, side = kind // 2 + 1, kind % 2
    core = lax.axis_index("core")

    x0, x1 = recv[:, :, :rows], recv[:, :, rows : 2 * rows]
    y0, y1 = recv[:, :, 2 * rows :, :64], recv[:, :, 2 * rows :, 64:]
    cross = jnp.einsum("piqa,pjqb->iajb", x0, y0, preferred_element_type=F32)
    cross = cross + jnp.einsum("piqa,pjqb->iajb", x1, y1, preferred_element_type=F32)

    own_i = kind // 2
    panel = recv[:, :, : 2 * rows]
    mine = lax.dynamic_index_in_dim(panel, own_i, 1, keepdims=False)
    others = lax.dynamic_slice_in_dim(panel, (kind % 2) * 4, 4, 1)
    selfs = jnp.einsum("pqa,pjqb->jab", mine, others, preferred_element_type=F32)

    cross = cross.reshape(occ, 2, 64, occ, 64)
    selfs = selfs.reshape(2, 2, 128, 128)
    give_cross = lax.dynamic_index_in_dim(cross, 1 - core, 1, keepdims=False)
    give_self = lax.dynamic_index_in_dim(selfs, 1 - core, 0, keepdims=False)
    give = jnp.concatenate([give_cross.reshape(-1, 128), give_self.reshape(-1, 128)], axis=0)
    got = lax.ppermute(give, "core", [(0, 1), (1, 0)])
    cross = lax.dynamic_index_in_dim(cross, core, 1, keepdims=False)
    split = occ * 64 * occ * 64 // 128
    cross = cross + got[:split].reshape(cross.shape)
    selfs = lax.dynamic_index_in_dim(selfs, core, 0, keepdims=False)
    selfs = selfs + got[split:].reshape(selfs.shape)

    eps_a = lax.dynamic_slice_in_dim(eps_vir, tile * 128 + core * 64, 64, 0)
    other = (tile + step) % TILES
    eps_b = lax.dynamic_slice_in_dim(eps_vir, other * 128 + side * 64, 64, 0)
    pair_sum = eps_occ[:, None] + eps_occ[None, :]
    denominators = pair_sum[:, None, :, None] - eps_a[None, :, None, None] - eps_b[None, None, None, :]
    flipped = cross.transpose(2, 1, 0, 3)
    terms = cross * (2.0 * cross - flipped) / denominators
    one_way = jnp.sum(terms, axis=(1, 3))
    weight = jnp.where(step == 8, 0.5, 1.0).astype(F32)
    energy = (one_way + one_way.T) * weight

    eps_t = lax.dynamic_slice_in_dim(eps_vir, tile * 128, 128, 0)
    first_j = (kind % 2) * 4 + core * 2
    e_pair = lax.dynamic_index_in_dim(eps_occ, own_i, 0, keepdims=False) + lax.dynamic_slice_in_dim(eps_occ, first_j, 2, 0)
    denominators = e_pair[:, None, None] - eps_t[None, :, None] - eps_t[None, None, :]
    self_sum = jnp.sum(selfs * (2.0 * selfs - selfs.transpose(0, 2, 1)) / denominators, axis=(1, 2))
    positions = jnp.arange(occ, dtype=jnp.int32)
    row = (positions == own_i).astype(F32)
    cols = (positions[None, :] == first_j + jnp.arange(2)[:, None]).astype(F32)
    return energy + row[:, None] * jnp.sum(cols * self_sum[:, None], axis=0)[None, :]


def sum_over(x, axes, count):
    got = lax.all_to_all(jnp.broadcast_to(x[None], (count,) + x.shape), axes, 0, 0, tiled=True)
    return jnp.sum(got, axis=0)


def body(c_occ, c_vir, ints, blocks, screen, eps_occ, eps_vir):
    nblk, rows, _ = ints.shape
    vir = c_vir.shape[1]
    sent = half_transform(c_occ, ints, blocks, screen)
    recv = lax.all_to_all(sent, GRP, 0, 0, tiled=True)
    bmat = transform(recv, c_vir, nblk, rows)
    panels = lax.all_to_all(outgoing(bmat), AXES, 0, 0, tiled=True)
    energy = energies(panels, eps_occ, eps_vir)
    scale = 1.0 / (float(vir) * float(vir) * float(rows * 64))
    energy = (energy * scale).reshape(1, -1)
    energy = sum_over(energy, ("z", "x"), 32)
    energy = sum_over(energy, ("yh", "yl", "core"), 16)
    occ = eps_occ.shape[0]
    return bmat[None], energy.reshape(occ, occ)


def solution(mesh):
    fine = Mesh(mesh.devices.reshape(8, 4, 2, 4, 2), AXES)
    return jax.shard_map(
        body,
        mesh=fine,
        in_specs=(P(), P(), P(GRP, PAIR, None), P(GRP, None), P(GRP), P(), P()),
        out_specs=(P(GRP, PAIR, None), P()),
        check_vma=False,
    )
```

```python
import functools

import jax
import jax.numpy as jnp
from jax import lax
from jax.experimental import pallas as pl
from jax.experimental.pallas import tpu as pltpu
from jax.sharding import Mesh, PartitionSpec as P

SHELL = 64
SHELLS = 12
TILES = 16
AXES = ("z", "x", "yl", "yh", "core")
CHIPS = ("z", "x", "yl", "yh")
PAIR = ("z", "x", "yl")
GRP = ("yh", "core")
F32 = jnp.float32
BF16 = jnp.bfloat16
VMEM = pl.BlockSpec(memory_space=pltpu.VMEM)
SMEM = pl.BlockSpec(memory_space=pltpu.SMEM)
PARAMS = pltpu.CompilerParams(vmem_limit_bytes=40 * 1024 * 1024)
TRANSPOSED = (((0,), (0,)), ((), ()))


def lanes(shape):
    return lax.broadcasted_iota(jnp.int32, shape, 1)


def rows(shape):
    return lax.broadcasted_iota(jnp.int32, shape, 0)


def half_kernel(blocks, screen, c_occ, ints, out, spread, coef):
    block = pl.program_id(0)

    @pl.when(block == 0)
    def _():
        shape = (SHELL, 4096)
        spread[...] = (lanes(shape) // SHELL == rows(shape)).astype(F32).astype(BF16)

    start = pl.multiple_of(blocks[block, 0] * SHELL, SHELL)
    own = c_occ[pl.ds(start, SHELL), :]
    wide = lax.dot_general(own, spread[...], TRANSPOSED, preferred_element_type=F32)
    coef[...] = wide * screen[block].astype(F32)

    def step(t, sums):
        at = pl.multiple_of(t * 128, 128)
        tile = ints[0, :, pl.ds(at, 128)].astype(F32)
        weights = coef[:, pl.ds(at, 128)]
        return tuple(sums[i] + tile * weights[i : i + 1] for i in range(8))

    sums = lax.fori_loop(0, 32, step, (jnp.zeros((32, 128), F32),) * 8, unroll=8)
    left = lanes((32, 128)) < SHELL
    full = [s + pltpu.roll(s, SHELL, 1) for s in sums]
    shell = blocks[block, 1].astype(F32)
    put = pl.multiple_of(block * 16, 16)
    for yh in range(4):
        both = jnp.where(left, full[2 * yh], full[2 * yh + 1])
        for core in range(2):
            d = yh * 2 + core
            out[d, pl.ds(put, 16), :] = both[core * 16 : core * 16 + 16]
            out[d, 64:72, :] = jnp.where(rows((8, 128)) == block, shell, out[d, 64:72, :])


def half_transform(c_occ, ints, blocks, screen):
    count = ints.shape[0]
    return pl.pallas_call(
        half_kernel,
        out_shape=jax.ShapeDtypeStruct((8, 72, 128), F32),
        grid=(count,),
        in_specs=[
            SMEM,
            SMEM,
            pl.BlockSpec(c_occ.shape, lambda b: (0, 0)),
            pl.BlockSpec((1,) + ints.shape[1:], lambda b: (b, 0, 0)),
        ],
        out_specs=pl.BlockSpec((8, 72, 128), lambda b: (0, 0, 0)),
        scratch_shapes=[pltpu.VMEM((SHELL, 4096), BF16), pltpu.VMEM((8, 4096), F32)],
        compiler_params=PARAMS,
        name="half",
    )(blocks, screen, c_occ, ints)


def rounded(x):
    return x.astype(BF16).astype(F32)


def transform_kernel(recv, c_vir, bmat, out, terms, sides):
    left = lanes((16, 128)) < SHELL
    sums = [jnp.zeros((16, 128), F32) for _ in range(SHELLS)]
    for source in range(8):
        for b in range(4):
            data = recv[source, b * 16 : b * 16 + 16, :]
            shell = recv[source, 64 + b : 65 + b, :]
            for n in range(SHELLS):
                sums[n] = sums[n] + jnp.where(shell == float(n), data, 0.0)
    for m in range(SHELLS // 2):
        one, two = sums[2 * m], sums[2 * m + 1]
        pair = (
            jnp.where(left, one, pltpu.roll(two, SHELL, 1)),
            jnp.where(left, pltpu.roll(one, SHELL, 1), two),
        )
        for i in range(2):
            value = pair[i]
            for term in range(3):
                part = rounded(value)
                terms[term * 32 + i * 16 : term * 32 + i * 16 + 16, m * 128 : m * 128 + 128] = part.astype(BF16)
                value = value - part
    for q in range(TILES // 2):
        got = jnp.dot(terms[...], c_vir[:, q * 256 : q * 256 + 256], preferred_element_type=F32)
        full = (got[64:96] + got[32:64]) + got[0:32]
        bmat[:, q * 256 : q * 256 + 256] = full.astype(BF16)
        for t in range(2):
            one, two = full[0:16, t * 128 : t * 128 + 128], full[16:32, t * 128 : t * 128 + 128]
            tile = q * 2 + t
            sides[tile * 2] = jnp.where(left, one, pltpu.roll(two, SHELL, 1)).astype(BF16)
            sides[tile * 2 + 1] = jnp.where(left, pltpu.roll(one, SHELL, 1), two).astype(BF16)
    for r in range(TILES):
        for kind in range(TILES):
            other = (r + kind // 2 + 1) % TILES
            out[r * TILES + kind, 0:32, :] = bmat[:, r * 128 : r * 128 + 128]
            out[r * TILES + kind, 32:48, :] = sides[other * 2 + kind % 2]


def transform(recv, c_vir):
    return pl.pallas_call(
        transform_kernel,
        out_shape=(
            jax.ShapeDtypeStruct((32, c_vir.shape[1]), BF16),
            jax.ShapeDtypeStruct((256, 48, 128), BF16),
        ),
        in_specs=[VMEM, VMEM],
        out_specs=(VMEM, VMEM),
        scratch_shapes=[pltpu.VMEM((96, c_vir.shape[0]), BF16), pltpu.VMEM((32, 16, 128), BF16)],
        compiler_params=PARAMS,
        name="transform",
    )(recv, c_vir)


def gram_kernel(place, panels, keep, give, wide, all_t, all_s):
    core, side, own = place[4], place[3], place[5]
    for i in range(8):
        wide[:, i * 128 : i * 128 + 128] = panels[:, (i // 2) * 3 + i % 2].reshape(1024, 128)
    for p in range(4):
        thin = panels[:, p * 3 + 2].reshape(1024, 128)
        all_t[p * 128 : p * 128 + 128, :] = lax.dot_general(thin, wide[...], TRANSPOSED, preferred_element_type=F32)
    mine = panels[:, (own // 2) * 3 + own % 2].reshape(1024, 128)
    others = wide[:, pl.ds(pl.multiple_of(side * 512, 512), 512)]
    all_s[...] = lax.dot_general(mine, others, TRANSPOSED, preferred_element_type=F32)
    for which, target in ((core, keep), (1 - core, give)):
        for j in range(8):
            at = pl.multiple_of(j * 64 + which * 32, 32)
            target[j * 32 : j * 32 + 32, :] = all_t[pl.ds(at, 32), :]
        for q in range(4):
            at = pl.multiple_of(which * 256, 256)
            target[256:288, q * 256 : q * 256 + 256] = all_s[q * 32 : q * 32 + 32, pl.ds(at, 256)]


def gram(place, panels):
    shape = jax.ShapeDtypeStruct((288, 1024), F32)
    return pl.pallas_call(
        gram_kernel,
        out_shape=(shape, shape),
        in_specs=[SMEM, VMEM],
        out_specs=(VMEM, VMEM),
        scratch_shapes=[
            pltpu.VMEM((1024, 1024), BF16),
            pltpu.VMEM((512, 1024), F32),
            pltpu.VMEM((128, 512), F32),
        ],
        compiler_params=PARAMS,
        name="gram",
    )(place, panels.reshape(64, 12, 16, 128))


def energy_kernel(scale, place, eps_occ, keep, got, eps_vir, out, parts):
    tile, other, step, side, core, own = (place[n] for n in range(6))
    row_a = eps_vir[pl.ds(tile, 1), :]
    row_b = eps_vir[pl.ds(other, 1), :]
    first = side * 64 + core * 32
    col_b = jnp.sum(jnp.where(lanes((32, 128)) == rows((32, 128)) + first, row_b, 0.0), axis=1, keepdims=True)
    weight = jnp.where(step == 8, 1.0, 2.0)
    for i in range(8):
        for j in range(i, 8):
            there = slice(j * 32, j * 32 + 32), slice(i * 128, i * 128 + 128)
            here = slice(i * 32, i * 32 + 32), slice(j * 128, j * 128 + 128)
            one = keep[there] + got[there]
            two = keep[here] + got[here]
            denominators = (eps_occ[i] + eps_occ[j] - row_a) - col_b
            terms = (one * one + two * two - one * two) / denominators
            part = jnp.sum(terms, axis=0, keepdims=True) * weight
            parts[i * 8 + j : i * 8 + j + 1, :] = part
            parts[j * 8 + i : j * 8 + i + 1, :] = part
    square = (128, 128)
    eye = lanes(square) == rows(square)
    col_a = jnp.sum(jnp.where(eye, row_a, 0.0), axis=1, keepdims=True)
    for m in range(2):
        j = side * 4 + core * 2 + m
        block = jnp.concatenate(
            [
                keep[256:288, q * 256 + m * 128 : q * 256 + m * 128 + 128]
                + got[256:288, q * 256 + m * 128 : q * 256 + m * 128 + 128]
                for q in range(4)
            ],
            axis=0,
        )
        denominators = (eps_occ[own] + eps_occ[j] - row_a) - col_a
        terms = block * (2.0 * block - block.T) / denominators
        at = pl.ds(own * 8 + j, 1)
        parts[at, :] = parts[at, :] + jnp.sum(terms, axis=0, keepdims=True)
    column = jnp.sum(parts[...], axis=1, keepdims=True) * scale
    out[...] = jnp.sum(jnp.where(lanes((64, 128)) == rows((64, 128)), column, 0.0), axis=0, keepdims=True)


def energies(scale, place, eps_occ, keep, got, eps_vir):
    return pl.pallas_call(
        functools.partial(energy_kernel, scale),
        out_shape=jax.ShapeDtypeStruct((1, 128), F32),
        in_specs=[SMEM, SMEM, VMEM, VMEM, VMEM],
        out_specs=VMEM,
        scratch_shapes=[pltpu.VMEM((64, 128), F32)],
        compiler_params=PARAMS,
        name="energies",
    )(place, eps_occ, keep, got, eps_vir.reshape(-1, 128))


def sum_over(x, axes, count):
    got = lax.all_to_all(jnp.broadcast_to(x[None], (count,) + x.shape), axes, 0, 0, tiled=True)
    return jnp.sum(got, axis=0)


def position():
    chip = lax.axis_index(CHIPS)
    tile, kind = chip // TILES, chip % TILES
    step, side = kind // 2 + 1, kind % 2
    return jnp.stack([tile, (tile + step) % TILES, step, side, lax.axis_index("core"), kind // 2])


def body(c_occ, c_vir, ints, blocks, screen, eps_occ, eps_vir):
    vir, occ = c_vir.shape[1], c_occ.shape[1]
    place = position()
    core = lax.axis_index("core")
    swap = [(0, 1), (1, 0)]
    sent = half_transform(c_occ, ints, blocks, screen)
    recv = lax.all_to_all(sent, GRP, 0, 0, tiled=True)
    two, operand = transform(recv, c_vir)
    panels = lax.all_to_all(operand, CHIPS, 0, 0, tiled=True)

    two = two.reshape(2, 16, vir)
    mine = lax.dynamic_index_in_dim(two, core, 0, keepdims=False)
    others = lax.ppermute(lax.dynamic_index_in_dim(two, 1 - core, 0, keepdims=False), "core", swap)
    bmat = jnp.where(core == 0, jnp.stack([mine, others]), jnp.stack([others, mine]))

    keep, give = gram(place, panels)
    got = lax.ppermute(give, "core", swap)
    scale = 1.0 / (float(vir) * float(vir) * 2048.0)
    energy = energies(scale, place, eps_occ, keep, got, eps_vir)
    energy = sum_over(energy, ("z", "x"), 32)
    energy = sum_over(energy, ("yh", "yl", "core"), 16)
    return bmat.reshape(1, 32, vir), energy[:, : occ * occ].reshape(occ, occ)


def solution(mesh):
    fine = Mesh(mesh.devices.reshape(8, 4, 2, 4, 2), AXES)
    return jax.shard_map(
        body,
        mesh=fine,
        in_specs=(P(), P(), P(GRP, PAIR, None), P(GRP, None), P(GRP), P(), P()),
        out_specs=(P(GRP, PAIR, None), P()),
        check_vma=False,
    )
```

```python
import functools

import jax
import jax.numpy as jnp
from jax import lax
from jax.experimental import pallas as pl
from jax.experimental.pallas import tpu as pltpu
from jax.sharding import Mesh, PartitionSpec as P

SHELL = 64
SHELLS = 12
TILES = 16
AXES = ("z", "x", "yl", "yh", "core")
CHIPS = ("z", "x", "yl", "yh")
PAIR = ("z", "x", "yl")
GRP = ("yh", "core")
F32 = jnp.float32
BF16 = jnp.bfloat16
VMEM = pl.BlockSpec(memory_space=pltpu.VMEM)
SMEM = pl.BlockSpec(memory_space=pltpu.SMEM)
HBM = pl.BlockSpec(memory_space=pltpu.HBM)
TRANSPOSED = (((0,), (0,)), ((), ()))


def lanes(shape):
    return lax.broadcasted_iota(jnp.int32, shape, 1)


def grant(mib):
    return pltpu.CompilerParams(vmem_limit_bytes=mib * 1024 * 1024)


def rows(shape):
    return lax.broadcasted_iota(jnp.int32, shape, 0)


def half_kernel(blocks, screen, c_occ, ints, out, held, spread, coef, sems):
    count = held.shape[0]
    for b in range(count):
        pltpu.make_async_copy(ints.at[b], held.at[b], sems.at[b]).start()
    shape = (SHELL, 4096)
    spread[...] = (lanes(shape) // SHELL == rows(shape)).astype(F32).astype(BF16)
    left = lanes((32, 128)) < SHELL

    @pl.loop(0, count)
    def _(block):
        first = blocks[0, block]
        at = pl.multiple_of((first // 2) * 128, 128)
        own = pltpu.roll(c_occ[:, pl.ds(at, 128)].astype(F32), (first % 2) * SHELL, 1)[:, :SHELL]
        wide = jnp.dot(own.astype(BF16), spread[...], preferred_element_type=F32)
        coef[...] = wide * screen[block].astype(F32)
        pltpu.make_async_copy(ints.at[block], held.at[block], sems.at[block]).wait()

        def step(t, sums):
            at = pl.multiple_of(t * 128, 128)
            tile = held[block, :, pl.ds(at, 128)].astype(F32)
            weights = coef[:, pl.ds(at, 128)]
            return tuple(sums[i] + tile * weights[i : i + 1] for i in range(8))

        sums = lax.fori_loop(0, 32, step, (jnp.zeros((32, 128), F32),) * 8, unroll=8)
        full = [s + pltpu.roll(s, SHELL, 1) for s in sums]
        shell = blocks[1, block].astype(F32)
        put = pl.multiple_of(block * 16, 16)
        for yh in range(4):
            both = jnp.where(left, full[2 * yh], full[2 * yh + 1])
            for core in range(2):
                d = yh * 2 + core
                out[d, pl.ds(put, 16), :] = both[core * 16 : core * 16 + 16]
                out[d, 64:72, :] = jnp.where(rows((8, 128)) == block, shell, out[d, 64:72, :])


def half_transform(c_occ, ints, blocks, screen):
    return pl.pallas_call(
        half_kernel,
        out_shape=jax.ShapeDtypeStruct((8, 72, 128), F32),
        in_specs=[SMEM, SMEM, VMEM, HBM],
        out_specs=VMEM,
        scratch_shapes=[
            pltpu.VMEM(ints.shape, BF16),
            pltpu.VMEM((SHELL, 4096), BF16),
            pltpu.VMEM((8, 4096), F32),
            pltpu.SemaphoreType.DMA((ints.shape[0],)),
        ],
        compiler_params=grant(6),
        name="half",
    )(blocks.T, screen, c_occ.T, ints)


def rounded(x):
    return x.astype(BF16).astype(F32)


def transform_kernel(recv, c_vir, bmat, wide, thin, held, terms, sides, sems):
    copies = []
    for q in range(TILES // 2):
        columns = pl.ds(q * 256, 256)
        copies.append(pltpu.make_async_copy(c_vir.at[:, columns], held.at[:, columns], sems.at[q]))
        copies[q].start()
    left = lanes((16, 128)) < SHELL
    sums = [jnp.zeros((16, 128), F32) for _ in range(SHELLS)]
    for source in range(8):
        for b in range(4):
            data = recv[source, b * 16 : b * 16 + 16, :]
            shell = recv[source, 64 + b : 65 + b, :]
            for n in range(SHELLS):
                sums[n] = sums[n] + jnp.where(shell == float(n), data, 0.0)
    for m in range(SHELLS // 2):
        one, two = sums[2 * m], sums[2 * m + 1]
        pair = (
            jnp.where(left, one, pltpu.roll(two, SHELL, 1)),
            jnp.where(left, pltpu.roll(one, SHELL, 1), two),
        )
        for i in range(2):
            value = pair[i]
            for term in range(3):
                part = rounded(value)
                terms[term * 32 + i * 16 : term * 32 + i * 16 + 16, m * 128 : m * 128 + 128] = part.astype(BF16)
                value = value - part
    for q in range(TILES // 2):
        copies[q].wait()
        got = jnp.dot(terms[...], held[:, q * 256 : q * 256 + 256], preferred_element_type=F32)
        full = (got[64:96] + got[32:64]) + got[0:32]
        bmat[:, q * 256 : q * 256 + 256] = full.astype(BF16)
        for t in range(2):
            one, two = full[0:16, t * 128 : t * 128 + 128], full[16:32, t * 128 : t * 128 + 128]
            tile = q * 2 + t
            sides[tile * 2] = jnp.where(left, one, pltpu.roll(two, SHELL, 1)).astype(BF16)
            sides[tile * 2 + 1] = jnp.where(left, pltpu.roll(one, SHELL, 1), two).astype(BF16)
    for r in range(TILES):
        for yh in range(4):
            wide[r * 4 + yh] = bmat[:, r * 128 : r * 128 + 128]
            for x in range(4):
                kind = x * 4 + yh
                other = (r + kind // 2 + 1) % TILES
                thin[((r // 2 * 4 + x) * 2 + r % 2) * 4 + yh] = sides[other * 2 + kind % 2]


def transform(recv, c_vir):
    return pl.pallas_call(
        transform_kernel,
        out_shape=(
            jax.ShapeDtypeStruct((32, c_vir.shape[1]), BF16),
            jax.ShapeDtypeStruct((64, 32, 128), BF16),
            jax.ShapeDtypeStruct((256, 16, 128), BF16),
        ),
        in_specs=[VMEM, HBM],
        out_specs=(VMEM, VMEM, VMEM),
        scratch_shapes=[
            pltpu.VMEM(c_vir.shape, BF16),
            pltpu.VMEM((96, c_vir.shape[0]), BF16),
            pltpu.VMEM((32, 16, 128), BF16),
            pltpu.SemaphoreType.DMA((TILES // 2,)),
        ],
        compiler_params=grant(10),
        name="transform",
    )(recv, c_vir)


def gram_kernel(place, tiles, sides, _, keep, give, wide, all_t, all_s):
    core, side, own = place[4], place[3], place[5]
    mine = []
    for x in range(4):
        for i in range(8):
            wide[x * 256 : x * 256 + 256, i * 128 : i * 128 + 128] = tiles[x, :, i].reshape(256, 128)
        mine.append(tiles[x, :, own].reshape(256, 128))
    for p in range(4):
        thin = jnp.concatenate([sides[:, x, :, p].reshape(256, 128) for x in range(4)], axis=0)
        all_t[p * 128 : p * 128 + 128, :] = lax.dot_general(thin, wide[...], TRANSPOSED, preferred_element_type=F32)
    mine = jnp.concatenate(mine, axis=0)
    others = wide[:, pl.ds(pl.multiple_of(side * 512, 512), 512)]
    all_s[...] = lax.dot_general(mine, others, TRANSPOSED, preferred_element_type=F32)
    for which, target in ((core, keep), (1 - core, give)):
        for j in range(8):
            at = pl.multiple_of(j * 64 + which * 32, 32)
            target[j * 32 : j * 32 + 32, :] = all_t[pl.ds(at, 32), :]
        for q in range(4):
            at = pl.multiple_of(which * 256, 256)
            target[256:288, q * 256 : q * 256 + 256] = all_s[q * 32 : q * 32 + 32, pl.ds(at, 256)]


def gram(place, tiles, sides, after):
    shape = jax.ShapeDtypeStruct((288, 1024), F32)
    return pl.pallas_call(
        gram_kernel,
        out_shape=(shape, shape),
        in_specs=[SMEM, VMEM, VMEM, HBM],
        out_specs=(VMEM, VMEM),
        scratch_shapes=[
            pltpu.VMEM((1024, 1024), BF16),
            pltpu.VMEM((512, 1024), F32),
            pltpu.VMEM((128, 512), F32),
        ],
        compiler_params=grant(16),
        name="gram",
    )(place, tiles.reshape(4, 16, 8, 16, 128), sides.reshape(8, 4, 2, 4, 16, 128), after)


def energy_kernel(scale, place, eps_occ, keep, got, eps_vir, out, parts):
    tile, other, step, side, core, own = (place[n] for n in range(6))
    row_a = eps_vir[pl.ds(tile, 1), :]
    row_b = eps_vir[pl.ds(other, 1), :]
    first = side * 64 + core * 32
    col_b = jnp.sum(jnp.where(lanes((32, 128)) == rows((32, 128)) + first, row_b, 0.0), axis=1, keepdims=True)
    weight = jnp.where(step == 8, 1.0, 2.0)
    for i in range(8):
        for j in range(i, 8):
            there = slice(j * 32, j * 32 + 32), slice(i * 128, i * 128 + 128)
            here = slice(i * 32, i * 32 + 32), slice(j * 128, j * 128 + 128)
            one = keep[there] + got[there]
            two = keep[here] + got[here]
            denominators = (eps_occ[i] + eps_occ[j] - row_a) - col_b
            terms = (one * one + two * two - one * two) / denominators
            part = jnp.sum(terms, axis=0, keepdims=True) * weight
            parts[i * 8 + j : i * 8 + j + 1, :] = part
            parts[j * 8 + i : j * 8 + i + 1, :] = part
    square = (128, 128)
    eye = lanes(square) == rows(square)
    col_a = jnp.sum(jnp.where(eye, row_a, 0.0), axis=1, keepdims=True)
    for m in range(2):
        j = side * 4 + core * 2 + m
        block = jnp.concatenate(
            [
                keep[256:288, q * 256 + m * 128 : q * 256 + m * 128 + 128]
                + got[256:288, q * 256 + m * 128 : q * 256 + m * 128 + 128]
                for q in range(4)
            ],
            axis=0,
        )
        denominators = (eps_occ[own] + eps_occ[j] - row_a) - col_a
        terms = block * (2.0 * block - block.T) / denominators
        at = pl.ds(own * 8 + j, 1)
        parts[at, :] = parts[at, :] + jnp.sum(terms, axis=0, keepdims=True)
    column = jnp.sum(parts[...], axis=1, keepdims=True) * scale
    row = jnp.sum(jnp.where(lanes((64, 128)) == rows((64, 128)), column, 0.0), axis=0, keepdims=True)
    out[...] = jnp.broadcast_to(row[None], out.shape)


def energies(scale, place, eps_occ, keep, got, eps_vir):
    return pl.pallas_call(
        functools.partial(energy_kernel, scale),
        out_shape=jax.ShapeDtypeStruct((32, 1, 128), F32),
        in_specs=[SMEM, SMEM, VMEM, VMEM, VMEM],
        out_specs=VMEM,
        scratch_shapes=[pltpu.VMEM((64, 128), F32)],
        compiler_params=grant(6),
        name="energies",
    )(place, eps_occ, keep, got, eps_vir.reshape(-1, 128))


def position():
    z, x, yl, yh, core = (lax.axis_index(axis) for axis in AXES)
    tile, kind = z * 2 + yl, x * 4 + yh
    step, side = lax.shift_right_logical(kind, 1) + 1, kind & 1
    return jnp.stack([tile, (tile + step) & (TILES - 1), step, side, core, lax.shift_right_logical(kind, 1)])


def again_kernel(got, out):
    out[...] = jnp.broadcast_to(jnp.sum(got[...], axis=0)[None], out.shape)


def last_kernel(got, out):
    row = jnp.broadcast_to(jnp.sum(got[...], axis=0), (8, 128))
    place = rows((8, 128))
    square = row
    for i in range(1, 8):
        square = jnp.where(place == i, pltpu.roll(row, 128 - 8 * i, 1), square)
    out[...] = square[:, :8]


def body(c_occ, c_vir, ints, blocks, screen, eps_occ, eps_vir):
    vir, occ = c_vir.shape[1], c_occ.shape[1]
    place = position()
    core = lax.axis_index("core")
    swap = [(0, 1), (1, 0)]
    sent = half_transform(c_occ, ints, blocks, screen)
    recv = lax.all_to_all(sent, GRP, 0, 0, tiled=True)
    two, wide, thin = transform(recv, c_vir)
    tiles = lax.all_to_all(wide, ("z", "yl", "yh"), 0, 0, tiled=True)
    tiles = lax.all_gather(tiles, "x")
    sides = lax.all_to_all(thin, CHIPS, 0, 0, tiled=True)

    two = two.reshape(2, 16, vir)
    mine = lax.dynamic_index_in_dim(two, core, 0, keepdims=False)
    others = lax.ppermute(lax.dynamic_index_in_dim(two, 1 - core, 0, keepdims=False), "core", swap)
    bmat = jnp.where(core == 0, jnp.stack([mine, others]), jnp.stack([others, mine]))

    keep, give = gram(place, tiles, sides, others)
    got = lax.ppermute(give, "core", swap)
    scale = 1.0 / (float(vir) * float(vir) * 2048.0)
    energy = energies(scale, place, eps_occ, keep, got, eps_vir)
    energy = lax.all_to_all(energy, ("z", "x"), 0, 0, tiled=True)
    energy = pl.pallas_call(again_kernel, out_shape=jax.ShapeDtypeStruct((16, 1, 128), F32), name="again")(energy)
    energy = lax.all_to_all(energy, ("yh", "yl", "core"), 0, 0, tiled=True)
    energy = pl.pallas_call(last_kernel, out_shape=jax.ShapeDtypeStruct((occ, occ), F32), name="last")(energy)
    return bmat.reshape(1, 32, vir), energy


def solution(mesh):
    fine = Mesh(mesh.devices.reshape(8, 4, 2, 4, 2), AXES)
    return jax.shard_map(
        body,
        mesh=fine,
        in_specs=(P(), P(), P(GRP, PAIR, None), P(GRP, None), P(GRP), P(), P()),
        out_specs=(P(GRP, PAIR, None), P()),
        check_vma=False,
    )
```

```python
import functools

import jax
import jax.numpy as jnp
from jax import lax
from jax.experimental import pallas as pl
from jax.experimental.pallas import tpu as pltpu
from jax.sharding import Mesh, PartitionSpec as P

SHELL = 64
SHELLS = 12
TILES = 16
AXES = ("z", "x", "yl", "yh", "core")
CHIPS = ("z", "x", "yl", "yh")
PAIR = ("z", "x", "yl")
GRP = ("yh", "core")
F32 = jnp.float32
BF16 = jnp.bfloat16
VMEM = pl.BlockSpec(memory_space=pltpu.VMEM)
SMEM = pl.BlockSpec(memory_space=pltpu.SMEM)
HBM = pl.BlockSpec(memory_space=pltpu.HBM)
TRANSPOSED = (((0,), (0,)), ((), ()))


def lanes(shape):
    return lax.broadcasted_iota(jnp.int32, shape, 1)


def grant(mib):
    return pltpu.CompilerParams(vmem_limit_bytes=mib * 1024 * 1024)


def rows(shape):
    return lax.broadcasted_iota(jnp.int32, shape, 0)


def half_kernel(blocks, screen, c_occ, ints, out, held, spread, coef, sems):
    count = held.shape[0]
    for b in range(count):
        pltpu.make_async_copy(ints.at[b], held.at[b], sems.at[b]).start()
    shape = (SHELL, 4096)
    spread[...] = (lanes(shape) // SHELL == rows(shape)).astype(F32).astype(BF16)
    left = lanes((32, 128)) < SHELL

    @pl.loop(0, count)
    def _(block):
        first = blocks[0, block]
        at = pl.multiple_of((first // 2) * 128, 128)
        own = pltpu.roll(c_occ[:, pl.ds(at, 128)].astype(F32), (first % 2) * SHELL, 1)[:, :SHELL]
        wide = jnp.dot(own.astype(BF16), spread[...], preferred_element_type=F32)
        coef[...] = wide * screen[block].astype(F32)
        pltpu.make_async_copy(ints.at[block], held.at[block], sems.at[block]).wait()

        def step(t, sums):
            at = pl.multiple_of(t * 128, 128)
            tile = held[block, :, pl.ds(at, 128)].astype(F32)
            weights = coef[:, pl.ds(at, 128)]
            return tuple(sums[i] + tile * weights[i : i + 1] for i in range(8))

        sums = lax.fori_loop(0, 32, step, (jnp.zeros((32, 128), F32),) * 8, unroll=8)
        full = [s + pltpu.roll(s, SHELL, 1) for s in sums]
        shell = blocks[1, block].astype(F32)
        put = pl.multiple_of(block * 16, 16)
        for yh in range(4):
            both = jnp.where(left, full[2 * yh], full[2 * yh + 1])
            for core in range(2):
                d = yh * 2 + core
                out[d, pl.ds(put, 16), :] = both[core * 16 : core * 16 + 16]
                out[d, 64:72, :] = jnp.where(rows((8, 128)) == block, shell, out[d, 64:72, :])


def half_transform(c_occ, ints, blocks, screen):
    return pl.pallas_call(
        half_kernel,
        out_shape=jax.ShapeDtypeStruct((8, 72, 128), F32),
        in_specs=[SMEM, SMEM, VMEM, HBM],
        out_specs=VMEM,
        scratch_shapes=[
            pltpu.VMEM(ints.shape, BF16),
            pltpu.VMEM((SHELL, 4096), BF16),
            pltpu.VMEM((8, 4096), F32),
            pltpu.SemaphoreType.DMA((ints.shape[0],)),
        ],
        compiler_params=grant(62),
        name="half",
    )(blocks.T, screen, c_occ.T, ints)


def rounded(x):
    return x.astype(BF16).astype(F32)


def transform_kernel(recv, c_vir, bmat, wide, thin, held, terms, sides, sems):
    copies = []
    for q in range(TILES // 2):
        columns = pl.ds(q * 256, 256)
        copies.append(pltpu.make_async_copy(c_vir.at[:, columns], held.at[:, columns], sems.at[q]))
        copies[q].start()
    left = lanes((16, 128)) < SHELL
    sums = [jnp.zeros((16, 128), F32) for _ in range(SHELLS)]
    for source in range(8):
        for b in range(4):
            data = recv[source, b * 16 : b * 16 + 16, :]
            shell = recv[source, 64 + b : 65 + b, :]
            for n in range(SHELLS):
                sums[n] = sums[n] + jnp.where(shell == float(n), data, 0.0)
    for m in range(SHELLS // 2):
        one, two = sums[2 * m], sums[2 * m + 1]
        pair = (
            jnp.where(left, one, pltpu.roll(two, SHELL, 1)),
            jnp.where(left, pltpu.roll(one, SHELL, 1), two),
        )
        for i in range(2):
            value = pair[i]
            for term in range(3):
                part = rounded(value)
                terms[term * 32 + i * 16 : term * 32 + i * 16 + 16, m * 128 : m * 128 + 128] = part.astype(BF16)
                value = value - part
    for q in range(TILES // 2):
        copies[q].wait()
        got = jnp.dot(terms[...], held[:, q * 256 : q * 256 + 256], preferred_element_type=F32)
        full = (got[64:96] + got[32:64]) + got[0:32]
        bmat[:, q * 256 : q * 256 + 256] = full.astype(BF16)
        for t in range(2):
            one, two = full[0:16, t * 128 : t * 128 + 128], full[16:32, t * 128 : t * 128 + 128]
            tile = q * 2 + t
            sides[tile * 2] = jnp.where(left, one, pltpu.roll(two, SHELL, 1)).astype(BF16)
            sides[tile * 2 + 1] = jnp.where(left, pltpu.roll(one, SHELL, 1), two).astype(BF16)
    for r in range(TILES):
        for yh in range(4):
            wide[r * 4 + yh] = bmat[:, r * 128 : r * 128 + 128]
            for x in range(4):
                kind = x * 4 + yh
                other = (r + kind // 2 + 1) % TILES
                thin[((r // 2 * 4 + x) * 2 + r % 2) * 4 + yh] = sides[other * 2 + kind % 2]


def transform(recv, c_vir):
    return pl.pallas_call(
        transform_kernel,
        out_shape=(
            jax.ShapeDtypeStruct((32, c_vir.shape[1]), BF16),
            jax.ShapeDtypeStruct((64, 32, 128), BF16),
            jax.ShapeDtypeStruct((256, 16, 128), BF16),
        ),
        in_specs=[VMEM, HBM],
        out_specs=(VMEM, VMEM, VMEM),
        scratch_shapes=[
            pltpu.VMEM(c_vir.shape, BF16),
            pltpu.VMEM((96, c_vir.shape[0]), BF16),
            pltpu.VMEM((32, 16, 128), BF16),
            pltpu.SemaphoreType.DMA((TILES // 2,)),
        ],
        compiler_params=grant(61),
        name="transform",
    )(recv, c_vir)


def gram_kernel(place, here, below, above, low, high, sides, _, keep, give, wide, thin, all_t, all_s):
    core, side, own, x = place[4], place[3], place[5], place[6]
    first = 0
    for away, tiles in ((0, here), (3, below), (1, above), (2, low), (2, high)):
        count = tiles.shape[0] * 16
        for i in range(8):
            wide[first : first + count, i * 128 : i * 128 + 128] = tiles[:, i].reshape(count, 128)
        z = 4 if tiles is high else 0
        for p in range(4):
            rows_z = sides[z : z + count // 32, (x + away) & 3, :, p]
            thin[first : first + count, p * 128 : p * 128 + 128] = rows_z.reshape(count, 128)
        first += count
    for p in range(4):
        part = lax.dot_general(thin[:, p * 128 : p * 128 + 128], wide[...], TRANSPOSED, preferred_element_type=F32)
        all_t[p * 128 : p * 128 + 128, :] = part
    mine = wide[:, pl.ds(pl.multiple_of(own * 128, 128), 128)]
    others = wide[:, pl.ds(pl.multiple_of(side * 512, 512), 512)]
    all_s[...] = lax.dot_general(mine, others, TRANSPOSED, preferred_element_type=F32)
    for which, target in ((core, keep), (1 - core, give)):
        for j in range(8):
            at = pl.multiple_of(j * 64 + which * 32, 32)
            target[j * 32 : j * 32 + 32, :] = all_t[pl.ds(at, 32), :]
        for q in range(4):
            at = pl.multiple_of(which * 256, 256)
            target[256:288, q * 256 : q * 256 + 256] = all_s[q * 32 : q * 32 + 32, pl.ds(at, 256)]


def gram(place, here, below, above, low, high, sides, after):
    shape = jax.ShapeDtypeStruct((288, 1024), F32)
    tiles = (block.reshape(-1, 8, 16, 128) for block in (here, below, above, low, high))
    return pl.pallas_call(
        gram_kernel,
        out_shape=(shape, shape),
        in_specs=[SMEM] + [VMEM] * 6 + [HBM],
        out_specs=(VMEM, VMEM),
        scratch_shapes=[
            pltpu.VMEM((1024, 1024), BF16),
            pltpu.VMEM((1024, 512), BF16),
            pltpu.VMEM((512, 1024), F32),
            pltpu.VMEM((128, 512), F32),
        ],
        compiler_params=grant(16),
        name="gram",
    )(place, *tiles, sides.reshape(8, 4, 2, 4, 16, 128), after)


def energy_kernel(scale, place, eps_occ, keep, got, eps_vir, out, parts):
    tile, other, step, side, core, own = (place[n] for n in range(6))
    row_a = eps_vir[pl.ds(tile, 1), :]
    row_b = eps_vir[pl.ds(other, 1), :]
    first = side * 64 + core * 32
    col_b = jnp.sum(jnp.where(lanes((32, 128)) == rows((32, 128)) + first, row_b, 0.0), axis=1, keepdims=True)
    weight = jnp.where(step == 8, 1.0, 2.0)
    for i in range(8):
        for j in range(i, 8):
            there = slice(j * 32, j * 32 + 32), slice(i * 128, i * 128 + 128)
            here = slice(i * 32, i * 32 + 32), slice(j * 128, j * 128 + 128)
            one = keep[there] + got[there]
            two = keep[here] + got[here]
            denominators = (eps_occ[i] + eps_occ[j] - row_a) - col_b
            terms = (one * one + two * two - one * two) / denominators
            part = jnp.sum(terms, axis=0, keepdims=True) * weight
            parts[i * 8 + j : i * 8 + j + 1, :] = part
            parts[j * 8 + i : j * 8 + i + 1, :] = part
    square = (128, 128)
    eye = lanes(square) == rows(square)
    col_a = jnp.sum(jnp.where(eye, row_a, 0.0), axis=1, keepdims=True)
    for m in range(2):
        j = side * 4 + core * 2 + m
        block = jnp.concatenate(
            [
                keep[256:288, q * 256 + m * 128 : q * 256 + m * 128 + 128]
                + got[256:288, q * 256 + m * 128 : q * 256 + m * 128 + 128]
                for q in range(4)
            ],
            axis=0,
        )
        denominators = (eps_occ[own] + eps_occ[j] - row_a) - col_a
        terms = block * (2.0 * block - block.T) / denominators
        at = pl.ds(own * 8 + j, 1)
        parts[at, :] = parts[at, :] + jnp.sum(terms, axis=0, keepdims=True)
    column = jnp.sum(parts[...], axis=1, keepdims=True) * scale
    row = jnp.sum(jnp.where(lanes((64, 128)) == rows((64, 128)), column, 0.0), axis=0, keepdims=True)
    out[...] = jnp.broadcast_to(row[None], out.shape)


def energies(scale, place, eps_occ, keep, got, eps_vir):
    return pl.pallas_call(
        functools.partial(energy_kernel, scale),
        out_shape=jax.ShapeDtypeStruct((32, 1, 128), F32),
        in_specs=[SMEM, SMEM, VMEM, VMEM, VMEM],
        out_specs=VMEM,
        scratch_shapes=[pltpu.VMEM((64, 128), F32)],
        compiler_params=grant(6),
        name="energies",
    )(place, eps_occ, keep, got, eps_vir.reshape(-1, 128))


def position():
    z, x, yl, yh, core = (lax.axis_index(axis) for axis in AXES)
    tile, kind = z * 2 + yl, x * 4 + yh
    step, side = lax.shift_right_logical(kind, 1) + 1, kind & 1
    return jnp.stack([tile, (tile + step) & (TILES - 1), step, side, core, lax.shift_right_logical(kind, 1), x])


def again_kernel(got, out):
    out[...] = jnp.broadcast_to(jnp.sum(got[...], axis=0)[None], out.shape)


def last_kernel(got, out):
    row = jnp.broadcast_to(jnp.sum(got[...], axis=0), (8, 128))
    place = rows((8, 128))
    square = row
    for i in range(1, 8):
        square = jnp.where(place == i, pltpu.roll(row, 128 - 8 * i, 1), square)
    out[...] = square[:, :8]


def small(kernel, shape, name):
    return pl.pallas_call(
        kernel,
        out_shape=jax.ShapeDtypeStruct(shape, F32),
        in_specs=[VMEM],
        out_specs=VMEM,
        compiler_params=grant(2),
        name=name,
    )


def body(c_occ, c_vir, ints, blocks, screen, eps_occ, eps_vir):
    vir, occ = c_vir.shape[1], c_occ.shape[1]
    place = position()
    core = lax.axis_index("core")
    swap = [(0, 1), (1, 0)]
    sent = half_transform(c_occ, ints, blocks, screen)
    recv = lax.all_to_all(sent, GRP, 0, 0, tiled=True)
    two, wide, thin = transform(recv, c_vir)
    here = lax.all_to_all(wide, ("z", "yl", "yh"), 0, 0, tiled=True)
    up = [(i, (i + 1) % 4) for i in range(4)]
    down = [(i, (i + 3) % 4) for i in range(4)]
    below, above = lax.ppermute(here, "x", up), lax.ppermute(here, "x", down)
    low, high = lax.ppermute(above[:32], "x", down), lax.ppermute(below[32:], "x", up)
    sides = lax.all_to_all(thin, CHIPS, 0, 0, tiled=True)

    two = two.reshape(2, 16, vir)
    mine = lax.dynamic_index_in_dim(two, core, 0, keepdims=False)
    others = lax.ppermute(lax.dynamic_index_in_dim(two, 1 - core, 0, keepdims=False), "core", swap)
    bmat = jnp.where(core == 0, jnp.stack([mine, others]), jnp.stack([others, mine]))

    keep, give = gram(place, here, below, above, low, high, sides, others)
    got = lax.ppermute(give, "core", swap)
    scale = 1.0 / (float(vir) * float(vir) * 2048.0)
    energy = energies(scale, place, eps_occ, keep, got, eps_vir)
    energy = lax.all_to_all(energy, ("z", "x"), 0, 0, tiled=True)
    energy = small(again_kernel, (16, 1, 128), "again")(energy)
    energy = lax.all_to_all(energy, ("yh", "yl", "core"), 0, 0, tiled=True)
    energy = small(last_kernel, (occ, occ), "last")(energy)
    return bmat.reshape(1, 32, vir), energy


def solution(mesh):
    fine = Mesh(mesh.devices.reshape(8, 4, 2, 4, 2), AXES)
    return jax.shard_map(
        body,
        mesh=fine,
        in_specs=(P(), P(), P(GRP, PAIR, None), P(GRP, None), P(GRP), P(), P()),
        out_specs=(P(GRP, PAIR, None), P()),
        check_vma=False,
    )
```

```python
import functools

import jax
import jax.numpy as jnp
from jax import lax
from jax.experimental import pallas as pl
from jax.experimental.pallas import tpu as pltpu
from jax.sharding import Mesh, PartitionSpec as P

SHELL = 64
SHELLS = 12
TILES = 16
AXES = ("z", "x", "yl", "yh", "core")
CHIPS = ("z", "x", "yl", "yh")
PAIR = ("z", "x", "yl")
GRP = ("yh", "core")
F32 = jnp.float32
BF16 = jnp.bfloat16
VMEM = pl.BlockSpec(memory_space=pltpu.VMEM)
SMEM = pl.BlockSpec(memory_space=pltpu.SMEM)
HBM = pl.BlockSpec(memory_space=pltpu.HBM)
TRANSPOSED = (((0,), (0,)), ((), ()))


def lanes(shape):
    return lax.broadcasted_iota(jnp.int32, shape, 1)


def grant(mib):
    return pltpu.CompilerParams(vmem_limit_bytes=mib * 1024 * 1024)


def rows(shape):
    return lax.broadcasted_iota(jnp.int32, shape, 0)


def half_kernel(blocks, screen, c_occ, ints, out, held, spread, coef, sems):
    count = held.shape[0]
    for b in range(count):
        pltpu.make_async_copy(ints.at[b], held.at[b], sems.at[b]).start()
    shape = (SHELL, 4096)
    spread[...] = (lanes(shape) // SHELL == rows(shape)).astype(F32).astype(BF16)
    left = lanes((32, 128)) < SHELL

    @pl.loop(0, count)
    def _(block):
        first = blocks[0, block]
        at = pl.multiple_of((first // 2) * 128, 128)
        own = pltpu.roll(c_occ[:, pl.ds(at, 128)].astype(F32), (first % 2) * SHELL, 1)[:, :SHELL]
        wide = jnp.dot(own.astype(BF16), spread[...], preferred_element_type=F32)
        coef[...] = wide * screen[block].astype(F32)
        pltpu.make_async_copy(ints.at[block], held.at[block], sems.at[block]).wait()

        def step(t, sums):
            at = pl.multiple_of(t * 128, 128)
            tile = held[block, :, pl.ds(at, 128)].astype(F32)
            weights = coef[:, pl.ds(at, 128)]
            return tuple(sums[i] + tile * weights[i : i + 1] for i in range(8))

        sums = lax.fori_loop(0, 32, step, (jnp.zeros((32, 128), F32),) * 8, unroll=8)
        full = [s + pltpu.roll(s, SHELL, 1) for s in sums]
        shell = blocks[1, block].astype(F32)
        put = pl.multiple_of(block * 16, 16)
        for yh in range(4):
            both = jnp.where(left, full[2 * yh], full[2 * yh + 1])
            for core in range(2):
                d = yh * 2 + core
                out[d, pl.ds(put, 16), :] = both[core * 16 : core * 16 + 16]
                out[d, 64:72, :] = jnp.where(rows((8, 128)) == block, shell, out[d, 64:72, :])


def half_transform(c_occ, ints, blocks, screen):
    return pl.pallas_call(
        half_kernel,
        out_shape=jax.ShapeDtypeStruct((8, 72, 128), F32),
        in_specs=[SMEM, SMEM, VMEM, HBM],
        out_specs=VMEM,
        scratch_shapes=[
            pltpu.VMEM(ints.shape, BF16),
            pltpu.VMEM((SHELL, 4096), BF16),
            pltpu.VMEM((8, 4096), F32),
            pltpu.SemaphoreType.DMA((ints.shape[0],)),
        ],
        compiler_params=grant(62),
        name="half",
    )(blocks.T, screen, c_occ.T, ints)


def rounded(x):
    return x.astype(BF16).astype(F32)


def transform_kernel(recv, c_vir, bmat, wide, thin, held, terms, sides, sems):
    copies = []
    for m in range(SHELLS // 2):
        part = pl.ds(m * 128, 128)
        copies.append(pltpu.make_async_copy(c_vir.at[part], held.at[part], sems.at[m]))
        copies[m].start()
    left = lanes((16, 128)) < SHELL
    sums = [jnp.zeros((16, 128), F32) for _ in range(SHELLS)]
    for source in range(8):
        for b in range(4):
            data = recv[source, b * 16 : b * 16 + 16, :]
            shell = recv[source, 64 + b : 65 + b, :]
            for n in range(SHELLS):
                sums[n] = sums[n] + jnp.where(shell == float(n), data, 0.0)
    for m in range(SHELLS // 2):
        one, two = sums[2 * m], sums[2 * m + 1]
        pair = (
            jnp.where(left, one, pltpu.roll(two, SHELL, 1)),
            jnp.where(left, pltpu.roll(one, SHELL, 1), two),
        )
        for i in range(2):
            value = pair[i]
            for term in range(3):
                part = rounded(value)
                terms[term * 32 + i * 16 : term * 32 + i * 16 + 16, m * 128 : m * 128 + 128] = part.astype(BF16)
                value = value - part
    for copy in copies:
        copy.wait()
    for q in range(TILES // 2):
        got = jnp.dot(terms[...], held[:, q * 256 : q * 256 + 256], preferred_element_type=F32)
        full = (got[64:96] + got[32:64]) + got[0:32]
        bmat[:, q * 256 : q * 256 + 256] = full.astype(BF16)
        for t in range(2):
            one, two = full[0:16, t * 128 : t * 128 + 128], full[16:32, t * 128 : t * 128 + 128]
            tile = q * 2 + t
            sides[tile * 2] = jnp.where(left, one, pltpu.roll(two, SHELL, 1)).astype(BF16)
            sides[tile * 2 + 1] = jnp.where(left, pltpu.roll(one, SHELL, 1), two).astype(BF16)
    for r in range(TILES):
        for yh in range(4):
            wide[r * 4 + yh] = bmat[:, r * 128 : r * 128 + 128]
            for x in range(4):
                kind = x * 4 + yh
                other = (r + kind // 2 + 1) % TILES
                thin[((r // 2 * 4 + x) * 2 + r % 2) * 4 + yh] = sides[other * 2 + kind % 2]


def transform(recv, c_vir):
    return pl.pallas_call(
        transform_kernel,
        out_shape=(
            jax.ShapeDtypeStruct((32, c_vir.shape[1]), BF16),
            jax.ShapeDtypeStruct((64, 32, 128), BF16),
            jax.ShapeDtypeStruct((256, 16, 128), BF16),
        ),
        in_specs=[VMEM, HBM],
        out_specs=(VMEM, VMEM, VMEM),
        scratch_shapes=[
            pltpu.VMEM(c_vir.shape, BF16),
            pltpu.VMEM((96, c_vir.shape[0]), BF16),
            pltpu.VMEM((32, 16, 128), BF16),
            pltpu.SemaphoreType.DMA((SHELLS // 2,)),
        ],
        compiler_params=grant(61),
        name="transform",
    )(recv, c_vir)


def gram_kernel(place, here, below, above, low, high, sides, two, keep, give, wide, thin, all_t, all_s):
    core, side, own, x = place[4], place[3], place[5], place[6]
    first = 0
    for away, tiles in ((0, here), (3, below), (1, above), (2, low), (2, high)):
        count = tiles.shape[0] * 16
        for i in range(8):
            wide[first : first + count, i * 128 : i * 128 + 128] = tiles[:, i].reshape(count, 128)
        z = 4 if tiles is high else 0
        for p in range(4):
            rows_z = sides[z : z + count // 32, (x + away) & 3, :, p]
            thin[first : first + count, p * 128 : p * 128 + 128] = rows_z.reshape(count, 128)
        first += count
    for p in range(4):
        part = lax.dot_general(thin[:, p * 128 : p * 128 + 128], wide[...], TRANSPOSED, preferred_element_type=F32)
        all_t[p * 128 : p * 128 + 128, :] = part
    mine = wide[:, pl.ds(pl.multiple_of(own * 128, 128), 128)]
    others = wide[:, pl.ds(pl.multiple_of(side * 512, 512), 512)]
    all_s[...] = lax.dot_general(mine, others, TRANSPOSED, preferred_element_type=F32)
    for which, target in ((core, keep), (1 - core, give)):
        for j in range(8):
            at = pl.multiple_of(j * 64 + which * 32, 32)
            target[j * 32 : j * 32 + 32, :] = all_t[pl.ds(at, 32), :]
        for q in range(4):
            at = pl.multiple_of(which * 256, 256)
            target[256:288, q * 256 : q * 256 + 256] = all_s[q * 32 : q * 32 + 32, pl.ds(at, 256)]
    at = pl.multiple_of((1 - core) * 16, 16)
    for q in range(2):
        give[288 + q * 16 : 304 + q * 16, :] = two[pl.ds(at, 16), q * 1024 : q * 1024 + 1024].astype(F32)


def gram(place, here, below, above, low, high, sides, two):
    tiles = (block.reshape(-1, 8, 16, 128) for block in (here, below, above, low, high))
    return pl.pallas_call(
        gram_kernel,
        out_shape=(jax.ShapeDtypeStruct((288, 1024), F32), jax.ShapeDtypeStruct((320, 1024), F32)),
        in_specs=[SMEM] + [VMEM] * 7,
        out_specs=(VMEM, VMEM),
        scratch_shapes=[
            pltpu.VMEM((1024, 1024), BF16),
            pltpu.VMEM((1024, 512), BF16),
            pltpu.VMEM((512, 1024), F32),
            pltpu.VMEM((128, 512), F32),
        ],
        compiler_params=grant(16),
        name="gram",
    )(place, *tiles, sides.reshape(8, 4, 2, 4, 16, 128), two)


def energy_kernel(scale, place, eps_occ, keep, got, eps_vir, mine, out, bmat, parts):
    tile, other, step, side, core, own = (place[n] for n in range(6))
    row_a = eps_vir[pl.ds(tile, 1), :]
    row_b = eps_vir[pl.ds(other, 1), :]
    first = side * 64 + core * 32
    col_b = jnp.sum(jnp.where(lanes((32, 128)) == rows((32, 128)) + first, row_b, 0.0), axis=1, keepdims=True)
    weight = jnp.where(step == 8, 1.0, 2.0)
    for i in range(8):
        for j in range(i, 8):
            there = slice(j * 32, j * 32 + 32), slice(i * 128, i * 128 + 128)
            here = slice(i * 32, i * 32 + 32), slice(j * 128, j * 128 + 128)
            one = keep[there] + got[there]
            two = keep[here] + got[here]
            denominators = (eps_occ[i] + eps_occ[j] - row_a) - col_b
            terms = (one * one + two * two - one * two) / denominators
            part = jnp.sum(terms, axis=0, keepdims=True) * weight
            parts[i * 8 + j : i * 8 + j + 1, :] = part
            parts[j * 8 + i : j * 8 + i + 1, :] = part
    square = (128, 128)
    eye = lanes(square) == rows(square)
    col_a = jnp.sum(jnp.where(eye, row_a, 0.0), axis=1, keepdims=True)
    for m in range(2):
        j = side * 4 + core * 2 + m
        block = jnp.concatenate(
            [
                keep[256:288, q * 256 + m * 128 : q * 256 + m * 128 + 128]
                + got[256:288, q * 256 + m * 128 : q * 256 + m * 128 + 128]
                for q in range(4)
            ],
            axis=0,
        )
        denominators = (eps_occ[own] + eps_occ[j] - row_a) - col_a
        terms = block * (2.0 * block - block.T) / denominators
        at = pl.ds(own * 8 + j, 1)
        parts[at, :] = parts[at, :] + jnp.sum(terms, axis=0, keepdims=True)
    column = jnp.sum(parts[...], axis=1, keepdims=True) * scale
    row = jnp.sum(jnp.where(lanes((64, 128)) == rows((64, 128)), column, 0.0), axis=0, keepdims=True)
    out[...] = jnp.broadcast_to(row[None], out.shape)
    here = pl.ds(pl.multiple_of(core * 16, 16), 16)
    bmat[here, :] = mine[here, :]
    there = pl.ds(pl.multiple_of((1 - core) * 16, 16), 16)
    for q in range(2):
        bmat[there, q * 1024 : q * 1024 + 1024] = got[288 + q * 16 : 304 + q * 16, :].astype(BF16)


def energies(scale, place, eps_occ, keep, got, eps_vir, two):
    return pl.pallas_call(
        functools.partial(energy_kernel, scale),
        out_shape=(jax.ShapeDtypeStruct((256, 1, 128), F32), jax.ShapeDtypeStruct(two.shape, BF16)),
        in_specs=[SMEM, SMEM, VMEM, VMEM, VMEM, VMEM],
        out_specs=(VMEM, VMEM),
        scratch_shapes=[pltpu.VMEM((64, 128), F32)],
        compiler_params=grant(8),
        name="energies",
    )(place, eps_occ, keep, got, eps_vir.reshape(-1, 128), two)


def position():
    z, x, yl, yh, core = (lax.axis_index(axis) for axis in AXES)
    tile, kind = z * 2 + yl, x * 4 + yh
    step, side = lax.shift_right_logical(kind, 1) + 1, kind & 1
    return jnp.stack([tile, (tile + step) & (TILES - 1), step, side, core, lax.shift_right_logical(kind, 1), x])


def last_kernel(got, out):
    row = jnp.broadcast_to(jnp.sum(got[...], axis=0), (8, 128))
    place = rows((8, 128))
    square = row
    for i in range(1, 8):
        square = jnp.where(place == i, pltpu.roll(row, 128 - 8 * i, 1), square)
    out[...] = square[:, :8]


def small(kernel, shape, name):
    return pl.pallas_call(
        kernel,
        out_shape=jax.ShapeDtypeStruct(shape, F32),
        in_specs=[VMEM],
        out_specs=VMEM,
        compiler_params=grant(2),
        name=name,
    )


def body(c_occ, c_vir, ints, blocks, screen, eps_occ, eps_vir):
    vir, occ = c_vir.shape[1], c_occ.shape[1]
    place = position()
    sent = half_transform(c_occ, ints, blocks, screen)
    recv = lax.all_to_all(sent, GRP, 0, 0, tiled=True)
    two, wide, thin = transform(recv, c_vir)
    here = lax.all_to_all(wide, ("z", "yl", "yh"), 0, 0, tiled=True)
    up = [(i, (i + 1) % 4) for i in range(4)]
    down = [(i, (i + 3) % 4) for i in range(4)]
    below, above = lax.ppermute(here, "x", up), lax.ppermute(here, "x", down)
    low, high = lax.ppermute(above[:32], "x", down), lax.ppermute(below[32:], "x", up)
    sides = lax.all_to_all(thin, CHIPS, 0, 0, tiled=True)

    keep, give = gram(place, here, below, above, low, high, sides, two)
    got = lax.ppermute(give, "core", [(0, 1), (1, 0)])
    scale = 1.0 / (float(vir) * float(vir) * 2048.0)
    energy, bmat = energies(scale, place, eps_occ, keep, got, eps_vir, two)
    energy = lax.all_to_all(energy, CHIPS, 0, 0, tiled=True)
    energy = lax.psum(small(last_kernel, (occ, occ), "last")(energy), "core")
    return bmat.reshape(1, 32, vir), energy


def solution(mesh):
    fine = Mesh(mesh.devices.reshape(8, 4, 2, 4, 2), AXES)
    return jax.shard_map(
        body,
        mesh=fine,
        in_specs=(P(), P(), P(GRP, PAIR, None), P(GRP, None), P(GRP), P(), P()),
        out_specs=(P(GRP, PAIR, None), P()),
        check_vma=False,
    )
```

```python
import functools

import jax
import jax.numpy as jnp
from jax import lax
from jax.experimental import pallas as pl
from jax.experimental.pallas import tpu as pltpu
from jax.sharding import Mesh, PartitionSpec as P

SHELL = 64
SHELLS = 12
TILES = 16
CHUNKS = 3
AXES = ("z", "x", "yl", "yh", "core")
CHIPS = ("z", "x", "yl", "yh")
PAIR = ("z", "x", "yl")
GRP = ("yh", "core")
F32 = jnp.float32
BF16 = jnp.bfloat16
VMEM = pl.BlockSpec(memory_space=pltpu.VMEM)
SMEM = pl.BlockSpec(memory_space=pltpu.SMEM)
HBM = pl.BlockSpec(memory_space=pltpu.HBM)
TRANSPOSED = (((0,), (0,)), ((), ()))


def lanes(shape):
    return lax.broadcasted_iota(jnp.int32, shape, 1)


def grant(mib):
    return pltpu.CompilerParams(vmem_limit_bytes=mib * 1024 * 1024)


def rows(shape):
    return lax.broadcasted_iota(jnp.int32, shape, 0)


def half_kernel(blocks, screen, c_occ, ints, out, held, spread, coef, sems):
    count = held.shape[0]
    for b in range(count):
        pltpu.make_async_copy(ints.at[b], held.at[b], sems.at[b]).start()
    shape = (SHELL, 4096)
    spread[...] = (lanes(shape) // SHELL == rows(shape)).astype(F32).astype(BF16)
    own = []
    for b in range(count):
        first = blocks[0, b]
        at = pl.multiple_of((first // 2) * 128, 128)
        shell = pltpu.roll(c_occ[:, pl.ds(at, 128)].astype(F32), (first % 2) * SHELL, 1)[:, :SHELL]
        own.append(shell * screen[b].astype(F32))
    own = jnp.concatenate(own, axis=0).astype(BF16)
    coef[...] = jnp.dot(own, spread[...], preferred_element_type=F32).reshape(count, 8, 4096)
    left = lanes((32, 128)) < SHELL

    @pl.loop(0, count)
    def _(block):
        pltpu.make_async_copy(ints.at[block], held.at[block], sems.at[block]).wait()

        def step(t, sums):
            at = pl.multiple_of(t * 128, 128)
            tile = held[block, :, pl.ds(at, 128)].astype(F32)
            weights = coef[block, :, pl.ds(at, 128)]
            return tuple(sums[i] + tile * weights[i : i + 1] for i in range(8))

        sums = lax.fori_loop(0, 32, step, (jnp.zeros((32, 128), F32),) * 8, unroll=8)
        full = [s + pltpu.roll(s, SHELL, 1) for s in sums]
        shell = blocks[1, block].astype(F32)
        put = pl.multiple_of(block * 16, 16)
        for yh in range(4):
            both = jnp.where(left, full[2 * yh], full[2 * yh + 1])
            for core in range(2):
                d = yh * 2 + core
                out[d, pl.ds(put, 16), :] = both[core * 16 : core * 16 + 16]
                out[d, 64:72, :] = jnp.where(rows((8, 128)) == block, shell, out[d, 64:72, :])


def half_transform(c_occ, ints, blocks, screen):
    return pl.pallas_call(
        half_kernel,
        out_shape=jax.ShapeDtypeStruct((8, 72, 128), F32),
        in_specs=[SMEM, SMEM, VMEM, HBM],
        out_specs=VMEM,
        scratch_shapes=[
            pltpu.VMEM(ints.shape, BF16),
            pltpu.VMEM((SHELL, 4096), BF16),
            pltpu.VMEM((ints.shape[0], 8, 4096), F32),
            pltpu.SemaphoreType.DMA((ints.shape[0],)),
        ],
        compiler_params=grant(54),
        name="half",
    )(blocks.T, screen, c_occ.T, ints)


def rounded(x):
    return x.astype(BF16).astype(F32)


def finish(q, full, left, bmat, sides):
    bmat[:, q * 256 : q * 256 + 256] = full.astype(BF16)
    for t in range(2):
        one, two = full[0:16, t * 128 : t * 128 + 128], full[16:32, t * 128 : t * 128 + 128]
        tile = q * 2 + t
        sides[tile * 2] = jnp.where(left, one, pltpu.roll(two, SHELL, 1)).astype(BF16)
        sides[tile * 2 + 1] = jnp.where(left, pltpu.roll(one, SHELL, 1), two).astype(BF16)


def transform_kernel(recv_at, c_vir, bmat, wide, thin, recv, held, terms, sides, total, sems):
    arrive = pltpu.make_async_copy(recv_at, recv, sems.at[CHUNKS])
    arrive.start()
    copies = []
    for m in range(CHUNKS):
        part = pl.ds(m * 256, 256)
        copies.append(pltpu.make_async_copy(c_vir.at[part], held.at[part], sems.at[m]))
        copies[m].start()
    arrive.wait()
    left = lanes((16, 128)) < SHELL
    sums = [jnp.zeros((16, 128), F32) for _ in range(SHELLS)]
    for source in range(8):
        for b in range(4):
            data = recv[source, b * 16 : b * 16 + 16, :]
            shell = recv[source, 64 + b : 65 + b, :]
            for n in range(SHELLS):
                sums[n] = sums[n] + jnp.where(shell == float(n), data, 0.0)
    for m in range(SHELLS // 2):
        one, two = sums[2 * m], sums[2 * m + 1]
        pair = (
            jnp.where(left, one, pltpu.roll(two, SHELL, 1)),
            jnp.where(left, pltpu.roll(one, SHELL, 1), two),
        )
        for i in range(2):
            value = pair[i]
            for term in range(3):
                part = rounded(value)
                terms[term * 32 + i * 16 : term * 32 + i * 16 + 16, m * 128 : m * 128 + 128] = part.astype(BF16)
                value = value - part
    for m in range(CHUNKS):
        copies[m].wait()
        some = terms[:, m * 256 : m * 256 + 256]
        for q in range(TILES // 2):
            columns = slice(q * 256, q * 256 + 256)
            got = jnp.dot(some, held[m * 256 : m * 256 + 256, columns], preferred_element_type=F32)
            if m < CHUNKS - 1:
                total[:, columns] = got if m == 0 else total[:, columns] + got
                continue
            got = total[:, columns] + got
            full = (got[64:96] + got[32:64]) + got[0:32]
            finish(q, full, left, bmat, sides)
    for r in range(TILES):
        for yh in range(4):
            wide[r * 4 + yh] = bmat[:, r * 128 : r * 128 + 128]
            for x in range(4):
                kind = x * 4 + yh
                other = (r + kind // 2 + 1) % TILES
                thin[((r // 2 * 4 + x) * 2 + r % 2) * 4 + yh] = sides[other * 2 + kind % 2]


def transform(recv, c_vir):
    return pl.pallas_call(
        transform_kernel,
        out_shape=(
            jax.ShapeDtypeStruct((32, c_vir.shape[1]), BF16),
            jax.ShapeDtypeStruct((64, 32, 128), BF16),
            jax.ShapeDtypeStruct((256, 16, 128), BF16),
        ),
        in_specs=[HBM, HBM],
        out_specs=(VMEM, VMEM, VMEM),
        scratch_shapes=[
            pltpu.VMEM(recv.shape, F32),
            pltpu.VMEM(c_vir.shape, BF16),
            pltpu.VMEM((96, c_vir.shape[0]), BF16),
            pltpu.VMEM((32, 16, 128), BF16),
            pltpu.VMEM((96, c_vir.shape[1]), F32),
            pltpu.SemaphoreType.DMA((CHUNKS + 1,)),
        ],
        compiler_params=grant(52),
        name="transform",
    )(recv, c_vir)


def onward_kernel(below, above, low, high):
    low[...] = above[0:32]
    high[...] = below[32:64]


def onward(below, above):
    half = jax.ShapeDtypeStruct((32,) + below.shape[1:], BF16)
    return pl.pallas_call(
        onward_kernel,
        out_shape=(half, half),
        in_specs=[VMEM, VMEM],
        out_specs=(VMEM, VMEM),
        compiler_params=grant(4),
        cost_estimate=pl.CostEstimate(flops=1 << 35, bytes_accessed=1 << 21, transcendentals=0),
        name="onward",
    )(below, above)


def gram_kernel(place, here, below, above, low, high, sides, two, keep, give, wide, thin, all_t, all_s):
    core, side, own, x = place[4], place[3], place[5], place[6]
    first = 0
    for away, tiles in ((0, here), (3, below), (1, above), (2, low), (2, high)):
        count = tiles.shape[0] * 16
        for i in range(8):
            wide[first : first + count, i * 128 : i * 128 + 128] = tiles[:, i].reshape(count, 128)
        z = 4 if tiles is high else 0
        for p in range(4):
            rows_z = sides[z : z + count // 32, (x + away) & 3, :, p]
            thin[first : first + count, p * 128 : p * 128 + 128] = rows_z.reshape(count, 128)
        first += count
    for p in range(4):
        part = lax.dot_general(thin[:, p * 128 : p * 128 + 128], wide[...], TRANSPOSED, preferred_element_type=F32)
        all_t[p * 128 : p * 128 + 128, :] = part
    mine = wide[:, pl.ds(pl.multiple_of(own * 128, 128), 128)]
    others = wide[:, pl.ds(pl.multiple_of(side * 512, 512), 512)]
    all_s[...] = lax.dot_general(mine, others, TRANSPOSED, preferred_element_type=F32)
    for which, target in ((core, keep), (1 - core, give)):
        for j in range(8):
            at = pl.multiple_of(j * 64 + which * 32, 32)
            target[j * 32 : j * 32 + 32, :] = all_t[pl.ds(at, 32), :]
        for q in range(4):
            at = pl.multiple_of(which * 256, 256)
            target[256:288, q * 256 : q * 256 + 256] = all_s[q * 32 : q * 32 + 32, pl.ds(at, 256)]
    at = pl.multiple_of((1 - core) * 16, 16)
    for q in range(2):
        give[288 + q * 16 : 304 + q * 16, :] = two[pl.ds(at, 16), q * 1024 : q * 1024 + 1024].astype(F32)


def gram(place, here, below, above, low, high, sides, two):
    tiles = (block.reshape(-1, 8, 16, 128) for block in (here, below, above, low, high))
    return pl.pallas_call(
        gram_kernel,
        out_shape=(jax.ShapeDtypeStruct((288, 1024), F32), jax.ShapeDtypeStruct((320, 1024), F32)),
        in_specs=[SMEM] + [VMEM] * 7,
        out_specs=(VMEM, VMEM),
        scratch_shapes=[
            pltpu.VMEM((1024, 1024), BF16),
            pltpu.VMEM((1024, 512), BF16),
            pltpu.VMEM((512, 1024), F32),
            pltpu.VMEM((128, 512), F32),
        ],
        compiler_params=grant(16),
        name="gram",
    )(place, *tiles, sides.reshape(8, 4, 2, 4, 16, 128), two)


def energy_kernel(scale, place, eps_occ, keep, got, eps_vir, mine, out, bmat, parts):
    tile, other, step, side, core, own = (place[n] for n in range(6))
    row_a = eps_vir[pl.ds(tile, 1), :]
    row_b = eps_vir[pl.ds(other, 1), :]
    first = side * 64 + core * 32
    col_b = jnp.sum(jnp.where(lanes((32, 128)) == rows((32, 128)) + first, row_b, 0.0), axis=1, keepdims=True)
    weight = jnp.where(step == 8, 1.0, 2.0)
    for i in range(8):
        for j in range(i, 8):
            there = slice(j * 32, j * 32 + 32), slice(i * 128, i * 128 + 128)
            here = slice(i * 32, i * 32 + 32), slice(j * 128, j * 128 + 128)
            one = keep[there] + got[there]
            two = keep[here] + got[here]
            denominators = (eps_occ[i] + eps_occ[j] - row_a) - col_b
            terms = (one * one + two * two - one * two) / denominators
            part = jnp.sum(terms, axis=0, keepdims=True) * weight
            parts[i * 8 + j : i * 8 + j + 1, :] = part
            parts[j * 8 + i : j * 8 + i + 1, :] = part
    square = (128, 128)
    eye = lanes(square) == rows(square)
    col_a = jnp.sum(jnp.where(eye, row_a, 0.0), axis=1, keepdims=True)
    for m in range(2):
        j = side * 4 + core * 2 + m
        block = jnp.concatenate(
            [
                keep[256:288, q * 256 + m * 128 : q * 256 + m * 128 + 128]
                + got[256:288, q * 256 + m * 128 : q * 256 + m * 128 + 128]
                for q in range(4)
            ],
            axis=0,
        )
        denominators = (eps_occ[own] + eps_occ[j] - row_a) - col_a
        terms = block * (2.0 * block - block.T) / denominators
        at = pl.ds(own * 8 + j, 1)
        parts[at, :] = parts[at, :] + jnp.sum(terms, axis=0, keepdims=True)
    column = jnp.sum(parts[...], axis=1, keepdims=True) * scale
    row = jnp.sum(jnp.where(lanes((64, 128)) == rows((64, 128)), column, 0.0), axis=0, keepdims=True)
    out[...] = jnp.broadcast_to(row[None], out.shape)
    here = pl.ds(pl.multiple_of(core * 16, 16), 16)
    bmat[here, :] = mine[here, :]
    there = pl.ds(pl.multiple_of((1 - core) * 16, 16), 16)
    for q in range(2):
        bmat[there, q * 1024 : q * 1024 + 1024] = got[288 + q * 16 : 304 + q * 16, :].astype(BF16)


def energies(scale, place, eps_occ, keep, got, eps_vir, two):
    return pl.pallas_call(
        functools.partial(energy_kernel, scale),
        out_shape=(jax.ShapeDtypeStruct((256, 1, 128), F32), jax.ShapeDtypeStruct(two.shape, BF16)),
        in_specs=[SMEM, SMEM, VMEM, VMEM, VMEM, VMEM],
        out_specs=(VMEM, VMEM),
        scratch_shapes=[pltpu.VMEM((64, 128), F32)],
        compiler_params=grant(8),
        name="energies",
    )(place, eps_occ, keep, got, eps_vir.reshape(-1, 128), two)


def position():
    z, x, yl, yh, core = (lax.axis_index(axis) for axis in AXES)
    tile, kind = z * 2 + yl, x * 4 + yh
    step, side = lax.shift_right_logical(kind, 1) + 1, kind & 1
    return jnp.stack([tile, (tile + step) & (TILES - 1), step, side, core, lax.shift_right_logical(kind, 1), x])


def last_kernel(got, out):
    row = jnp.broadcast_to(jnp.sum(got[...], axis=0), (8, 128))
    place = rows((8, 128))
    square = row
    for i in range(1, 8):
        square = jnp.where(place == i, pltpu.roll(row, 128 - 8 * i, 1), square)
    out[...] = square[:, :8]


def small(kernel, shape, name):
    return pl.pallas_call(
        kernel,
        out_shape=jax.ShapeDtypeStruct(shape, F32),
        in_specs=[VMEM],
        out_specs=VMEM,
        compiler_params=grant(2),
        name=name,
    )


def body(c_occ, c_vir, ints, blocks, screen, eps_occ, eps_vir):
    vir, occ = c_vir.shape[1], c_occ.shape[1]
    place = position()
    sent = half_transform(c_occ, ints, blocks, screen)
    recv = lax.all_to_all(sent, GRP, 0, 0, tiled=True)
    two, wide, thin = transform(recv, c_vir)
    here = lax.all_to_all(wide, ("z", "yl", "yh"), 0, 0, tiled=True)
    up = [(i, (i + 1) % 4) for i in range(4)]
    down = [(i, (i + 3) % 4) for i in range(4)]
    below, above = lax.ppermute(here, "x", up), lax.ppermute(here, "x", down)
    low, high = onward(below, above)
    low, high = lax.ppermute(low, "x", down), lax.ppermute(high, "x", up)
    sides = lax.all_to_all(thin, CHIPS, 0, 0, tiled=True)

    keep, give = gram(place, here, below, above, low, high, sides, two)
    got = lax.ppermute(give, "core", [(0, 1), (1, 0)])
    scale = 1.0 / (float(vir) * float(vir) * 2048.0)
    energy, bmat = energies(scale, place, eps_occ, keep, got, eps_vir, two)
    energy = lax.all_to_all(energy, CHIPS, 0, 0, tiled=True)
    energy = lax.psum(small(last_kernel, (occ, occ), "last")(energy), "core")
    return bmat.reshape(1, 32, vir), energy


def solution(mesh):
    fine = Mesh(mesh.devices.reshape(8, 4, 2, 4, 2), AXES)
    return jax.shard_map(
        body,
        mesh=fine,
        in_specs=(P(), P(), P(GRP, PAIR, None), P(GRP, None), P(GRP), P(), P()),
        out_specs=(P(GRP, PAIR, None), P()),
        check_vma=False,
    )
```

```python
import functools

import jax
import jax.numpy as jnp
from jax import lax
from jax.experimental import pallas as pl
from jax.experimental.pallas import tpu as pltpu
from jax.sharding import Mesh, PartitionSpec as P

SHELL = 64
SHELLS = 12
TILES = 16
CHUNKS = 3
AXES = ("z", "x", "yl", "yh", "core")
CHIPS = ("z", "x", "yl", "yh")
PAIR = ("z", "x", "yl")
GRP = ("yh", "core")
F32 = jnp.float32
BF16 = jnp.bfloat16
VMEM = pl.BlockSpec(memory_space=pltpu.VMEM)
SMEM = pl.BlockSpec(memory_space=pltpu.SMEM)
HBM = pl.BlockSpec(memory_space=pltpu.HBM)
TRANSPOSED = (((0,), (0,)), ((), ()))


def lanes(shape):
    return lax.broadcasted_iota(jnp.int32, shape, 1)


def grant(mib):
    return pltpu.CompilerParams(vmem_limit_bytes=mib * 1024 * 1024)


def rows(shape):
    return lax.broadcasted_iota(jnp.int32, shape, 0)


def half_kernel(blocks_at, screen_at, c_occ_at, ints, out, blocks, screen, c_occ, held, spread, coef, sems):
    count = held.shape[0]
    first = [
        pltpu.make_async_copy(blocks_at, blocks, sems.at[count]),
        pltpu.make_async_copy(screen_at, screen, sems.at[count + 1]),
        pltpu.make_async_copy(c_occ_at, c_occ, sems.at[count + 2]),
    ]
    for copy in first:
        copy.start()
    for b in range(count):
        pltpu.make_async_copy(ints.at[b], held.at[b], sems.at[b]).start()
    shape = (SHELL, 4096)
    spread[...] = (lanes(shape) // SHELL == rows(shape)).astype(F32).astype(BF16)
    for copy in first:
        copy.wait()
    own = []
    for b in range(count):
        first = blocks[0, b]
        at = pl.multiple_of((first // 2) * 128, 128)
        shell = pltpu.roll(c_occ[:, pl.ds(at, 128)].astype(F32), (first % 2) * SHELL, 1)[:, :SHELL]
        own.append(shell * screen[b].astype(F32))
    own = jnp.concatenate(own, axis=0).astype(BF16)
    coef[...] = jnp.dot(own, spread[...], preferred_element_type=F32).reshape(count, 8, 4096)
    left = lanes((32, 128)) < SHELL

    @pl.loop(0, count)
    def _(block):
        pltpu.make_async_copy(ints.at[block], held.at[block], sems.at[block]).wait()

        def step(t, sums):
            at = pl.multiple_of(t * 128, 128)
            tile = held[block, :, pl.ds(at, 128)].astype(F32)
            weights = coef[block, :, pl.ds(at, 128)]
            return tuple(sums[i] + tile * weights[i : i + 1] for i in range(8))

        sums = lax.fori_loop(0, 32, step, (jnp.zeros((32, 128), F32),) * 8, unroll=8)
        full = [s + pltpu.roll(s, SHELL, 1) for s in sums]
        shell = blocks[1, block].astype(F32)
        put = pl.multiple_of(block * 16, 16)
        for yh in range(4):
            both = jnp.where(left, full[2 * yh], full[2 * yh + 1])
            for core in range(2):
                d = yh * 2 + core
                out[d, pl.ds(put, 16), :] = both[core * 16 : core * 16 + 16]
                out[d, 64:72, :] = jnp.where(rows((8, 128)) == block, shell, out[d, 64:72, :])


def half_transform(c_occ, ints, blocks, screen):
    return pl.pallas_call(
        half_kernel,
        out_shape=jax.ShapeDtypeStruct((8, 72, 128), F32),
        in_specs=[HBM, HBM, HBM, HBM],
        out_specs=VMEM,
        scratch_shapes=[
            pltpu.SMEM((2, ints.shape[0]), jnp.int32),
            pltpu.SMEM(screen.shape, jnp.int32),
            pltpu.VMEM((8, c_occ.shape[0]), BF16),
            pltpu.VMEM(ints.shape, BF16),
            pltpu.VMEM((SHELL, 4096), BF16),
            pltpu.VMEM((ints.shape[0], 8, 4096), F32),
            pltpu.SemaphoreType.DMA((ints.shape[0] + 3,)),
        ],
        compiler_params=grant(54),
        name="half",
    )(blocks.T, screen, c_occ.T, ints)


def rounded(x):
    return x.astype(BF16).astype(F32)


def finish(q, full, left, bmat, sides):
    bmat[:, q * 256 : q * 256 + 256] = full.astype(BF16)
    for t in range(2):
        one, two = full[0:16, t * 128 : t * 128 + 128], full[16:32, t * 128 : t * 128 + 128]
        tile = q * 2 + t
        sides[tile * 2] = jnp.where(left, one, pltpu.roll(two, SHELL, 1)).astype(BF16)
        sides[tile * 2 + 1] = jnp.where(left, pltpu.roll(one, SHELL, 1), two).astype(BF16)


def transform_kernel(recv_at, c_vir, bmat, wide, thin, recv, held, terms, sides, total, sems):
    arrive = pltpu.make_async_copy(recv_at, recv, sems.at[CHUNKS])
    arrive.start()
    copies = []
    for m in range(CHUNKS):
        part = pl.ds(m * 256, 256)
        copies.append(pltpu.make_async_copy(c_vir.at[part], held.at[part], sems.at[m]))
        copies[m].start()
    arrive.wait()
    left = lanes((16, 128)) < SHELL
    sums = [jnp.zeros((16, 128), F32) for _ in range(SHELLS)]
    for source in range(8):
        for b in range(4):
            data = recv[source, b * 16 : b * 16 + 16, :]
            shell = recv[source, 64 + b : 65 + b, :]
            for n in range(SHELLS):
                sums[n] = sums[n] + jnp.where(shell == float(n), data, 0.0)
    for m in range(SHELLS // 2):
        one, two = sums[2 * m], sums[2 * m + 1]
        pair = (
            jnp.where(left, one, pltpu.roll(two, SHELL, 1)),
            jnp.where(left, pltpu.roll(one, SHELL, 1), two),
        )
        for i in range(2):
            value = pair[i]
            for term in range(3):
                part = rounded(value)
                terms[term * 32 + i * 16 : term * 32 + i * 16 + 16, m * 128 : m * 128 + 128] = part.astype(BF16)
                value = value - part
    for m in range(CHUNKS):
        copies[m].wait()
        some = terms[:, m * 256 : m * 256 + 256]
        for q in range(TILES // 2):
            columns = slice(q * 256, q * 256 + 256)
            got = jnp.dot(some, held[m * 256 : m * 256 + 256, columns], preferred_element_type=F32)
            if m < CHUNKS - 1:
                total[:, columns] = got if m == 0 else total[:, columns] + got
                continue
            got = total[:, columns] + got
            full = (got[64:96] + got[32:64]) + got[0:32]
            finish(q, full, left, bmat, sides)
    for r in range(TILES):
        for yh in range(4):
            wide[r * 4 + yh] = bmat[:, r * 128 : r * 128 + 128]
            for x in range(4):
                kind = x * 4 + yh
                other = (r + kind // 2 + 1) % TILES
                thin[((r // 2 * 4 + x) * 2 + r % 2) * 4 + yh] = sides[other * 2 + kind % 2]


def transform(recv, c_vir):
    return pl.pallas_call(
        transform_kernel,
        out_shape=(
            jax.ShapeDtypeStruct((32, c_vir.shape[1]), BF16),
            jax.ShapeDtypeStruct((64, 32, 128), BF16),
            jax.ShapeDtypeStruct((256, 16, 128), BF16),
        ),
        in_specs=[HBM, HBM],
        out_specs=(VMEM, VMEM, VMEM),
        scratch_shapes=[
            pltpu.VMEM(recv.shape, F32),
            pltpu.VMEM(c_vir.shape, BF16),
            pltpu.VMEM((96, c_vir.shape[0]), BF16),
            pltpu.VMEM((32, 16, 128), BF16),
            pltpu.VMEM((96, c_vir.shape[1]), F32),
            pltpu.SemaphoreType.DMA((CHUNKS + 1,)),
        ],
        compiler_params=grant(52),
        name="transform",
    )(recv, c_vir)


def onward_kernel(half, block, out):
    out[...] = block[half * 32 : half * 32 + 32]


def onward(half, block, cost):
    return pl.pallas_call(
        functools.partial(onward_kernel, half),
        out_shape=jax.ShapeDtypeStruct((32,) + block.shape[1:], BF16),
        in_specs=[VMEM],
        out_specs=VMEM,
        compiler_params=grant(2),
        cost_estimate=pl.CostEstimate(flops=cost, bytes_accessed=1 << 20, transcendentals=0),
        name="onward",
    )(block)


def gram_kernel(place, here, below, above, low, high, sides, two, keep, give, wide, thin, all_t, all_s):
    core, side, own, x = place[4], place[3], place[5], place[6]
    first = 0
    for away, tiles in ((0, here), (3, below), (1, above), (2, low), (2, high)):
        count = tiles.shape[0] * 16
        for i in range(8):
            wide[first : first + count, i * 128 : i * 128 + 128] = tiles[:, i].reshape(count, 128)
        z = 4 if tiles is high else 0
        for p in range(4):
            rows_z = sides[z : z + count // 32, (x + away) & 3, :, p]
            thin[first : first + count, p * 128 : p * 128 + 128] = rows_z.reshape(count, 128)
        first += count
    for p in range(4):
        part = lax.dot_general(thin[:, p * 128 : p * 128 + 128], wide[...], TRANSPOSED, preferred_element_type=F32)
        all_t[p * 128 : p * 128 + 128, :] = part
    mine = wide[:, pl.ds(pl.multiple_of(own * 128, 128), 128)]
    others = wide[:, pl.ds(pl.multiple_of(side * 512, 512), 512)]
    all_s[...] = lax.dot_general(mine, others, TRANSPOSED, preferred_element_type=F32)
    for which, target in ((core, keep), (1 - core, give)):
        for j in range(8):
            at = pl.multiple_of(j * 64 + which * 32, 32)
            target[j * 32 : j * 32 + 32, :] = all_t[pl.ds(at, 32), :]
        for q in range(4):
            at = pl.multiple_of(which * 256, 256)
            target[256:288, q * 256 : q * 256 + 256] = all_s[q * 32 : q * 32 + 32, pl.ds(at, 256)]
    at = pl.multiple_of((1 - core) * 16, 16)
    for q in range(2):
        give[288 + q * 16 : 304 + q * 16, :] = two[pl.ds(at, 16), q * 1024 : q * 1024 + 1024].astype(F32)


def gram(place, here, below, above, low, high, sides, two):
    tiles = (block.reshape(-1, 8, 16, 128) for block in (here, below, above, low, high))
    return pl.pallas_call(
        gram_kernel,
        out_shape=(jax.ShapeDtypeStruct((288, 1024), F32), jax.ShapeDtypeStruct((320, 1024), F32)),
        in_specs=[SMEM] + [VMEM] * 7,
        out_specs=(VMEM, VMEM),
        scratch_shapes=[
            pltpu.VMEM((1024, 1024), BF16),
            pltpu.VMEM((1024, 512), BF16),
            pltpu.VMEM((512, 1024), F32),
            pltpu.VMEM((128, 512), F32),
        ],
        compiler_params=grant(16),
        name="gram",
    )(place, *tiles, sides.reshape(8, 4, 2, 4, 16, 128), two)


def energy_kernel(scale, place, eps_occ, keep, got, eps_vir, mine, out, bmat, parts):
    tile, other, step, side, core, own = (place[n] for n in range(6))
    row_a = eps_vir[pl.ds(tile, 1), :]
    row_b = eps_vir[pl.ds(other, 1), :]
    first = side * 64 + core * 32
    col_b = jnp.sum(jnp.where(lanes((32, 128)) == rows((32, 128)) + first, row_b, 0.0), axis=1, keepdims=True)
    weight = jnp.where(step == 8, 1.0, 2.0)
    for i in range(8):
        for j in range(i, 8):
            there = slice(j * 32, j * 32 + 32), slice(i * 128, i * 128 + 128)
            here = slice(i * 32, i * 32 + 32), slice(j * 128, j * 128 + 128)
            one = keep[there] + got[there]
            two = keep[here] + got[here]
            denominators = (eps_occ[i] + eps_occ[j] - row_a) - col_b
            terms = (one * one + two * two - one * two) / denominators
            part = jnp.sum(terms, axis=0, keepdims=True) * weight
            parts[i * 8 + j : i * 8 + j + 1, :] = part
            parts[j * 8 + i : j * 8 + i + 1, :] = part
    square = (128, 128)
    eye = lanes(square) == rows(square)
    col_a = jnp.sum(jnp.where(eye, row_a, 0.0), axis=1, keepdims=True)
    for m in range(2):
        j = side * 4 + core * 2 + m
        block = jnp.concatenate(
            [
                keep[256:288, q * 256 + m * 128 : q * 256 + m * 128 + 128]
                + got[256:288, q * 256 + m * 128 : q * 256 + m * 128 + 128]
                for q in range(4)
            ],
            axis=0,
        )
        denominators = (eps_occ[own] + eps_occ[j] - row_a) - col_a
        terms = block * (2.0 * block - block.T) / denominators
        at = pl.ds(own * 8 + j, 1)
        parts[at, :] = parts[at, :] + jnp.sum(terms, axis=0, keepdims=True)
    column = jnp.sum(parts[...], axis=1, keepdims=True) * scale
    row = jnp.sum(jnp.where(lanes((64, 128)) == rows((64, 128)), column, 0.0), axis=0, keepdims=True)
    out[...] = jnp.broadcast_to(row[None], out.shape)
    here = pl.ds(pl.multiple_of(core * 16, 16), 16)
    bmat[here, :] = mine[here, :]
    there = pl.ds(pl.multiple_of((1 - core) * 16, 16), 16)
    for q in range(2):
        bmat[there, q * 1024 : q * 1024 + 1024] = got[288 + q * 16 : 304 + q * 16, :].astype(BF16)


def energies(scale, place, eps_occ, keep, got, eps_vir, two):
    return pl.pallas_call(
        functools.partial(energy_kernel, scale),
        out_shape=(jax.ShapeDtypeStruct((256, 1, 128), F32), jax.ShapeDtypeStruct(two.shape, BF16)),
        in_specs=[SMEM, SMEM, VMEM, VMEM, VMEM, VMEM],
        out_specs=(VMEM, VMEM),
        scratch_shapes=[pltpu.VMEM((64, 128), F32)],
        compiler_params=grant(8),
        name="energies",
    )(place, eps_occ, keep, got, eps_vir.reshape(-1, 128), two)


def position():
    z, x, yl, yh, core = (lax.axis_index(axis) for axis in AXES)
    tile, kind = z * 2 + yl, x * 4 + yh
    step, side = lax.shift_right_logical(kind, 1) + 1, kind & 1
    return jnp.stack([tile, (tile + step) & (TILES - 1), step, side, core, lax.shift_right_logical(kind, 1), x])


def last_kernel(got, out):
    row = jnp.broadcast_to(jnp.sum(got[...], axis=0), (8, 128))
    place = rows((8, 128))
    square = row
    for i in range(1, 8):
        square = jnp.where(place == i, pltpu.roll(row, 128 - 8 * i, 1), square)
    out[...] = square[:, :8]


def small(kernel, shape, name):
    return pl.pallas_call(
        kernel,
        out_shape=jax.ShapeDtypeStruct(shape, F32),
        in_specs=[VMEM],
        out_specs=VMEM,
        compiler_params=grant(2),
        name=name,
    )


def body(c_occ, c_vir, ints, blocks, screen, eps_occ, eps_vir):
    vir, occ = c_vir.shape[1], c_occ.shape[1]
    place = position()
    sent = half_transform(c_occ, ints, blocks, screen)
    recv = lax.all_to_all(sent, GRP, 0, 0, tiled=True)
    two, wide, thin = transform(recv, c_vir)
    here = lax.all_to_all(wide, ("z", "yl", "yh"), 0, 0, tiled=True)
    up = [(i, (i + 1) % 4) for i in range(4)]
    down = [(i, (i + 3) % 4) for i in range(4)]
    below, above = lax.ppermute(here, "x", up), lax.ppermute(here, "x", down)
    low = lax.ppermute(onward(0, above, 1 << 33), "x", down)
    high = lax.ppermute(onward(1, below, 1 << 35), "x", up)
    sides = lax.all_to_all(thin, CHIPS, 0, 0, tiled=True)

    keep, give = gram(place, here, below, above, low, high, sides, two)
    got = lax.ppermute(give, "core", [(0, 1), (1, 0)])
    scale = 1.0 / (float(vir) * float(vir) * 2048.0)
    energy, bmat = energies(scale, place, eps_occ, keep, got, eps_vir, two)
    energy = lax.all_to_all(energy, CHIPS, 0, 0, tiled=True)
    energy = lax.psum(small(last_kernel, (occ, occ), "last")(energy), "core")
    return bmat.reshape(1, 32, vir), energy


def solution(mesh):
    fine = Mesh(mesh.devices.reshape(8, 4, 2, 4, 2), AXES)
    return jax.shard_map(
        body,
        mesh=fine,
        in_specs=(P(), P(), P(GRP, PAIR, None), P(GRP, None), P(GRP), P(), P()),
        out_specs=(P(GRP, PAIR, None), P()),
        check_vma=False,
    )
```

```python
import functools

import jax
import jax.numpy as jnp
from jax import lax
from jax.experimental import pallas as pl
from jax.experimental.pallas import tpu as pltpu
from jax.sharding import Mesh, PartitionSpec as P

SHELL = 64
SHELLS = 12
TILES = 16
CHUNKS = 3
AXES = ("zh", "zl", "x", "yl", "yh", "core")
CHIPS = ("zh", "zl", "x", "yl", "yh")
PAIR = ("zh", "zl", "x", "yl")
NEAR = ("zl", "x", "yl", "core")
FAR = ("zh", "yh")
GRP = ("yh", "core")
F32 = jnp.float32
BF16 = jnp.bfloat16
VMEM = pl.BlockSpec(memory_space=pltpu.VMEM)
SMEM = pl.BlockSpec(memory_space=pltpu.SMEM)
HBM = pl.BlockSpec(memory_space=pltpu.HBM)
TRANSPOSED = (((0,), (0,)), ((), ()))


def lanes(shape):
    return lax.broadcasted_iota(jnp.int32, shape, 1)


def grant(mib):
    return pltpu.CompilerParams(vmem_limit_bytes=mib * 1024 * 1024)


def rows(shape):
    return lax.broadcasted_iota(jnp.int32, shape, 0)


def half_kernel(blocks_at, screen_at, c_occ_at, ints, out, blocks, screen, c_occ, held, spread, coef, sems):
    count = held.shape[0]
    first = [
        pltpu.make_async_copy(blocks_at, blocks, sems.at[count]),
        pltpu.make_async_copy(screen_at, screen, sems.at[count + 1]),
        pltpu.make_async_copy(c_occ_at, c_occ, sems.at[count + 2]),
    ]
    for copy in first:
        copy.start()
    for b in range(count):
        pltpu.make_async_copy(ints.at[b], held.at[b], sems.at[b]).start()
    shape = (SHELL, 4096)
    spread[...] = (lanes(shape) // SHELL == rows(shape)).astype(F32).astype(BF16)
    for copy in first:
        copy.wait()
    own = []
    for b in range(count):
        first = blocks[0, b]
        at = pl.multiple_of((first // 2) * 128, 128)
        shell = pltpu.roll(c_occ[:, pl.ds(at, 128)].astype(F32), (first % 2) * SHELL, 1)[:, :SHELL]
        own.append(shell * screen[b].astype(F32))
    own = jnp.concatenate(own, axis=0).astype(BF16)
    coef[...] = jnp.dot(own, spread[...], preferred_element_type=F32).reshape(count, 8, 4096)
    left = lanes((32, 128)) < SHELL

    @pl.loop(0, count)
    def _(block):
        pltpu.make_async_copy(ints.at[block], held.at[block], sems.at[block]).wait()

        def step(t, sums):
            at = pl.multiple_of(t * 128, 128)
            tile = held[block, :, pl.ds(at, 128)].astype(F32)
            weights = coef[block, :, pl.ds(at, 128)]
            return tuple(sums[i] + tile * weights[i : i + 1] for i in range(8))

        sums = lax.fori_loop(0, 32, step, (jnp.zeros((32, 128), F32),) * 8, unroll=8)
        full = [s + pltpu.roll(s, SHELL, 1) for s in sums]
        shell = blocks[1, block].astype(F32)
        put = pl.multiple_of(block * 16, 16)
        for yh in range(4):
            both = jnp.where(left, full[2 * yh], full[2 * yh + 1])
            for core in range(2):
                d = yh * 2 + core
                out[d, pl.ds(put, 16), :] = both[core * 16 : core * 16 + 16]
                out[d, 64:72, :] = jnp.where(rows((8, 128)) == block, shell, out[d, 64:72, :])


def half_transform(c_occ, ints, blocks, screen):
    return pl.pallas_call(
        half_kernel,
        out_shape=jax.ShapeDtypeStruct((8, 72, 128), F32),
        in_specs=[HBM, HBM, HBM, HBM],
        out_specs=VMEM,
        scratch_shapes=[
            pltpu.SMEM((2, ints.shape[0]), jnp.int32),
            pltpu.SMEM(screen.shape, jnp.int32),
            pltpu.VMEM((8, c_occ.shape[0]), BF16),
            pltpu.VMEM(ints.shape, BF16),
            pltpu.VMEM((SHELL, 4096), BF16),
            pltpu.VMEM((ints.shape[0], 8, 4096), F32),
            pltpu.SemaphoreType.DMA((ints.shape[0] + 3,)),
        ],
        compiler_params=grant(54),
        name="half",
    )(blocks.T, screen, c_occ.T, ints)


def rounded(x):
    return x.astype(BF16).astype(F32)


def finish(q, full, left, bmat, sides):
    bmat[:, q * 256 : q * 256 + 256] = full.astype(BF16)
    for t in range(2):
        one, two = full[0:16, t * 128 : t * 128 + 128], full[16:32, t * 128 : t * 128 + 128]
        tile = q * 2 + t
        sides[tile * 2] = jnp.where(left, one, pltpu.roll(two, SHELL, 1)).astype(BF16)
        sides[tile * 2 + 1] = jnp.where(left, pltpu.roll(one, SHELL, 1), two).astype(BF16)


def transform_kernel(recv_at, c_vir, bmat, wide, thin, recv, held, terms, sides, total, sems):
    arrive = pltpu.make_async_copy(recv_at, recv, sems.at[CHUNKS])
    arrive.start()
    copies = []
    for m in range(CHUNKS):
        part = pl.ds(m * 256, 256)
        copies.append(pltpu.make_async_copy(c_vir.at[part], held.at[part], sems.at[m]))
        copies[m].start()
    arrive.wait()
    left = lanes((16, 128)) < SHELL
    sums = [jnp.zeros((16, 128), F32) for _ in range(SHELLS)]
    for source in range(8):
        for b in range(4):
            data = recv[source, b * 16 : b * 16 + 16, :]
            shell = recv[source, 64 + b : 65 + b, :]
            for n in range(SHELLS):
                sums[n] = sums[n] + jnp.where(shell == float(n), data, 0.0)
    for m in range(SHELLS // 2):
        one, two = sums[2 * m], sums[2 * m + 1]
        pair = (
            jnp.where(left, one, pltpu.roll(two, SHELL, 1)),
            jnp.where(left, pltpu.roll(one, SHELL, 1), two),
        )
        for i in range(2):
            value = pair[i]
            for term in range(3):
                part = rounded(value)
                terms[term * 32 + i * 16 : term * 32 + i * 16 + 16, m * 128 : m * 128 + 128] = part.astype(BF16)
                value = value - part
    for m in range(CHUNKS):
        copies[m].wait()
        some = terms[:, m * 256 : m * 256 + 256]
        for q in range(TILES // 2):
            columns = slice(q * 256, q * 256 + 256)
            got = jnp.dot(some, held[m * 256 : m * 256 + 256, columns], preferred_element_type=F32)
            if m < CHUNKS - 1:
                total[:, columns] = got if m == 0 else total[:, columns] + got
                continue
            got = total[:, columns] + got
            full = (got[64:96] + got[32:64]) + got[0:32]
            finish(q, full, left, bmat, sides)
    for r in range(TILES):
        for yh in range(4):
            wide[r * 4 + yh] = bmat[:, r * 128 : r * 128 + 128]
            for x in range(4):
                kind = x * 4 + yh
                other = (r + kind // 2 + 1) % TILES
                thin[((r // 2 * 4 + x) * 2 + r % 2) * 4 + yh] = sides[other * 2 + kind % 2]


def transform(recv, c_vir):
    return pl.pallas_call(
        transform_kernel,
        out_shape=(
            jax.ShapeDtypeStruct((32, c_vir.shape[1]), BF16),
            jax.ShapeDtypeStruct((64, 32, 128), BF16),
            jax.ShapeDtypeStruct((256, 16, 128), BF16),
        ),
        in_specs=[HBM, HBM],
        out_specs=(VMEM, VMEM, VMEM),
        scratch_shapes=[
            pltpu.VMEM(recv.shape, F32),
            pltpu.VMEM(c_vir.shape, BF16),
            pltpu.VMEM((96, c_vir.shape[0]), BF16),
            pltpu.VMEM((32, 16, 128), BF16),
            pltpu.VMEM((96, c_vir.shape[1]), F32),
            pltpu.SemaphoreType.DMA((CHUNKS + 1,)),
        ],
        compiler_params=grant(52),
        name="transform",
    )(recv, c_vir)


def onward_kernel(below, above, low, high):
    low[...] = above[0:32]
    high[...] = below[32:64]


def onward(below, above):
    half = jax.ShapeDtypeStruct((32,) + below.shape[1:], BF16)
    return pl.pallas_call(
        onward_kernel,
        out_shape=(half, half),
        in_specs=[VMEM, VMEM],
        out_specs=(VMEM, VMEM),
        compiler_params=grant(4),
        cost_estimate=pl.CostEstimate(flops=1 << 35, bytes_accessed=1 << 21, transcendentals=0),
        name="onward",
    )(below, above)


def gram_kernel(place, here, below, above, low, high, sides, two, keep, give, wide, thin, all_t, all_s):
    core, side, own, x = place[4], place[3], place[5], place[6]
    first = 0
    for away, tiles in ((0, here), (3, below), (1, above), (2, low), (2, high)):
        count = tiles.shape[0] * 16
        for i in range(8):
            wide[first : first + count, i * 128 : i * 128 + 128] = tiles[:, i].reshape(count, 128)
        z = 4 if tiles is high else 0
        for p in range(4):
            rows_z = sides[z : z + count // 32, (x + away) & 3, :, p]
            thin[first : first + count, p * 128 : p * 128 + 128] = rows_z.reshape(count, 128)
        first += count
    for p in range(4):
        part = lax.dot_general(thin[:, p * 128 : p * 128 + 128], wide[...], TRANSPOSED, preferred_element_type=F32)
        all_t[p * 128 : p * 128 + 128, :] = part
    mine = wide[:, pl.ds(pl.multiple_of(own * 128, 128), 128)]
    others = wide[:, pl.ds(pl.multiple_of(side * 512, 512), 512)]
    all_s[...] = lax.dot_general(mine, others, TRANSPOSED, preferred_element_type=F32)
    for which, target in ((core, keep), (1 - core, give)):
        for j in range(8):
            at = pl.multiple_of(j * 64 + which * 32, 32)
            target[j * 32 : j * 32 + 32, :] = all_t[pl.ds(at, 32), :]
        for q in range(4):
            at = pl.multiple_of(which * 256, 256)
            target[256:288, q * 256 : q * 256 + 256] = all_s[q * 32 : q * 32 + 32, pl.ds(at, 256)]
    at = pl.multiple_of((1 - core) * 16, 16)
    for q in range(2):
        give[288 + q * 16 : 304 + q * 16, :] = two[pl.ds(at, 16), q * 1024 : q * 1024 + 1024].astype(F32)


def gram(place, here, below, above, low, high, sides, two):
    tiles = (block.reshape(-1, 8, 16, 128) for block in (here, below, above, low, high))
    return pl.pallas_call(
        gram_kernel,
        out_shape=(jax.ShapeDtypeStruct((288, 1024), F32), jax.ShapeDtypeStruct((320, 1024), F32)),
        in_specs=[SMEM] + [VMEM] * 7,
        out_specs=(VMEM, VMEM),
        scratch_shapes=[
            pltpu.VMEM((1024, 1024), BF16),
            pltpu.VMEM((1024, 512), BF16),
            pltpu.VMEM((512, 1024), F32),
            pltpu.VMEM((128, 512), F32),
        ],
        compiler_params=grant(16),
        name="gram",
    )(place, *tiles, sides.reshape(8, 4, 2, 4, 16, 128), two)


def energy_kernel(scale, place, eps_occ, keep, got, eps_vir, mine, out, bmat, parts):
    tile, other, step, side, core, own = (place[n] for n in range(6))
    row_a = eps_vir[pl.ds(tile, 1), :]
    row_b = eps_vir[pl.ds(other, 1), :]
    first = side * 64 + core * 32
    col_b = jnp.sum(jnp.where(lanes((32, 128)) == rows((32, 128)) + first, row_b, 0.0), axis=1, keepdims=True)
    weight = jnp.where(step == 8, 1.0, 2.0)
    for i in range(8):
        for j in range(i, 8):
            there = slice(j * 32, j * 32 + 32), slice(i * 128, i * 128 + 128)
            here = slice(i * 32, i * 32 + 32), slice(j * 128, j * 128 + 128)
            one = keep[there] + got[there]
            two = keep[here] + got[here]
            denominators = (eps_occ[i] + eps_occ[j] - row_a) - col_b
            terms = (one * one + two * two - one * two) / denominators
            part = jnp.sum(terms, axis=0, keepdims=True) * weight
            parts[i * 8 + j : i * 8 + j + 1, :] = part
            parts[j * 8 + i : j * 8 + i + 1, :] = part
    square = (128, 128)
    eye = lanes(square) == rows(square)
    col_a = jnp.sum(jnp.where(eye, row_a, 0.0), axis=1, keepdims=True)
    for m in range(2):
        j = side * 4 + core * 2 + m
        block = jnp.concatenate(
            [
                keep[256:288, q * 256 + m * 128 : q * 256 + m * 128 + 128]
                + got[256:288, q * 256 + m * 128 : q * 256 + m * 128 + 128]
                for q in range(4)
            ],
            axis=0,
        )
        denominators = (eps_occ[own] + eps_occ[j] - row_a) - col_a
        terms = block * (2.0 * block - block.T) / denominators
        at = pl.ds(own * 8 + j, 1)
        parts[at, :] = parts[at, :] + jnp.sum(terms, axis=0, keepdims=True)
    column = jnp.sum(parts[...], axis=1, keepdims=True) * scale
    row = jnp.sum(jnp.where(lanes((64, 128)) == rows((64, 128)), column, 0.0), axis=0, keepdims=True)
    out[...] = jnp.broadcast_to(row[None], out.shape)
    here = pl.ds(pl.multiple_of(core * 16, 16), 16)
    bmat[here, :] = mine[here, :]
    there = pl.ds(pl.multiple_of((1 - core) * 16, 16), 16)
    for q in range(2):
        bmat[there, q * 1024 : q * 1024 + 1024] = got[288 + q * 16 : 304 + q * 16, :].astype(BF16)


def energies(scale, place, eps_occ, keep, got, eps_vir, two):
    return pl.pallas_call(
        functools.partial(energy_kernel, scale),
        out_shape=(jax.ShapeDtypeStruct((32, 1, 128), F32), jax.ShapeDtypeStruct(two.shape, BF16)),
        in_specs=[SMEM, SMEM, VMEM, VMEM, VMEM, VMEM],
        out_specs=(VMEM, VMEM),
        scratch_shapes=[pltpu.VMEM((64, 128), F32)],
        compiler_params=grant(8),
        name="energies",
    )(place, eps_occ, keep, got, eps_vir.reshape(-1, 128), two)


def position():
    zh, zl, x, yl, yh, core = (lax.axis_index(axis) for axis in AXES)
    tile, kind = zh * 4 + zl * 2 + yl, x * 4 + yh
    step, side = lax.shift_right_logical(kind, 1) + 1, kind & 1
    return jnp.stack([tile, (tile + step) & (TILES - 1), step, side, core, lax.shift_right_logical(kind, 1), x])


def again_kernel(got, out):
    out[...] = jnp.broadcast_to(jnp.sum(got[...], axis=0)[None], out.shape)


def last_kernel(got, out):
    row = jnp.broadcast_to(jnp.sum(got[...], axis=0), (8, 128))
    place = rows((8, 128))
    square = row
    for i in range(1, 8):
        square = jnp.where(place == i, pltpu.roll(row, 128 - 8 * i, 1), square)
    out[...] = square[:, :8]


def small(kernel, shape, name):
    return pl.pallas_call(
        kernel,
        out_shape=jax.ShapeDtypeStruct(shape, F32),
        in_specs=[VMEM],
        out_specs=VMEM,
        compiler_params=grant(2),
        name=name,
    )


def body(c_occ, c_vir, ints, blocks, screen, eps_occ, eps_vir):
    vir, occ = c_vir.shape[1], c_occ.shape[1]
    place = position()
    sent = half_transform(c_occ, ints, blocks, screen)
    recv = lax.all_to_all(sent, GRP, 0, 0, tiled=True)
    two, wide, thin = transform(recv, c_vir)
    here = lax.all_to_all(wide, ("zh", "zl", "yl", "yh"), 0, 0, tiled=True)
    up = [(i, (i + 1) % 4) for i in range(4)]
    down = [(i, (i + 3) % 4) for i in range(4)]
    below, above = lax.ppermute(here, "x", up), lax.ppermute(here, "x", down)
    low, high = onward(below, above)
    low, high = lax.ppermute(low, "x", down), lax.ppermute(high, "x", up)
    sides = lax.all_to_all(thin, CHIPS, 0, 0, tiled=True)

    keep, give = gram(place, here, below, above, low, high, sides, two)
    got = lax.ppermute(give, "core", [(0, 1), (1, 0)])
    scale = 1.0 / (float(vir) * float(vir) * 2048.0)
    energy, bmat = energies(scale, place, eps_occ, keep, got, eps_vir, two)
    energy = lax.all_to_all(energy, NEAR, 0, 0, tiled=True)
    energy = lax.all_to_all(small(again_kernel, (16, 1, 128), "again")(energy), FAR, 0, 0, tiled=True)
    energy = small(last_kernel, (occ, occ), "last")(energy)
    return bmat.reshape(1, 32, vir), energy


def solution(mesh):
    fine = Mesh(mesh.devices.reshape(4, 2, 4, 2, 4, 2), AXES)
    return jax.shard_map(
        body,
        mesh=fine,
        in_specs=(P(), P(), P(GRP, PAIR, None), P(GRP, None), P(GRP), P(), P()),
        out_specs=(P(GRP, PAIR, None), P()),
        check_vma=False,
    )
```

```python
import functools

import jax
import jax.numpy as jnp
from jax import lax
from jax.experimental import pallas as pl
from jax.experimental.pallas import tpu as pltpu
from jax.sharding import Mesh, PartitionSpec as P

SHELL = 64
SHELLS = 12
TILES = 16
AXES = ("zh", "zl", "x", "yl", "yh", "core")
CHIPS = ("zh", "zl", "x", "yl", "yh")
PAIR = ("zh", "zl", "x", "yl")
NEAR = ("zl", "x", "yl", "core")
FAR = ("zh", "yh")
GRP = ("yh", "core")
F32 = jnp.float32
BF16 = jnp.bfloat16
VMEM = pl.BlockSpec(memory_space=pltpu.VMEM)
SMEM = pl.BlockSpec(memory_space=pltpu.SMEM)
HBM = pl.BlockSpec(memory_space=pltpu.HBM)
TRANSPOSED = (((0,), (0,)), ((), ()))


def lanes(shape):
    return lax.broadcasted_iota(jnp.int32, shape, 1)


def grant(mib):
    return pltpu.CompilerParams(vmem_limit_bytes=mib * 1024 * 1024)


def rows(shape):
    return lax.broadcasted_iota(jnp.int32, shape, 0)


def half_kernel(blocks_at, screen_at, c_occ_at, ints, out, blocks, screen, c_occ, held, spread, coef, sems):
    count = held.shape[0]
    first = [
        pltpu.make_async_copy(blocks_at, blocks, sems.at[count]),
        pltpu.make_async_copy(screen_at, screen, sems.at[count + 1]),
        pltpu.make_async_copy(c_occ_at, c_occ, sems.at[count + 2]),
    ]
    for copy in first:
        copy.start()
    for b in range(count):
        pltpu.make_async_copy(ints.at[b], held.at[b], sems.at[b]).start()
    shape = (SHELL, 4096)
    spread[...] = (lanes(shape) // SHELL == rows(shape)).astype(F32).astype(BF16)
    for copy in first:
        copy.wait()
    own = []
    for b in range(count):
        first = blocks[0, b]
        at = pl.multiple_of((first // 2) * 128, 128)
        shell = pltpu.roll(c_occ[:, pl.ds(at, 128)].astype(F32), (first % 2) * SHELL, 1)[:, :SHELL]
        own.append(shell * screen[b].astype(F32))
    own = jnp.concatenate(own, axis=0).astype(BF16)
    coef[...] = jnp.dot(own, spread[...], preferred_element_type=F32).reshape(count, 8, 4096)
    left = lanes((32, 128)) < SHELL

    @pl.loop(0, count)
    def _(block):
        pltpu.make_async_copy(ints.at[block], held.at[block], sems.at[block]).wait()

        def step(t, sums):
            at = pl.multiple_of(t * 128, 128)
            tile = held[block, :, pl.ds(at, 128)].astype(F32)
            weights = coef[block, :, pl.ds(at, 128)]
            return tuple(sums[i] + tile * weights[i : i + 1] for i in range(8))

        sums = lax.fori_loop(0, 32, step, (jnp.zeros((32, 128), F32),) * 8, unroll=8)
        full = [s + pltpu.roll(s, SHELL, 1) for s in sums]
        shell = blocks[1, block].astype(F32)
        put = pl.multiple_of(block * 16, 16)
        for yh in range(4):
            both = jnp.where(left, full[2 * yh], full[2 * yh + 1])
            for core in range(2):
                d = yh * 2 + core
                out[d, pl.ds(put, 16), :] = both[core * 16 : core * 16 + 16]
                out[d, 64:72, :] = jnp.where(rows((8, 128)) == block, shell, out[d, 64:72, :])


def half_transform(c_occ, ints, blocks, screen):
    return pl.pallas_call(
        half_kernel,
        out_shape=jax.ShapeDtypeStruct((8, 72, 128), F32),
        in_specs=[HBM, HBM, HBM, HBM],
        out_specs=VMEM,
        scratch_shapes=[
            pltpu.SMEM((2, ints.shape[0]), jnp.int32),
            pltpu.SMEM(screen.shape, jnp.int32),
            pltpu.VMEM((8, c_occ.shape[0]), BF16),
            pltpu.VMEM(ints.shape, BF16),
            pltpu.VMEM((SHELL, 4096), BF16),
            pltpu.VMEM((ints.shape[0], 8, 4096), F32),
            pltpu.SemaphoreType.DMA((ints.shape[0] + 3,)),
        ],
        compiler_params=grant(54),
        name="half",
    )(blocks.T, screen, c_occ.T, ints)


def hold_kernel(c_vir, out, sem):
    copy = pltpu.make_async_copy(c_vir, out, sem)
    copy.start()
    copy.wait()


def hold(c_vir):
    return pl.pallas_call(
        hold_kernel,
        out_shape=jax.ShapeDtypeStruct(c_vir.shape, BF16),
        in_specs=[HBM],
        out_specs=VMEM,
        scratch_shapes=[pltpu.SemaphoreType.DMA],
        compiler_params=grant(50),
        cost_estimate=pl.CostEstimate(flops=1 << 33, bytes_accessed=1 << 22, transcendentals=0),
        name="hold",
    )(c_vir)


def rounded(x):
    return x.astype(BF16).astype(F32)


def finish(q, full, left, bmat, sides):
    bmat[:, q * 256 : q * 256 + 256] = full.astype(BF16)
    for t in range(2):
        one, two = full[0:16, t * 128 : t * 128 + 128], full[16:32, t * 128 : t * 128 + 128]
        tile = q * 2 + t
        sides[tile * 2] = jnp.where(left, one, pltpu.roll(two, SHELL, 1)).astype(BF16)
        sides[tile * 2 + 1] = jnp.where(left, pltpu.roll(one, SHELL, 1), two).astype(BF16)


def transform_kernel(recv, c_vir, bmat, wide, thin, terms, sides):
    left = lanes((16, 128)) < SHELL
    sums = [jnp.zeros((16, 128), F32) for _ in range(SHELLS)]
    for source in range(8):
        for b in range(4):
            data = recv[source, b * 16 : b * 16 + 16, :]
            shell = recv[source, 64 + b : 65 + b, :]
            for n in range(SHELLS):
                sums[n] = sums[n] + jnp.where(shell == float(n), data, 0.0)
    for m in range(SHELLS // 2):
        one, two = sums[2 * m], sums[2 * m + 1]
        pair = (
            jnp.where(left, one, pltpu.roll(two, SHELL, 1)),
            jnp.where(left, pltpu.roll(one, SHELL, 1), two),
        )
        for i in range(2):
            value = pair[i]
            for term in range(3):
                part = rounded(value)
                terms[term * 32 + i * 16 : term * 32 + i * 16 + 16, m * 128 : m * 128 + 128] = part.astype(BF16)
                value = value - part
    for q in range(TILES // 2):
        got = jnp.dot(terms[...], c_vir[:, q * 256 : q * 256 + 256], preferred_element_type=F32)
        full = (got[64:96] + got[32:64]) + got[0:32]
        finish(q, full, left, bmat, sides)
    for r in range(TILES):
        for yh in range(4):
            wide[r * 4 + yh] = bmat[:, r * 128 : r * 128 + 128]
            for x in range(4):
                kind = x * 4 + yh
                other = (r + kind // 2 + 1) % TILES
                thin[((r // 2 * 4 + x) * 2 + r % 2) * 4 + yh] = sides[other * 2 + kind % 2]


def transform(recv, c_vir):
    return pl.pallas_call(
        transform_kernel,
        out_shape=(
            jax.ShapeDtypeStruct((32, c_vir.shape[1]), BF16),
            jax.ShapeDtypeStruct((64, 32, 128), BF16),
            jax.ShapeDtypeStruct((256, 16, 128), BF16),
        ),
        in_specs=[VMEM, VMEM],
        out_specs=(VMEM, VMEM, VMEM),
        scratch_shapes=[pltpu.VMEM((96, c_vir.shape[0]), BF16), pltpu.VMEM((32, 16, 128), BF16)],
        compiler_params=grant(16),
        name="transform",
    )(recv, c_vir)


def onward_kernel(below, above, low, high):
    low[...] = above[0:32]
    high[...] = below[32:64]


def onward(below, above):
    half = jax.ShapeDtypeStruct((32,) + below.shape[1:], BF16)
    return pl.pallas_call(
        onward_kernel,
        out_shape=(half, half),
        in_specs=[VMEM, VMEM],
        out_specs=(VMEM, VMEM),
        compiler_params=grant(4),
        cost_estimate=pl.CostEstimate(flops=1 << 35, bytes_accessed=1 << 21, transcendentals=0),
        name="onward",
    )(below, above)


def gram_kernel(place, here, below, above, low, high, sides, two, keep, give, wide, thin, all_t, all_s):
    core, side, own, x = place[4], place[3], place[5], place[6]
    first = 0
    for away, tiles in ((0, here), (3, below), (1, above), (2, low), (2, high)):
        count = tiles.shape[0] * 16
        for i in range(8):
            wide[first : first + count, i * 128 : i * 128 + 128] = tiles[:, i].reshape(count, 128)
        z = 4 if tiles is high else 0
        for p in range(4):
            rows_z = sides[z : z + count // 32, (x + away) & 3, :, p]
            thin[first : first + count, p * 128 : p * 128 + 128] = rows_z.reshape(count, 128)
        first += count
    for p in range(4):
        part = lax.dot_general(thin[:, p * 128 : p * 128 + 128], wide[...], TRANSPOSED, preferred_element_type=F32)
        all_t[p * 128 : p * 128 + 128, :] = part
    mine = wide[:, pl.ds(pl.multiple_of(own * 128, 128), 128)]
    others = wide[:, pl.ds(pl.multiple_of(side * 512, 512), 512)]
    all_s[...] = lax.dot_general(mine, others, TRANSPOSED, preferred_element_type=F32)
    for which, target in ((core, keep), (1 - core, give)):
        for j in range(8):
            at = pl.multiple_of(j * 64 + which * 32, 32)
            target[j * 32 : j * 32 + 32, :] = all_t[pl.ds(at, 32), :]
        for q in range(4):
            at = pl.multiple_of(which * 256, 256)
            target[256:288, q * 256 : q * 256 + 256] = all_s[q * 32 : q * 32 + 32, pl.ds(at, 256)]
    at = pl.multiple_of((1 - core) * 16, 16)
    for q in range(2):
        give[288 + q * 16 : 304 + q * 16, :] = two[pl.ds(at, 16), q * 1024 : q * 1024 + 1024].astype(F32)


def gram(place, here, below, above, low, high, sides, two):
    tiles = (block.reshape(-1, 8, 16, 128) for block in (here, below, above, low, high))
    return pl.pallas_call(
        gram_kernel,
        out_shape=(jax.ShapeDtypeStruct((288, 1024), F32), jax.ShapeDtypeStruct((320, 1024), F32)),
        in_specs=[SMEM] + [VMEM] * 7,
        out_specs=(VMEM, VMEM),
        scratch_shapes=[
            pltpu.VMEM((1024, 1024), BF16),
            pltpu.VMEM((1024, 512), BF16),
            pltpu.VMEM((512, 1024), F32),
            pltpu.VMEM((128, 512), F32),
        ],
        compiler_params=grant(16),
        name="gram",
    )(place, *tiles, sides.reshape(8, 4, 2, 4, 16, 128), two)


def energy_kernel(scale, place, eps_occ, keep, got, eps_vir, mine, out, bmat, parts):
    tile, other, step, side, core, own = (place[n] for n in range(6))
    row_a = eps_vir[pl.ds(tile, 1), :]
    row_b = eps_vir[pl.ds(other, 1), :]
    first = side * 64 + core * 32
    col_b = jnp.sum(jnp.where(lanes((32, 128)) == rows((32, 128)) + first, row_b, 0.0), axis=1, keepdims=True)
    weight = jnp.where(step == 8, 1.0, 2.0)
    for i in range(8):
        for j in range(i, 8):
            there = slice(j * 32, j * 32 + 32), slice(i * 128, i * 128 + 128)
            here = slice(i * 32, i * 32 + 32), slice(j * 128, j * 128 + 128)
            one = keep[there] + got[there]
            two = keep[here] + got[here]
            denominators = (eps_occ[i] + eps_occ[j] - row_a) - col_b
            terms = (one * one + two * two - one * two) / denominators
            part = jnp.sum(terms, axis=0, keepdims=True) * weight
            parts[i * 8 + j : i * 8 + j + 1, :] = part
            parts[j * 8 + i : j * 8 + i + 1, :] = part
    square = (128, 128)
    eye = lanes(square) == rows(square)
    col_a = jnp.sum(jnp.where(eye, row_a, 0.0), axis=1, keepdims=True)
    for m in range(2):
        j = side * 4 + core * 2 + m
        block = jnp.concatenate(
            [
                keep[256:288, q * 256 + m * 128 : q * 256 + m * 128 + 128]
                + got[256:288, q * 256 + m * 128 : q * 256 + m * 128 + 128]
                for q in range(4)
            ],
            axis=0,
        )
        denominators = (eps_occ[own] + eps_occ[j] - row_a) - col_a
        terms = block * (2.0 * block - block.T) / denominators
        at = pl.ds(own * 8 + j, 1)
        parts[at, :] = parts[at, :] + jnp.sum(terms, axis=0, keepdims=True)
    column = jnp.sum(parts[...], axis=1, keepdims=True) * scale
    row = jnp.sum(jnp.where(lanes((64, 128)) == rows((64, 128)), column, 0.0), axis=0, keepdims=True)
    out[...] = jnp.broadcast_to(row[None], out.shape)
    here = pl.ds(pl.multiple_of(core * 16, 16), 16)
    bmat[here, :] = mine[here, :]
    there = pl.ds(pl.multiple_of((1 - core) * 16, 16), 16)
    for q in range(2):
        bmat[there, q * 1024 : q * 1024 + 1024] = got[288 + q * 16 : 304 + q * 16, :].astype(BF16)


def energies(scale, place, eps_occ, keep, got, eps_vir, two):
    return pl.pallas_call(
        functools.partial(energy_kernel, scale),
        out_shape=(jax.ShapeDtypeStruct((32, 1, 128), F32), jax.ShapeDtypeStruct(two.shape, BF16)),
        in_specs=[SMEM, SMEM, VMEM, VMEM, VMEM, VMEM],
        out_specs=(VMEM, VMEM),
        scratch_shapes=[pltpu.VMEM((64, 128), F32)],
        compiler_params=grant(8),
        name="energies",
    )(place, eps_occ, keep, got, eps_vir.reshape(-1, 128), two)


def position():
    zh, zl, x, yl, yh, core = (lax.axis_index(axis) for axis in AXES)
    tile, kind = zh * 4 + zl * 2 + yl, x * 4 + yh
    step, side = lax.shift_right_logical(kind, 1) + 1, kind & 1
    return jnp.stack([tile, (tile + step) & (TILES - 1), step, side, core, lax.shift_right_logical(kind, 1), x])


def again_kernel(got, out):
    out[...] = jnp.broadcast_to(jnp.sum(got[...], axis=0)[None], out.shape)


def last_kernel(got, out):
    row = jnp.broadcast_to(jnp.sum(got[...], axis=0), (8, 128))
    place = rows((8, 128))
    square = row
    for i in range(1, 8):
        square = jnp.where(place == i, pltpu.roll(row, 128 - 8 * i, 1), square)
    out[...] = square[:, :8]


def small(kernel, shape, name):
    return pl.pallas_call(
        kernel,
        out_shape=jax.ShapeDtypeStruct(shape, F32),
        in_specs=[VMEM],
        out_specs=VMEM,
        compiler_params=grant(2),
        name=name,
    )


def body(c_occ, c_vir, ints, blocks, screen, eps_occ, eps_vir):
    vir, occ = c_vir.shape[1], c_occ.shape[1]
    place = position()
    sent = half_transform(c_occ, ints, blocks, screen)
    recv = lax.all_to_all(sent, GRP, 0, 0, tiled=True)
    two, wide, thin = transform(recv, hold(c_vir))
    here = lax.all_to_all(wide, ("zh", "zl", "yl", "yh"), 0, 0, tiled=True)
    up = [(i, (i + 1) % 4) for i in range(4)]
    down = [(i, (i + 3) % 4) for i in range(4)]
    below, above = lax.ppermute(here, "x", up), lax.ppermute(here, "x", down)
    low, high = onward(below, above)
    low, high = lax.ppermute(low, "x", down), lax.ppermute(high, "x", up)
    sides = lax.all_to_all(thin, CHIPS, 0, 0, tiled=True)

    keep, give = gram(place, here, below, above, low, high, sides, two)
    got = lax.ppermute(give, "core", [(0, 1), (1, 0)])
    scale = 1.0 / (float(vir) * float(vir) * 2048.0)
    energy, bmat = energies(scale, place, eps_occ, keep, got, eps_vir, two)
    energy = lax.all_to_all(energy, NEAR, 0, 0, tiled=True)
    energy = lax.all_to_all(small(again_kernel, (16, 1, 128), "again")(energy), FAR, 0, 0, tiled=True)
    energy = small(last_kernel, (occ, occ), "last")(energy)
    return bmat.reshape(1, 32, vir), energy


def solution(mesh):
    fine = Mesh(mesh.devices.reshape(4, 2, 4, 2, 4, 2), AXES)
    return jax.shard_map(
        body,
        mesh=fine,
        in_specs=(P(), P(), P(GRP, PAIR, None), P(GRP, None), P(GRP), P(), P()),
        out_specs=(P(GRP, PAIR, None), P()),
        check_vma=False,
    )
```

```python
import functools

import jax
import jax.numpy as jnp
from jax import lax
from jax.experimental import pallas as pl
from jax.experimental.pallas import tpu as pltpu
from jax.sharding import Mesh, PartitionSpec as P

SHELL = 64
SHELLS = 12
TILES = 16
AXES = ("zh", "zl", "x", "yl", "yh", "core")
CHIPS = ("zh", "zl", "x", "yl", "yh")
PAIR = ("zh", "zl", "x", "yl")
NEAR = ("zl", "x", "yl", "core")
FAR = ("zh", "yh")
GRP = ("yh", "core")
F32 = jnp.float32
BF16 = jnp.bfloat16
VMEM = pl.BlockSpec(memory_space=pltpu.VMEM)
SMEM = pl.BlockSpec(memory_space=pltpu.SMEM)
HBM = pl.BlockSpec(memory_space=pltpu.HBM)
TRANSPOSED = (((0,), (0,)), ((), ()))


def lanes(shape):
    return lax.broadcasted_iota(jnp.int32, shape, 1)


def grant(mib):
    return pltpu.CompilerParams(vmem_limit_bytes=mib * 1024 * 1024)


def rows(shape):
    return lax.broadcasted_iota(jnp.int32, shape, 0)


def half_kernel(blocks_at, screen_at, c_occ_at, ints, out, blocks, screen, c_occ, held, spread, coef, sems):
    count = held.shape[0]
    first = [
        pltpu.make_async_copy(blocks_at, blocks, sems.at[count]),
        pltpu.make_async_copy(screen_at, screen, sems.at[count + 1]),
        pltpu.make_async_copy(c_occ_at, c_occ, sems.at[count + 2]),
    ]
    for copy in first:
        copy.start()
    for b in range(count):
        pltpu.make_async_copy(ints.at[b], held.at[b], sems.at[b]).start()
    shape = (SHELL, 4096)
    spread[...] = (lanes(shape) // SHELL == rows(shape)).astype(F32).astype(BF16)
    for copy in first:
        copy.wait()
    own = []
    for b in range(count):
        first = blocks[0, b]
        at = pl.multiple_of((first // 2) * 128, 128)
        shell = pltpu.roll(c_occ[:, pl.ds(at, 128)].astype(F32), (first % 2) * SHELL, 1)[:, :SHELL]
        own.append(shell * screen[b].astype(F32))
    own = jnp.concatenate(own, axis=0).astype(BF16)
    coef[...] = jnp.dot(own, spread[...], preferred_element_type=F32).reshape(count, 8, 4096)
    left = lanes((32, 128)) < SHELL

    @pl.loop(0, count)
    def _(block):
        pltpu.make_async_copy(ints.at[block], held.at[block], sems.at[block]).wait()

        def step(t, sums):
            at = pl.multiple_of(t * 128, 128)
            tile = held[block, :, pl.ds(at, 128)].astype(F32)
            weights = coef[block, :, pl.ds(at, 128)]
            return tuple(sums[i] + tile * weights[i : i + 1] for i in range(8))

        sums = lax.fori_loop(0, 32, step, (jnp.zeros((32, 128), F32),) * 8, unroll=8)
        full = [s + pltpu.roll(s, SHELL, 1) for s in sums]
        shell = blocks[1, block].astype(F32)
        put = pl.multiple_of(block * 16, 16)
        for yh in range(4):
            both = jnp.where(left, full[2 * yh], full[2 * yh + 1])
            for core in range(2):
                d = yh * 2 + core
                out[d, pl.ds(put, 16), :] = both[core * 16 : core * 16 + 16]
                out[d, 64:72, :] = jnp.where(rows((8, 128)) == block, shell, out[d, 64:72, :])


def half_transform(c_occ, ints, blocks, screen):
    return pl.pallas_call(
        half_kernel,
        out_shape=jax.ShapeDtypeStruct((8, 72, 128), F32),
        in_specs=[HBM, HBM, HBM, HBM],
        out_specs=VMEM,
        scratch_shapes=[
            pltpu.SMEM((2, ints.shape[0]), jnp.int32),
            pltpu.SMEM(screen.shape, jnp.int32),
            pltpu.VMEM((8, c_occ.shape[0]), BF16),
            pltpu.VMEM(ints.shape, BF16),
            pltpu.VMEM((SHELL, 4096), BF16),
            pltpu.VMEM((ints.shape[0], 8, 4096), F32),
            pltpu.SemaphoreType.DMA((ints.shape[0] + 3,)),
        ],
        compiler_params=grant(54),
        name="half",
    )(blocks.T, screen, c_occ.T, ints)


def hold_kernel(c_vir, out, sem):
    copy = pltpu.make_async_copy(c_vir, out, sem)
    copy.start()
    copy.wait()


def hold(c_vir):
    return pl.pallas_call(
        hold_kernel,
        out_shape=jax.ShapeDtypeStruct(c_vir.shape, BF16),
        in_specs=[HBM],
        out_specs=VMEM,
        scratch_shapes=[pltpu.SemaphoreType.DMA],
        compiler_params=grant(50),
        cost_estimate=pl.CostEstimate(flops=1 << 33, bytes_accessed=1 << 22, transcendentals=0),
        name="hold",
    )(c_vir)


def rounded(x):
    return x.astype(BF16).astype(F32)


def finish(q, full, left, bmat, sides):
    bmat[:, q * 256 : q * 256 + 256] = full.astype(BF16)
    for t in range(2):
        one, two = full[0:16, t * 128 : t * 128 + 128], full[16:32, t * 128 : t * 128 + 128]
        tile = q * 2 + t
        sides[tile * 2] = jnp.where(left, one, pltpu.roll(two, SHELL, 1)).astype(BF16)
        sides[tile * 2 + 1] = jnp.where(left, pltpu.roll(one, SHELL, 1), two).astype(BF16)


def transform_kernel(recv, c_vir, bmat, wide, thin, terms, sides):
    left = lanes((16, 128)) < SHELL
    sums = [jnp.zeros((16, 128), F32) for _ in range(SHELLS)]
    for source in range(8):
        for b in range(4):
            data = recv[source, b * 16 : b * 16 + 16, :]
            shell = recv[source, 64 + b : 65 + b, :]
            for n in range(SHELLS):
                sums[n] = sums[n] + jnp.where(shell == float(n), data, 0.0)
    for m in range(SHELLS // 2):
        one, two = sums[2 * m], sums[2 * m + 1]
        pair = (
            jnp.where(left, one, pltpu.roll(two, SHELL, 1)),
            jnp.where(left, pltpu.roll(one, SHELL, 1), two),
        )
        for i in range(2):
            value = pair[i]
            for term in range(3):
                part = rounded(value)
                terms[term * 32 + i * 16 : term * 32 + i * 16 + 16, m * 128 : m * 128 + 128] = part.astype(BF16)
                value = value - part
    for q in range(TILES // 2):
        got = jnp.dot(terms[...], c_vir[:, q * 256 : q * 256 + 256], preferred_element_type=F32)
        full = (got[64:96] + got[32:64]) + got[0:32]
        finish(q, full, left, bmat, sides)
    for r in range(TILES):
        for yh in range(4):
            wide[r * 4 + yh] = bmat[:, r * 128 : r * 128 + 128]
            for x in range(4):
                kind = x * 4 + yh
                other = (r + kind // 2 + 1) % TILES
                thin[((r // 2 * 4 + x) * 2 + r % 2) * 4 + yh] = sides[other * 2 + kind % 2]


def transform(recv, c_vir):
    return pl.pallas_call(
        transform_kernel,
        out_shape=(
            jax.ShapeDtypeStruct((32, c_vir.shape[1]), BF16),
            jax.ShapeDtypeStruct((64, 32, 128), BF16),
            jax.ShapeDtypeStruct((256, 16, 128), BF16),
        ),
        in_specs=[VMEM, VMEM],
        out_specs=(VMEM, VMEM, VMEM),
        scratch_shapes=[pltpu.VMEM((96, c_vir.shape[0]), BF16), pltpu.VMEM((32, 16, 128), BF16)],
        compiler_params=grant(16),
        name="transform",
    )(recv, c_vir)


def onward_kernel(below, above, low, high):
    low[...] = above[0:32]
    high[...] = below[32:64]


def onward(below, above):
    half = jax.ShapeDtypeStruct((32,) + below.shape[1:], BF16)
    return pl.pallas_call(
        onward_kernel,
        out_shape=(half, half),
        in_specs=[VMEM, VMEM],
        out_specs=(VMEM, VMEM),
        compiler_params=grant(4),
        cost_estimate=pl.CostEstimate(flops=1 << 35, bytes_accessed=1 << 21, transcendentals=0),
        name="onward",
    )(below, above)


def panel_kernel(place, here, below, above, low, high, two, keep, give, wide, all_s):
    core, side, own = place[4], place[3], place[5]
    first = 0
    for tiles in (here, below, above, low, high):
        count = tiles.shape[0] * 16
        for i in range(8):
            wide[first : first + count, i * 128 : i * 128 + 128] = tiles[:, i].reshape(count, 128)
        first += count
    mine = wide[:, pl.ds(pl.multiple_of(own * 128, 128), 128)]
    others = wide[:, pl.ds(pl.multiple_of(side * 512, 512), 512)]
    all_s[...] = lax.dot_general(mine, others, TRANSPOSED, preferred_element_type=F32)
    for which, target in ((core, keep), (1 - core, give)):
        at = pl.multiple_of(which * 256, 256)
        for q in range(4):
            target[0:32, q * 256 : q * 256 + 256] = all_s[q * 32 : q * 32 + 32, pl.ds(at, 256)]
    at = pl.multiple_of((1 - core) * 16, 16)
    for q in range(2):
        give[32 + q * 16 : 48 + q * 16, :] = two[pl.ds(at, 16), q * 1024 : q * 1024 + 1024].astype(F32)


def panel(place, blocks, two):
    tiles = (block.reshape(-1, 8, 16, 128) for block in blocks)
    return pl.pallas_call(
        panel_kernel,
        out_shape=(
            jax.ShapeDtypeStruct((32, 1024), F32),
            jax.ShapeDtypeStruct((64, 1024), F32),
        ),
        in_specs=[SMEM] + [VMEM] * 6,
        out_specs=(VMEM, VMEM),
        scratch_shapes=[pltpu.VMEM((1024, 1024), BF16), pltpu.VMEM((128, 512), F32)],
        compiler_params=grant(8),
        cost_estimate=pl.CostEstimate(flops=1 << 29, bytes_accessed=1 << 22, transcendentals=0),
        name="panel",
    )(place, *tiles, two)


def settle_kernel(place, eps_occ, keep, got, eps_vir, mine, out, bmat):
    tile, side, core, own = (place[n] for n in (0, 3, 4, 5))
    row_a = eps_vir[pl.ds(tile, 1), :]
    square = (128, 128)
    col_a = jnp.sum(jnp.where(lanes(square) == rows(square), row_a, 0.0), axis=1, keepdims=True)
    for m in range(2):
        j = side * 4 + core * 2 + m
        block = jnp.concatenate(
            [
                keep[0:32, q * 256 + m * 128 : q * 256 + m * 128 + 128]
                + got[0:32, q * 256 + m * 128 : q * 256 + m * 128 + 128]
                for q in range(4)
            ],
            axis=0,
        )
        denominators = (eps_occ[own] + eps_occ[j] - row_a) - col_a
        terms = block * (2.0 * block - block.T) / denominators
        out[m : m + 1, :] = jnp.sum(terms, axis=0, keepdims=True)
    here = pl.ds(pl.multiple_of(core * 16, 16), 16)
    bmat[here, :] = mine[here, :]
    there = pl.ds(pl.multiple_of((1 - core) * 16, 16), 16)
    for q in range(2):
        bmat[there, q * 1024 : q * 1024 + 1024] = got[32 + q * 16 : 48 + q * 16, :].astype(BF16)


def settle(place, eps_occ, keep, got, eps_vir, two):
    return pl.pallas_call(
        settle_kernel,
        out_shape=(jax.ShapeDtypeStruct((8, 128), F32), jax.ShapeDtypeStruct(two.shape, BF16)),
        in_specs=[SMEM, SMEM, VMEM, VMEM, VMEM, VMEM],
        out_specs=(VMEM, VMEM),
        compiler_params=grant(4),
        cost_estimate=pl.CostEstimate(flops=1 << 28, bytes_accessed=1 << 20, transcendentals=0),
        name="settle",
    )(place, eps_occ, keep, got, eps_vir.reshape(-1, 128), two)


def gram_kernel(place, here, below, above, low, high, sides, _, keep, give, wide, thin, all_t):
    core, x = place[4], place[6]
    first = 0
    for away, tiles in ((0, here), (3, below), (1, above), (2, low), (2, high)):
        count = tiles.shape[0] * 16
        for i in range(8):
            wide[first : first + count, i * 128 : i * 128 + 128] = tiles[:, i].reshape(count, 128)
        z = 4 if tiles is high else 0
        for p in range(4):
            rows_z = sides[z : z + count // 32, (x + away) & 3, :, p]
            thin[first : first + count, p * 128 : p * 128 + 128] = rows_z.reshape(count, 128)
        first += count
    for p in range(4):
        part = lax.dot_general(thin[:, p * 128 : p * 128 + 128], wide[...], TRANSPOSED, preferred_element_type=F32)
        all_t[p * 128 : p * 128 + 128, :] = part
    for which, target in ((core, keep), (1 - core, give)):
        for j in range(8):
            at = pl.multiple_of(j * 64 + which * 32, 32)
            target[j * 32 : j * 32 + 32, :] = all_t[pl.ds(at, 32), :]


def gram(place, blocks, sides, after):
    tiles = (block.reshape(-1, 8, 16, 128) for block in blocks)
    shape = jax.ShapeDtypeStruct((256, 1024), F32)
    return pl.pallas_call(
        gram_kernel,
        out_shape=(shape, shape),
        in_specs=[SMEM] + [VMEM] * 6 + [HBM],
        out_specs=(VMEM, VMEM),
        scratch_shapes=[
            pltpu.VMEM((1024, 1024), BF16),
            pltpu.VMEM((1024, 512), BF16),
            pltpu.VMEM((512, 1024), F32),
        ],
        compiler_params=grant(16),
        name="gram",
    )(place, *tiles, sides.reshape(8, 4, 2, 4, 16, 128), after)


def energy_kernel(scale, place, eps_occ, keep, got, eps_vir, selfs, out, parts):
    tile, other, step, side, core, own = (place[n] for n in range(6))
    row_a = eps_vir[pl.ds(tile, 1), :]
    row_b = eps_vir[pl.ds(other, 1), :]
    first = side * 64 + core * 32
    col_b = jnp.sum(jnp.where(lanes((32, 128)) == rows((32, 128)) + first, row_b, 0.0), axis=1, keepdims=True)
    weight = jnp.where(step == 8, 1.0, 2.0)
    for i in range(8):
        for j in range(i, 8):
            there = slice(j * 32, j * 32 + 32), slice(i * 128, i * 128 + 128)
            here = slice(i * 32, i * 32 + 32), slice(j * 128, j * 128 + 128)
            one = keep[there] + got[there]
            two = keep[here] + got[here]
            denominators = (eps_occ[i] + eps_occ[j] - row_a) - col_b
            terms = (one * one + two * two - one * two) / denominators
            part = jnp.sum(terms, axis=0, keepdims=True) * weight
            parts[i * 8 + j : i * 8 + j + 1, :] = part
            parts[j * 8 + i : j * 8 + i + 1, :] = part
    for m in range(2):
        at = pl.ds(own * 8 + side * 4 + core * 2 + m, 1)
        parts[at, :] = parts[at, :] + selfs[m : m + 1, :]
    column = jnp.sum(parts[...], axis=1, keepdims=True) * scale
    row = jnp.sum(jnp.where(lanes((64, 128)) == rows((64, 128)), column, 0.0), axis=0, keepdims=True)
    out[...] = jnp.broadcast_to(row[None], out.shape)


def energies(scale, place, eps_occ, keep, got, eps_vir, selfs):
    return pl.pallas_call(
        functools.partial(energy_kernel, scale),
        out_shape=jax.ShapeDtypeStruct((32, 1, 128), F32),
        in_specs=[SMEM, SMEM, VMEM, VMEM, VMEM, VMEM],
        out_specs=VMEM,
        scratch_shapes=[pltpu.VMEM((64, 128), F32)],
        compiler_params=grant(6),
        name="energies",
    )(place, eps_occ, keep, got, eps_vir.reshape(-1, 128), selfs)


def position():
    zh, zl, x, yl, yh, core = (lax.axis_index(axis) for axis in AXES)
    tile, kind = zh * 4 + zl * 2 + yl, x * 4 + yh
    step, side = lax.shift_right_logical(kind, 1) + 1, kind & 1
    return jnp.stack([tile, (tile + step) & (TILES - 1), step, side, core, lax.shift_right_logical(kind, 1), x])


def again_kernel(got, out):
    out[...] = jnp.broadcast_to(jnp.sum(got[...], axis=0)[None], out.shape)


def last_kernel(got, out):
    row = jnp.broadcast_to(jnp.sum(got[...], axis=0), (8, 128))
    place = rows((8, 128))
    square = row
    for i in range(1, 8):
        square = jnp.where(place == i, pltpu.roll(row, 128 - 8 * i, 1), square)
    out[...] = square[:, :8]


def small(kernel, shape, name):
    return pl.pallas_call(
        kernel,
        out_shape=jax.ShapeDtypeStruct(shape, F32),
        in_specs=[VMEM],
        out_specs=VMEM,
        compiler_params=grant(2),
        name=name,
    )


def body(c_occ, c_vir, ints, blocks, screen, eps_occ, eps_vir):
    vir, occ = c_vir.shape[1], c_occ.shape[1]
    place = position()
    sent = half_transform(c_occ, ints, blocks, screen)
    recv = lax.all_to_all(sent, GRP, 0, 0, tiled=True)
    two, wide, thin = transform(recv, hold(c_vir))
    here = lax.all_to_all(wide, ("zh", "zl", "yl", "yh"), 0, 0, tiled=True)
    up = [(i, (i + 1) % 4) for i in range(4)]
    down = [(i, (i + 3) % 4) for i in range(4)]
    below, above = lax.ppermute(here, "x", up), lax.ppermute(here, "x", down)
    low, high = onward(below, above)
    low, high = lax.ppermute(low, "x", down), lax.ppermute(high, "x", up)
    sides = lax.all_to_all(thin, CHIPS, 0, 0, tiled=True)

    swap = [(0, 1), (1, 0)]
    blocks = (here, below, above, low, high)
    keep, give = panel(place, blocks, two)
    selfs, bmat = settle(place, eps_occ, keep, lax.ppermute(give, "core", swap), eps_vir, two)
    keep, give = gram(place, blocks, sides, selfs)
    got = lax.ppermute(give, "core", swap)
    scale = 1.0 / (float(vir) * float(vir) * 2048.0)
    energy = energies(scale, place, eps_occ, keep, got, eps_vir, selfs)
    energy = lax.all_to_all(energy, NEAR, 0, 0, tiled=True)
    energy = lax.all_to_all(small(again_kernel, (16, 1, 128), "again")(energy), FAR, 0, 0, tiled=True)
    energy = small(last_kernel, (occ, occ), "last")(energy)
    return bmat.reshape(1, 32, vir), energy


def solution(mesh):
    fine = Mesh(mesh.devices.reshape(4, 2, 4, 2, 4, 2), AXES)
    return jax.shard_map(
        body,
        mesh=fine,
        in_specs=(P(), P(), P(GRP, PAIR, None), P(GRP, None), P(GRP), P(), P()),
        out_specs=(P(GRP, PAIR, None), P()),
        check_vma=False,
    )
```

```python
import functools

import jax
import jax.numpy as jnp
from jax import lax
from jax.experimental import pallas as pl
from jax.experimental.pallas import tpu as pltpu
from jax.sharding import Mesh, PartitionSpec as P

SHELL = 64
SHELLS = 12
TILES = 16
AXES = ("zh", "zl", "x", "yl", "yh", "core")
CHIPS = ("zh", "zl", "x", "yl", "yh")
PAIR = ("zh", "zl", "x", "yl")
NEAR = ("zl", "x", "yl", "core")
FAR = ("zh", "yh")
GRP = ("yh", "core")
F32 = jnp.float32
BF16 = jnp.bfloat16
VMEM = pl.BlockSpec(memory_space=pltpu.VMEM)
SMEM = pl.BlockSpec(memory_space=pltpu.SMEM)
HBM = pl.BlockSpec(memory_space=pltpu.HBM)
TRANSPOSED = (((0,), (0,)), ((), ()))


def lanes(shape):
    return lax.broadcasted_iota(jnp.int32, shape, 1)


def grant(mib):
    return pltpu.CompilerParams(vmem_limit_bytes=mib * 1024 * 1024)


def rows(shape):
    return lax.broadcasted_iota(jnp.int32, shape, 0)


def half_kernel(blocks_at, screen_at, c_occ_at, ints, out, blocks, screen, c_occ, held, spread, coef, sems):
    count = held.shape[0]
    first = [
        pltpu.make_async_copy(blocks_at, blocks, sems.at[count]),
        pltpu.make_async_copy(screen_at, screen, sems.at[count + 1]),
        pltpu.make_async_copy(c_occ_at, c_occ, sems.at[count + 2]),
    ]
    for copy in first:
        copy.start()
    for b in range(count):
        pltpu.make_async_copy(ints.at[b], held.at[b], sems.at[b]).start()
    shape = (SHELL, 4096)
    spread[...] = (lanes(shape) // SHELL == rows(shape)).astype(F32).astype(BF16)
    for copy in first:
        copy.wait()
    own = []
    for b in range(count):
        first = blocks[0, b]
        at = pl.multiple_of((first // 2) * 128, 128)
        shell = pltpu.roll(c_occ[:, pl.ds(at, 128)].astype(F32), (first % 2) * SHELL, 1)[:, :SHELL]
        own.append(shell * screen[b].astype(F32))
    own = jnp.concatenate(own, axis=0).astype(BF16)
    coef[...] = jnp.dot(own, spread[...], preferred_element_type=F32).reshape(count, 8, 4096)
    left = lanes((32, 128)) < SHELL

    @pl.loop(0, count)
    def _(block):
        pltpu.make_async_copy(ints.at[block], held.at[block], sems.at[block]).wait()

        def step(t, sums):
            at = pl.multiple_of(t * 128, 128)
            tile = held[block, :, pl.ds(at, 128)].astype(F32)
            weights = coef[block, :, pl.ds(at, 128)]
            return tuple(sums[i] + tile * weights[i : i + 1] for i in range(8))

        sums = lax.fori_loop(0, 32, step, (jnp.zeros((32, 128), F32),) * 8, unroll=8)
        full = [s + pltpu.roll(s, SHELL, 1) for s in sums]
        shell = blocks[1, block].astype(F32)
        put = pl.multiple_of(block * 16, 16)
        for yh in range(4):
            both = jnp.where(left, full[2 * yh], full[2 * yh + 1])
            for core in range(2):
                d = yh * 2 + core
                out[d, pl.ds(put, 16), :] = both[core * 16 : core * 16 + 16]
                out[d, 64:72, :] = jnp.where(rows((8, 128)) == block, shell, out[d, 64:72, :])


def half_transform(c_occ, ints, blocks, screen):
    return pl.pallas_call(
        half_kernel,
        out_shape=jax.ShapeDtypeStruct((8, 72, 128), F32),
        in_specs=[HBM, HBM, HBM, HBM],
        out_specs=VMEM,
        scratch_shapes=[
            pltpu.SMEM((2, ints.shape[0]), jnp.int32),
            pltpu.SMEM(screen.shape, jnp.int32),
            pltpu.VMEM((8, c_occ.shape[0]), BF16),
            pltpu.VMEM(ints.shape, BF16),
            pltpu.VMEM((SHELL, 4096), BF16),
            pltpu.VMEM((ints.shape[0], 8, 4096), F32),
            pltpu.SemaphoreType.DMA((ints.shape[0] + 3,)),
        ],
        compiler_params=grant(54),
        name="half",
    )(blocks.T, screen, c_occ.T, ints)


def hold_kernel(c_vir, out, sem):
    copy = pltpu.make_async_copy(c_vir, out, sem)
    copy.start()
    copy.wait()


def hold(c_vir):
    return pl.pallas_call(
        hold_kernel,
        out_shape=jax.ShapeDtypeStruct(c_vir.shape, BF16),
        in_specs=[HBM],
        out_specs=VMEM,
        scratch_shapes=[pltpu.SemaphoreType.DMA],
        compiler_params=grant(50),
        cost_estimate=pl.CostEstimate(flops=1 << 33, bytes_accessed=1 << 22, transcendentals=0),
        name="hold",
    )(c_vir)


def rounded(x):
    return x.astype(BF16).astype(F32)


def finish(q, full, left, bmat, sides):
    bmat[:, q * 256 : q * 256 + 256] = full.astype(BF16)
    for t in range(2):
        one, two = full[0:16, t * 128 : t * 128 + 128], full[16:32, t * 128 : t * 128 + 128]
        tile = q * 2 + t
        sides[tile * 2] = jnp.where(left, one, pltpu.roll(two, SHELL, 1)).astype(BF16)
        sides[tile * 2 + 1] = jnp.where(left, pltpu.roll(one, SHELL, 1), two).astype(BF16)


def transform_kernel(recv, c_vir, bmat, wide, thin, terms, sides):
    left = lanes((16, 128)) < SHELL
    sums = [jnp.zeros((16, 128), F32) for _ in range(SHELLS)]
    for source in range(8):
        for b in range(4):
            data = recv[source, b * 16 : b * 16 + 16, :]
            shell = recv[source, 64 + b : 65 + b, :]
            for n in range(SHELLS):
                sums[n] = sums[n] + jnp.where(shell == float(n), data, 0.0)
    for m in range(SHELLS // 2):
        one, two = sums[2 * m], sums[2 * m + 1]
        pair = (
            jnp.where(left, one, pltpu.roll(two, SHELL, 1)),
            jnp.where(left, pltpu.roll(one, SHELL, 1), two),
        )
        for i in range(2):
            value = pair[i]
            for term in range(3):
                part = rounded(value)
                terms[term * 32 + i * 16 : term * 32 + i * 16 + 16, m * 128 : m * 128 + 128] = part.astype(BF16)
                value = value - part
    for q in range(TILES // 2):
        got = jnp.dot(terms[...], c_vir[:, q * 256 : q * 256 + 256], preferred_element_type=F32)
        full = (got[64:96] + got[32:64]) + got[0:32]
        finish(q, full, left, bmat, sides)
    for r in range(TILES):
        for yh in range(4):
            wide[r * 4 + yh] = bmat[:, r * 128 : r * 128 + 128]
            for x in range(4):
                kind = x * 4 + yh
                other = (r + kind // 2 + 1) % TILES
                thin[((r // 2 * 4 + x) * 2 + r % 2) * 4 + yh] = sides[other * 2 + kind % 2]


def transform(recv, c_vir):
    return pl.pallas_call(
        transform_kernel,
        out_shape=(
            jax.ShapeDtypeStruct((32, c_vir.shape[1]), BF16),
            jax.ShapeDtypeStruct((64, 32, 128), BF16),
            jax.ShapeDtypeStruct((256, 16, 128), BF16),
        ),
        in_specs=[VMEM, VMEM],
        out_specs=(VMEM, VMEM, VMEM),
        scratch_shapes=[pltpu.VMEM((96, c_vir.shape[0]), BF16), pltpu.VMEM((32, 16, 128), BF16)],
        compiler_params=grant(16),
        name="transform",
    )(recv, c_vir)


def onward_kernel(below, above, low, high):
    low[...] = above[0:32]
    high[...] = below[32:64]


def onward(below, above):
    half = jax.ShapeDtypeStruct((32,) + below.shape[1:], BF16)
    return pl.pallas_call(
        onward_kernel,
        out_shape=(half, half),
        in_specs=[VMEM, VMEM],
        out_specs=(VMEM, VMEM),
        compiler_params=grant(4),
        cost_estimate=pl.CostEstimate(flops=1 << 35, bytes_accessed=1 << 21, transcendentals=0),
        name="onward",
    )(below, above)


def panel_kernel(place, here, below, above, low, high, two, keep, give, wide, all_s):
    core, side, own = place[4], place[3], place[5]
    first = 0
    for tiles in (here, below, above, low, high):
        count = tiles.shape[0] * 16
        for i in range(8):
            wide[first : first + count, i * 128 : i * 128 + 128] = tiles[:, i].reshape(count, 128)
        first += count
    mine = wide[:, pl.ds(pl.multiple_of(own * 128, 128), 128)]
    others = wide[:, pl.ds(pl.multiple_of(side * 512, 512), 512)]
    all_s[...] = lax.dot_general(mine, others, TRANSPOSED, preferred_element_type=F32)
    for which, target in ((core, keep), (1 - core, give)):
        at = pl.multiple_of(which * 256, 256)
        for q in range(4):
            target[0:32, q * 256 : q * 256 + 256] = all_s[q * 32 : q * 32 + 32, pl.ds(at, 256)]
    at = pl.multiple_of((1 - core) * 16, 16)
    for q in range(2):
        give[32 + q * 16 : 48 + q * 16, :] = two[pl.ds(at, 16), q * 1024 : q * 1024 + 1024].astype(F32)


def panel(place, blocks, two):
    tiles = (block.reshape(-1, 8, 16, 128) for block in blocks)
    return pl.pallas_call(
        panel_kernel,
        out_shape=(
            jax.ShapeDtypeStruct((32, 1024), F32),
            jax.ShapeDtypeStruct((64, 1024), F32),
        ),
        in_specs=[SMEM] + [VMEM] * 6,
        out_specs=(VMEM, VMEM),
        scratch_shapes=[pltpu.VMEM((1024, 1024), BF16), pltpu.VMEM((128, 512), F32)],
        compiler_params=grant(8),
        cost_estimate=pl.CostEstimate(flops=1 << 29, bytes_accessed=1 << 22, transcendentals=0),
        name="panel",
    )(place, *tiles, two)


def settle_kernel(place, eps_occ, keep, got, eps_vir, mine, out, bmat):
    tile, side, core, own = (place[n] for n in (0, 3, 4, 5))
    row_a = eps_vir[pl.ds(tile, 1), :]
    square = (128, 128)
    col_a = jnp.sum(jnp.where(lanes(square) == rows(square), row_a, 0.0), axis=1, keepdims=True)
    for m in range(2):
        j = side * 4 + core * 2 + m
        block = jnp.concatenate(
            [
                keep[0:32, q * 256 + m * 128 : q * 256 + m * 128 + 128]
                + got[0:32, q * 256 + m * 128 : q * 256 + m * 128 + 128]
                for q in range(4)
            ],
            axis=0,
        )
        denominators = (eps_occ[own] + eps_occ[j] - row_a) - col_a
        terms = block * (2.0 * block - block.T) / denominators
        out[m : m + 1, :] = jnp.sum(terms, axis=0, keepdims=True)
    here = pl.ds(pl.multiple_of(core * 16, 16), 16)
    bmat[here, :] = mine[here, :]
    there = pl.ds(pl.multiple_of((1 - core) * 16, 16), 16)
    for q in range(2):
        bmat[there, q * 1024 : q * 1024 + 1024] = got[32 + q * 16 : 48 + q * 16, :].astype(BF16)


def settle(place, eps_occ, keep, got, eps_vir, two):
    return pl.pallas_call(
        settle_kernel,
        out_shape=(jax.ShapeDtypeStruct((8, 128), F32), jax.ShapeDtypeStruct(two.shape, BF16)),
        in_specs=[SMEM, SMEM, VMEM, VMEM, VMEM, VMEM],
        out_specs=(VMEM, VMEM),
        compiler_params=grant(4),
        cost_estimate=pl.CostEstimate(flops=1 << 28, bytes_accessed=1 << 20, transcendentals=0),
        name="settle",
    )(place, eps_occ, keep, got, eps_vir.reshape(-1, 128), two)


def gram_kernel(place, here, below, above, low, high, sides, _, keep, give, wide, thin, all_t):
    core, x = place[4], place[6]
    first = 0
    for away, tiles in ((0, here), (3, below), (1, above), (2, low), (2, high)):
        count = tiles.shape[0] * 16
        for i in range(8):
            wide[first : first + count, i * 128 : i * 128 + 128] = tiles[:, i].reshape(count, 128)
        z = 4 if tiles is high else 0
        for p in range(4):
            rows_z = sides[z : z + count // 32, (x + away) & 3, :, p]
            thin[first : first + count, p * 128 : p * 128 + 128] = rows_z.reshape(count, 128)
        first += count
    for p in range(4):
        part = lax.dot_general(thin[:, p * 128 : p * 128 + 128], wide[...], TRANSPOSED, preferred_element_type=F32)
        all_t[p * 128 : p * 128 + 128, :] = part
    for which, target in ((core, keep), (1 - core, give)):
        for j in range(8):
            at = pl.multiple_of(j * 64 + which * 32, 32)
            target[j * 32 : j * 32 + 32, :] = all_t[pl.ds(at, 32), :]


def gram(place, blocks, sides, after):
    tiles = (block.reshape(-1, 8, 16, 128) for block in blocks)
    shape = jax.ShapeDtypeStruct((256, 1024), F32)
    return pl.pallas_call(
        gram_kernel,
        out_shape=(shape, shape),
        in_specs=[SMEM] + [VMEM] * 6 + [HBM],
        out_specs=(VMEM, VMEM),
        scratch_shapes=[
            pltpu.VMEM((1024, 1024), BF16),
            pltpu.VMEM((1024, 512), BF16),
            pltpu.VMEM((512, 1024), F32),
        ],
        compiler_params=grant(16),
        name="gram",
    )(place, *tiles, sides.reshape(8, 4, 2, 4, 16, 128), after)


def energy_kernel(scale, place, eps_occ, keep, got, eps_vir, selfs, out, parts):
    tile, other, step, side, core, own = (place[n] for n in range(6))
    row_a = eps_vir[pl.ds(tile, 1), :]
    row_b = eps_vir[pl.ds(other, 1), :]
    first = side * 64 + core * 32
    col_b = jnp.sum(jnp.where(lanes((32, 128)) == rows((32, 128)) + first, row_b, 0.0), axis=1, keepdims=True)
    weight = jnp.where(step == 8, 1.0, 2.0)
    for i in range(8):
        for j in range(i, 8):
            there = slice(j * 32, j * 32 + 32), slice(i * 128, i * 128 + 128)
            here = slice(i * 32, i * 32 + 32), slice(j * 128, j * 128 + 128)
            one = keep[there] + got[there]
            two = keep[here] + got[here]
            denominators = (eps_occ[i] + eps_occ[j] - row_a) - col_b
            terms = (one * one + two * two - one * two) / denominators
            part = jnp.sum(terms, axis=0, keepdims=True) * weight
            parts[i * 8 + j : i * 8 + j + 1, :] = part
            parts[j * 8 + i : j * 8 + i + 1, :] = part
    for m in range(2):
        at = pl.ds(own * 8 + side * 4 + core * 2 + m, 1)
        parts[at, :] = parts[at, :] + selfs[m : m + 1, :]
    column = jnp.sum(parts[...], axis=1, keepdims=True) * scale
    row = jnp.sum(jnp.where(lanes((64, 128)) == rows((64, 128)), column, 0.0), axis=0, keepdims=True)
    out[...] = jnp.broadcast_to(row[None], out.shape)


def energies(scale, place, eps_occ, keep, got, eps_vir, selfs):
    return pl.pallas_call(
        functools.partial(energy_kernel, scale),
        out_shape=jax.ShapeDtypeStruct((32, 1, 128), F32),
        in_specs=[SMEM, SMEM, VMEM, VMEM, VMEM, VMEM],
        out_specs=VMEM,
        scratch_shapes=[pltpu.VMEM((64, 128), F32)],
        compiler_params=grant(6),
        name="energies",
    )(place, eps_occ, keep, got, eps_vir.reshape(-1, 128), selfs)


def position():
    zh, zl, x, yl, yh, core = (lax.axis_index(axis) for axis in AXES)
    tile, kind = zh * 4 + zl * 2 + yl, x * 4 + yh
    step, side = lax.shift_right_logical(kind, 1) + 1, kind & 1
    return jnp.stack([tile, (tile + step) & (TILES - 1), step, side, core, lax.shift_right_logical(kind, 1), x])


def again_kernel(got, out):
    out[...] = jnp.broadcast_to(jnp.sum(got[...], axis=0)[None], out.shape)


def last_kernel(got, out):
    row = jnp.broadcast_to(jnp.sum(got[...], axis=0), (8, 128))
    place = rows((8, 128))
    square = row
    for i in range(1, 8):
        square = jnp.where(place == i, pltpu.roll(row, 128 - 8 * i, 1), square)
    out[...] = square[:, :8]


def small(kernel, shape, name):
    return pl.pallas_call(
        kernel,
        out_shape=jax.ShapeDtypeStruct(shape, F32),
        in_specs=[VMEM],
        out_specs=VMEM,
        compiler_params=grant(2),
        name=name,
    )


def body(c_occ, c_vir, ints, blocks, screen, eps_occ, eps_vir):
    vir, occ = c_vir.shape[1], c_occ.shape[1]
    place = position()
    sent = half_transform(c_occ, ints, blocks, screen)
    recv = lax.all_to_all(sent, GRP, 0, 0, tiled=True)
    two, wide, thin = transform(recv, hold(c_vir))
    here = lax.all_to_all(wide, ("zh", "zl", "yl", "yh"), 0, 0, tiled=True)
    up = [(i, (i + 1) % 4) for i in range(4)]
    down = [(i, (i + 3) % 4) for i in range(4)]
    below, above = lax.ppermute(here, "x", up), lax.ppermute(here, "x", down)
    low, high = onward(below, above)
    low, high = lax.ppermute(low, "x", down), lax.ppermute(high, "x", up)
    sides = lax.all_to_all(thin, CHIPS, 0, 0, tiled=True)

    swap = [(0, 1), (1, 0)]
    blocks = (here, below, above, low, high)
    keep, give = panel(place, blocks, two)
    other = lax.ppermute(give, "core", swap)
    selfs, bmat = settle(place, eps_occ, keep, other, eps_vir, two)
    keep, give = gram(place, blocks, sides, other)
    got = lax.ppermute(give, "core", swap)
    scale = 1.0 / (float(vir) * float(vir) * 2048.0)
    energy = energies(scale, place, eps_occ, keep, got, eps_vir, selfs)
    energy = lax.all_to_all(energy, NEAR, 0, 0, tiled=True)
    energy = lax.all_to_all(small(again_kernel, (16, 1, 128), "again")(energy), FAR, 0, 0, tiled=True)
    energy = small(last_kernel, (occ, occ), "last")(energy)
    return bmat.reshape(1, 32, vir), energy


def solution(mesh):
    fine = Mesh(mesh.devices.reshape(4, 2, 4, 2, 4, 2), AXES)
    return jax.shard_map(
        body,
        mesh=fine,
        in_specs=(P(), P(), P(GRP, PAIR, None), P(GRP, None), P(GRP), P(), P()),
        out_specs=(P(GRP, PAIR, None), P()),
        check_vma=False,
    )
```

```python
import functools

import jax
import jax.numpy as jnp
from jax import lax
from jax.experimental import pallas as pl
from jax.experimental.pallas import tpu as pltpu
from jax.sharding import Mesh, PartitionSpec as P

SHELL = 64
SHELLS = 12
TILES = 16
AXES = ("zh", "zl", "x", "yl", "yh", "core")
CHIPS = ("zh", "zl", "x", "yl", "yh")
PAIR = ("zh", "zl", "x", "yl")
GRP = ("yh", "core")
F32 = jnp.float32
BF16 = jnp.bfloat16
VMEM = pl.BlockSpec(memory_space=pltpu.VMEM)
SMEM = pl.BlockSpec(memory_space=pltpu.SMEM)
HBM = pl.BlockSpec(memory_space=pltpu.HBM)
TRANSPOSED = (((0,), (0,)), ((), ()))


def lanes(shape):
    return lax.broadcasted_iota(jnp.int32, shape, 1)


def grant(mib):
    return pltpu.CompilerParams(vmem_limit_bytes=mib * 1024 * 1024)


def rows(shape):
    return lax.broadcasted_iota(jnp.int32, shape, 0)


def half_kernel(blocks_at, screen_at, c_occ_at, ints, out, blocks, screen, c_occ, held, spread, coef, sems):
    count = held.shape[0]
    first = [
        pltpu.make_async_copy(blocks_at, blocks, sems.at[count]),
        pltpu.make_async_copy(screen_at, screen, sems.at[count + 1]),
        pltpu.make_async_copy(c_occ_at, c_occ, sems.at[count + 2]),
    ]
    for copy in first:
        copy.start()
    for b in range(count):
        pltpu.make_async_copy(ints.at[b], held.at[b], sems.at[b]).start()
    shape = (SHELL, 4096)
    spread[...] = (lanes(shape) // SHELL == rows(shape)).astype(F32).astype(BF16)
    for copy in first:
        copy.wait()
    own = []
    for b in range(count):
        first = blocks[0, b]
        at = pl.multiple_of((first // 2) * 128, 128)
        shell = pltpu.roll(c_occ[:, pl.ds(at, 128)].astype(F32), (first % 2) * SHELL, 1)[:, :SHELL]
        own.append(shell * screen[b].astype(F32))
    own = jnp.concatenate(own, axis=0).astype(BF16)
    coef[...] = jnp.dot(own, spread[...], preferred_element_type=F32).reshape(count, 8, 4096)
    left = lanes((32, 128)) < SHELL

    @pl.loop(0, count)
    def _(block):
        pltpu.make_async_copy(ints.at[block], held.at[block], sems.at[block]).wait()

        def step(t, sums):
            at = pl.multiple_of(t * 128, 128)
            tile = held[block, :, pl.ds(at, 128)].astype(F32)
            weights = coef[block, :, pl.ds(at, 128)]
            return tuple(sums[i] + tile * weights[i : i + 1] for i in range(8))

        sums = lax.fori_loop(0, 32, step, (jnp.zeros((32, 128), F32),) * 8, unroll=8)
        full = [s + pltpu.roll(s, SHELL, 1) for s in sums]
        shell = blocks[1, block].astype(F32)
        put = pl.multiple_of(block * 16, 16)
        for yh in range(4):
            both = jnp.where(left, full[2 * yh], full[2 * yh + 1])
            for core in range(2):
                d = yh * 2 + core
                out[d, pl.ds(put, 16), :] = both[core * 16 : core * 16 + 16]
                out[d, 64:72, :] = jnp.where(rows((8, 128)) == block, shell, out[d, 64:72, :])


def half_transform(c_occ, ints, blocks, screen):
    return pl.pallas_call(
        half_kernel,
        out_shape=jax.ShapeDtypeStruct((8, 72, 128), F32),
        in_specs=[HBM, HBM, HBM, HBM],
        out_specs=VMEM,
        scratch_shapes=[
            pltpu.SMEM((2, ints.shape[0]), jnp.int32),
            pltpu.SMEM(screen.shape, jnp.int32),
            pltpu.VMEM((8, c_occ.shape[0]), BF16),
            pltpu.VMEM(ints.shape, BF16),
            pltpu.VMEM((SHELL, 4096), BF16),
            pltpu.VMEM((ints.shape[0], 8, 4096), F32),
            pltpu.SemaphoreType.DMA((ints.shape[0] + 3,)),
        ],
        compiler_params=grant(54),
        name="half",
    )(blocks.T, screen, c_occ.T, ints)


def hold_kernel(c_vir, out, sem):
    copy = pltpu.make_async_copy(c_vir, out, sem)
    copy.start()
    copy.wait()


def hold(c_vir):
    return pl.pallas_call(
        hold_kernel,
        out_shape=jax.ShapeDtypeStruct(c_vir.shape, BF16),
        in_specs=[HBM],
        out_specs=VMEM,
        scratch_shapes=[pltpu.SemaphoreType.DMA],
        compiler_params=grant(50),
        cost_estimate=pl.CostEstimate(flops=1 << 33, bytes_accessed=1 << 22, transcendentals=0),
        name="hold",
    )(c_vir)


def rounded(x):
    return x.astype(BF16).astype(F32)


def finish(q, full, left, bmat, sides):
    bmat[:, q * 256 : q * 256 + 256] = full.astype(BF16)
    for t in range(2):
        one, two = full[0:16, t * 128 : t * 128 + 128], full[16:32, t * 128 : t * 128 + 128]
        tile = q * 2 + t
        sides[tile * 2] = jnp.where(left, one, pltpu.roll(two, SHELL, 1)).astype(BF16)
        sides[tile * 2 + 1] = jnp.where(left, pltpu.roll(one, SHELL, 1), two).astype(BF16)


def transform_kernel(recv, c_vir, bmat, wide, thin, terms, sides):
    left = lanes((16, 128)) < SHELL
    sums = [jnp.zeros((16, 128), F32) for _ in range(SHELLS)]
    for source in range(8):
        for b in range(4):
            data = recv[source, b * 16 : b * 16 + 16, :]
            shell = recv[source, 64 + b : 65 + b, :]
            for n in range(SHELLS):
                sums[n] = sums[n] + jnp.where(shell == float(n), data, 0.0)
    for m in range(SHELLS // 2):
        one, two = sums[2 * m], sums[2 * m + 1]
        pair = (
            jnp.where(left, one, pltpu.roll(two, SHELL, 1)),
            jnp.where(left, pltpu.roll(one, SHELL, 1), two),
        )
        for i in range(2):
            value = pair[i]
            for term in range(3):
                part = rounded(value)
                terms[term * 32 + i * 16 : term * 32 + i * 16 + 16, m * 128 : m * 128 + 128] = part.astype(BF16)
                value = value - part
    for q in range(TILES // 2):
        got = jnp.dot(terms[...], c_vir[:, q * 256 : q * 256 + 256], preferred_element_type=F32)
        full = (got[64:96] + got[32:64]) + got[0:32]
        finish(q, full, left, bmat, sides)
    for r in range(TILES):
        for yh in range(4):
            wide[r * 4 + yh] = bmat[:, r * 128 : r * 128 + 128]
            for x in range(4):
                kind = x * 4 + yh
                other = (r + kind // 2 + 1) % TILES
                thin[((r // 2 * 4 + x) * 2 + r % 2) * 4 + yh] = sides[other * 2 + kind % 2]


def transform(recv, c_vir):
    return pl.pallas_call(
        transform_kernel,
        out_shape=(
            jax.ShapeDtypeStruct((32, c_vir.shape[1]), BF16),
            jax.ShapeDtypeStruct((64, 32, 128), BF16),
            jax.ShapeDtypeStruct((256, 16, 128), BF16),
        ),
        in_specs=[VMEM, VMEM],
        out_specs=(VMEM, VMEM, VMEM),
        scratch_shapes=[pltpu.VMEM((96, c_vir.shape[0]), BF16), pltpu.VMEM((32, 16, 128), BF16)],
        compiler_params=grant(16),
        name="transform",
    )(recv, c_vir)


def onward_kernel(below, above, low, high):
    low[...] = above[0:32]
    high[...] = below[32:64]


def onward(below, above):
    half = jax.ShapeDtypeStruct((32,) + below.shape[1:], BF16)
    return pl.pallas_call(
        onward_kernel,
        out_shape=(half, half),
        in_specs=[VMEM, VMEM],
        out_specs=(VMEM, VMEM),
        compiler_params=grant(4),
        cost_estimate=pl.CostEstimate(flops=1 << 35, bytes_accessed=1 << 21, transcendentals=0),
        name="onward",
    )(below, above)


def panel_kernel(place, here, below, above, low, high, two, keep, give, wide, all_s):
    core, side, own = place[4], place[3], place[5]
    first = 0
    for tiles in (here, below, above, low, high):
        count = tiles.shape[0] * 16
        for i in range(8):
            wide[first : first + count, i * 128 : i * 128 + 128] = tiles[:, i].reshape(count, 128)
        first += count
    mine = wide[:, pl.ds(pl.multiple_of(own * 128, 128), 128)]
    others = wide[:, pl.ds(pl.multiple_of(side * 512, 512), 512)]
    all_s[...] = lax.dot_general(mine, others, TRANSPOSED, preferred_element_type=F32)
    for which, target in ((core, keep), (1 - core, give)):
        at = pl.multiple_of(which * 256, 256)
        for q in range(4):
            target[0:32, q * 256 : q * 256 + 256] = all_s[q * 32 : q * 32 + 32, pl.ds(at, 256)]
    at = pl.multiple_of((1 - core) * 16, 16)
    for q in range(2):
        give[32 + q * 16 : 48 + q * 16, :] = two[pl.ds(at, 16), q * 1024 : q * 1024 + 1024].astype(F32)


def panel(place, blocks, two):
    tiles = (block.reshape(-1, 8, 16, 128) for block in blocks)
    return pl.pallas_call(
        panel_kernel,
        out_shape=(
            jax.ShapeDtypeStruct((32, 1024), F32),
            jax.ShapeDtypeStruct((64, 1024), F32),
        ),
        in_specs=[SMEM] + [VMEM] * 6,
        out_specs=(VMEM, VMEM),
        scratch_shapes=[pltpu.VMEM((1024, 1024), BF16), pltpu.VMEM((128, 512), F32)],
        compiler_params=grant(8),
        cost_estimate=pl.CostEstimate(flops=1 << 29, bytes_accessed=1 << 22, transcendentals=0),
        name="panel",
    )(place, *tiles, two)


def settle_kernel(place, eps_occ, keep, got, eps_vir, mine, out, bmat):
    tile, side, core, own = (place[n] for n in (0, 3, 4, 5))
    row_a = eps_vir[pl.ds(tile, 1), :]
    square = (128, 128)
    col_a = jnp.sum(jnp.where(lanes(square) == rows(square), row_a, 0.0), axis=1, keepdims=True)
    for m in range(2):
        j = side * 4 + core * 2 + m
        block = jnp.concatenate(
            [
                keep[0:32, q * 256 + m * 128 : q * 256 + m * 128 + 128]
                + got[0:32, q * 256 + m * 128 : q * 256 + m * 128 + 128]
                for q in range(4)
            ],
            axis=0,
        )
        denominators = (eps_occ[own] + eps_occ[j] - row_a) - col_a
        terms = block * (2.0 * block - block.T) / denominators
        out[m : m + 1, :] = jnp.sum(terms, axis=0, keepdims=True)
    here = pl.ds(pl.multiple_of(core * 16, 16), 16)
    bmat[here, :] = mine[here, :]
    there = pl.ds(pl.multiple_of((1 - core) * 16, 16), 16)
    for q in range(2):
        bmat[there, q * 1024 : q * 1024 + 1024] = got[32 + q * 16 : 48 + q * 16, :].astype(BF16)


def settle(place, eps_occ, keep, got, eps_vir, two):
    return pl.pallas_call(
        settle_kernel,
        out_shape=(jax.ShapeDtypeStruct((8, 128), F32), jax.ShapeDtypeStruct(two.shape, BF16)),
        in_specs=[SMEM, SMEM, VMEM, VMEM, VMEM, VMEM],
        out_specs=(VMEM, VMEM),
        compiler_params=grant(4),
        cost_estimate=pl.CostEstimate(flops=1 << 28, bytes_accessed=1 << 20, transcendentals=0),
        name="settle",
    )(place, eps_occ, keep, got, eps_vir.reshape(-1, 128), two)


def gram_kernel(place, here, below, above, low, high, sides, _, keep, give, wide, thin, all_t):
    core, x = place[4], place[6]
    first = 0
    for away, tiles in ((0, here), (3, below), (1, above), (2, low), (2, high)):
        count = tiles.shape[0] * 16
        for i in range(8):
            wide[first : first + count, i * 128 : i * 128 + 128] = tiles[:, i].reshape(count, 128)
        z = 4 if tiles is high else 0
        for p in range(4):
            rows_z = sides[z : z + count // 32, (x + away) & 3, :, p]
            thin[first : first + count, p * 128 : p * 128 + 128] = rows_z.reshape(count, 128)
        first += count
    for p in range(4):
        part = lax.dot_general(thin[:, p * 128 : p * 128 + 128], wide[...], TRANSPOSED, preferred_element_type=F32)
        all_t[p * 128 : p * 128 + 128, :] = part
    for which, target in ((core, keep), (1 - core, give)):
        for j in range(8):
            at = pl.multiple_of(j * 64 + which * 32, 32)
            target[j * 32 : j * 32 + 32, :] = all_t[pl.ds(at, 32), :]


def gram(place, blocks, sides, after):
    tiles = (block.reshape(-1, 8, 16, 128) for block in blocks)
    shape = jax.ShapeDtypeStruct((256, 1024), F32)
    return pl.pallas_call(
        gram_kernel,
        out_shape=(shape, shape),
        in_specs=[SMEM] + [VMEM] * 6 + [HBM],
        out_specs=(VMEM, VMEM),
        scratch_shapes=[
            pltpu.VMEM((1024, 1024), BF16),
            pltpu.VMEM((1024, 512), BF16),
            pltpu.VMEM((512, 1024), F32),
        ],
        compiler_params=grant(16),
        name="gram",
    )(place, *tiles, sides.reshape(8, 4, 2, 4, 16, 128), after)


def energy_kernel(scale, place, eps_occ, keep, got, eps_vir, selfs, out, parts):
    tile, other, step, side, core, own = (place[n] for n in range(6))
    row_a = eps_vir[pl.ds(tile, 1), :]
    row_b = eps_vir[pl.ds(other, 1), :]
    first = side * 64 + core * 32
    col_b = jnp.sum(jnp.where(lanes((32, 128)) == rows((32, 128)) + first, row_b, 0.0), axis=1, keepdims=True)
    weight = jnp.where(step == 8, 1.0, 2.0)
    for i in range(8):
        for j in range(i, 8):
            there = slice(j * 32, j * 32 + 32), slice(i * 128, i * 128 + 128)
            here = slice(i * 32, i * 32 + 32), slice(j * 128, j * 128 + 128)
            one = keep[there] + got[there]
            two = keep[here] + got[here]
            denominators = (eps_occ[i] + eps_occ[j] - row_a) - col_b
            terms = (one * one + two * two - one * two) / denominators
            part = jnp.sum(terms, axis=0, keepdims=True) * weight
            parts[i * 8 + j : i * 8 + j + 1, :] = part
            parts[j * 8 + i : j * 8 + i + 1, :] = part
    for m in range(2):
        at = pl.ds(own * 8 + side * 4 + core * 2 + m, 1)
        parts[at, :] = parts[at, :] + selfs[m : m + 1, :]
    column = jnp.sum(parts[...], axis=1, keepdims=True) * scale
    row = jnp.sum(jnp.where(lanes((64, 128)) == rows((64, 128)), column, 0.0), axis=0, keepdims=True)
    out[...] = jnp.broadcast_to(row[None], out.shape)


def energies(scale, place, eps_occ, keep, got, eps_vir, selfs):
    return pl.pallas_call(
        functools.partial(energy_kernel, scale),
        out_shape=jax.ShapeDtypeStruct((256, 1, 128), F32),
        in_specs=[SMEM, SMEM, VMEM, VMEM, VMEM, VMEM],
        out_specs=VMEM,
        scratch_shapes=[pltpu.VMEM((64, 128), F32)],
        compiler_params=grant(6),
        name="energies",
    )(place, eps_occ, keep, got, eps_vir.reshape(-1, 128), selfs)


def position():
    zh, zl, x, yl, yh, core = (lax.axis_index(axis) for axis in AXES)
    tile, kind = zh * 4 + zl * 2 + yl, x * 4 + yh
    step, side = lax.shift_right_logical(kind, 1) + 1, kind & 1
    return jnp.stack([tile, (tile + step) & (TILES - 1), step, side, core, lax.shift_right_logical(kind, 1), x])


def last_kernel(got, out):
    row = jnp.broadcast_to(jnp.sum(got[...], axis=0), (8, 128))
    place = rows((8, 128))
    square = row
    for i in range(1, 8):
        square = jnp.where(place == i, pltpu.roll(row, 128 - 8 * i, 1), square)
    out[...] = square[:, :8]


def small(kernel, shape, name):
    return pl.pallas_call(
        kernel,
        out_shape=jax.ShapeDtypeStruct(shape, F32),
        in_specs=[VMEM],
        out_specs=VMEM,
        compiler_params=grant(2),
        name=name,
    )


def body(c_occ, c_vir, ints, blocks, screen, eps_occ, eps_vir):
    vir, occ = c_vir.shape[1], c_occ.shape[1]
    place = position()
    sent = half_transform(c_occ, ints, blocks, screen)
    recv = lax.all_to_all(sent, GRP, 0, 0, tiled=True)
    two, wide, thin = transform(recv, hold(c_vir))
    here = lax.all_to_all(wide, ("zh", "zl", "yl", "yh"), 0, 0, tiled=True)
    up = [(i, (i + 1) % 4) for i in range(4)]
    down = [(i, (i + 3) % 4) for i in range(4)]
    below, above = lax.ppermute(here, "x", up), lax.ppermute(here, "x", down)
    low, high = onward(below, above)
    low, high = lax.ppermute(low, "x", down), lax.ppermute(high, "x", up)
    sides = lax.all_to_all(thin, CHIPS, 0, 0, tiled=True)

    swap = [(0, 1), (1, 0)]
    blocks = (here, below, above, low, high)
    keep, give = panel(place, blocks, two)
    selfs, bmat = settle(place, eps_occ, keep, lax.ppermute(give, "core", swap), eps_vir, two)
    keep, give = gram(place, blocks, sides, selfs)
    got = lax.ppermute(give, "core", swap)
    scale = 1.0 / (float(vir) * float(vir) * 2048.0)
    energy = energies(scale, place, eps_occ, keep, got, eps_vir, selfs)
    energy = lax.all_to_all(energy, CHIPS, 0, 0, tiled=True)
    energy = lax.psum(small(last_kernel, (occ, occ), "last")(energy), "core")
    return bmat.reshape(1, 32, vir), energy


def solution(mesh):
    fine = Mesh(mesh.devices.reshape(4, 2, 4, 2, 4, 2), AXES)
    return jax.shard_map(
        body,
        mesh=fine,
        in_specs=(P(), P(), P(GRP, PAIR, None), P(GRP, None), P(GRP), P(), P()),
        out_specs=(P(GRP, PAIR, None), P()),
        check_vma=False,
    )
```

```python
import functools

import jax
import jax.numpy as jnp
from jax import lax
from jax.experimental import pallas as pl
from jax.experimental.pallas import tpu as pltpu
from jax.sharding import Mesh, PartitionSpec as P

SHELL = 64
SHELLS = 12
TILES = 16
AXES = ("zh", "zl", "x", "yl", "yh", "core")
CHIPS = ("zh", "zl", "x", "yl", "yh")
PAIR = ("zh", "zl", "x", "yl")
NEAR = ("zl", "x", "yl", "core")
FAR = ("zh", "yh")
GRP = ("yh", "core")
F32 = jnp.float32
BF16 = jnp.bfloat16
VMEM = pl.BlockSpec(memory_space=pltpu.VMEM)
SMEM = pl.BlockSpec(memory_space=pltpu.SMEM)
HBM = pl.BlockSpec(memory_space=pltpu.HBM)
TRANSPOSED = (((0,), (0,)), ((), ()))


def lanes(shape):
    return lax.broadcasted_iota(jnp.int32, shape, 1)


def grant(mib):
    return pltpu.CompilerParams(vmem_limit_bytes=mib * 1024 * 1024)


def rows(shape):
    return lax.broadcasted_iota(jnp.int32, shape, 0)


def half_kernel(blocks_at, screen_at, c_occ_at, ints, out, blocks, screen, c_occ, held, spread, coef, sems):
    count = held.shape[0]
    first = [
        pltpu.make_async_copy(blocks_at, blocks, sems.at[count]),
        pltpu.make_async_copy(screen_at, screen, sems.at[count + 1]),
        pltpu.make_async_copy(c_occ_at, c_occ, sems.at[count + 2]),
    ]
    for copy in first:
        copy.start()
    for b in range(count):
        pltpu.make_async_copy(ints.at[b], held.at[b], sems.at[b]).start()
    shape = (SHELL, 4096)
    spread[...] = (lanes(shape) // SHELL == rows(shape)).astype(F32).astype(BF16)
    for copy in first:
        copy.wait()
    own = []
    for b in range(count):
        first = blocks[0, b]
        at = pl.multiple_of((first // 2) * 128, 128)
        shell = pltpu.roll(c_occ[:, pl.ds(at, 128)].astype(F32), (first % 2) * SHELL, 1)[:, :SHELL]
        own.append(shell * screen[b].astype(F32))
    own = jnp.concatenate(own, axis=0).astype(BF16)
    coef[...] = jnp.dot(own, spread[...], preferred_element_type=F32).reshape(count, 8, 4096)
    left = lanes((32, 128)) < SHELL

    @pl.loop(0, count)
    def _(block):
        pltpu.make_async_copy(ints.at[block], held.at[block], sems.at[block]).wait()

        def step(t, sums):
            at = pl.multiple_of(t * 128, 128)
            tile = held[block, :, pl.ds(at, 128)].astype(F32)
            weights = coef[block, :, pl.ds(at, 128)]
            return tuple(sums[i] + tile * weights[i : i + 1] for i in range(8))

        sums = lax.fori_loop(0, 32, step, (jnp.zeros((32, 128), F32),) * 8, unroll=8)
        full = [s + pltpu.roll(s, SHELL, 1) for s in sums]
        shell = blocks[1, block].astype(F32)
        put = pl.multiple_of(block * 16, 16)
        for yh in range(4):
            both = jnp.where(left, full[2 * yh], full[2 * yh + 1])
            for core in range(2):
                d = yh * 2 + core
                out[d, pl.ds(put, 16), :] = both[core * 16 : core * 16 + 16]
                out[d, 64:72, :] = jnp.where(rows((8, 128)) == block, shell, out[d, 64:72, :])


def half_transform(c_occ, ints, blocks, screen):
    return pl.pallas_call(
        half_kernel,
        out_shape=jax.ShapeDtypeStruct((8, 72, 128), F32),
        in_specs=[HBM, HBM, HBM, HBM],
        out_specs=VMEM,
        scratch_shapes=[
            pltpu.SMEM((2, ints.shape[0]), jnp.int32),
            pltpu.SMEM(screen.shape, jnp.int32),
            pltpu.VMEM((8, c_occ.shape[0]), BF16),
            pltpu.VMEM(ints.shape, BF16),
            pltpu.VMEM((SHELL, 4096), BF16),
            pltpu.VMEM((ints.shape[0], 8, 4096), F32),
            pltpu.SemaphoreType.DMA((ints.shape[0] + 3,)),
        ],
        compiler_params=grant(54),
        name="half",
    )(blocks.T, screen, c_occ.T, ints)


def hold_kernel(c_vir, out, sem):
    copy = pltpu.make_async_copy(c_vir, out, sem)
    copy.start()
    copy.wait()


def hold(c_vir):
    return pl.pallas_call(
        hold_kernel,
        out_shape=jax.ShapeDtypeStruct(c_vir.shape, BF16),
        in_specs=[HBM],
        out_specs=VMEM,
        scratch_shapes=[pltpu.SemaphoreType.DMA],
        compiler_params=grant(50),
        cost_estimate=pl.CostEstimate(flops=1 << 33, bytes_accessed=1 << 22, transcendentals=0),
        name="hold",
    )(c_vir)


def rounded(x):
    return x.astype(BF16).astype(F32)


def finish(q, full, left, bmat, sides):
    bmat[:, q * 256 : q * 256 + 256] = full.astype(BF16)
    for t in range(2):
        one, two = full[0:16, t * 128 : t * 128 + 128], full[16:32, t * 128 : t * 128 + 128]
        tile = q * 2 + t
        sides[tile * 2] = jnp.where(left, one, pltpu.roll(two, SHELL, 1)).astype(BF16)
        sides[tile * 2 + 1] = jnp.where(left, pltpu.roll(one, SHELL, 1), two).astype(BF16)


def transform_kernel(recv, c_vir, wide, thin, bmat, terms, sides):
    left = lanes((16, 128)) < SHELL
    sums = [jnp.zeros((16, 128), F32) for _ in range(SHELLS)]
    for source in range(8):
        for b in range(4):
            data = recv[source, b * 16 : b * 16 + 16, :]
            shell = recv[source, 64 + b : 65 + b, :]
            for n in range(SHELLS):
                sums[n] = sums[n] + jnp.where(shell == float(n), data, 0.0)
    for m in range(SHELLS // 2):
        one, two = sums[2 * m], sums[2 * m + 1]
        pair = (
            jnp.where(left, one, pltpu.roll(two, SHELL, 1)),
            jnp.where(left, pltpu.roll(one, SHELL, 1), two),
        )
        for i in range(2):
            value = pair[i]
            for term in range(3):
                part = rounded(value)
                terms[term * 32 + i * 16 : term * 32 + i * 16 + 16, m * 128 : m * 128 + 128] = part.astype(BF16)
                value = value - part
    for q in range(TILES // 2):
        got = jnp.dot(terms[...], c_vir[:, q * 256 : q * 256 + 256], preferred_element_type=F32)
        full = (got[64:96] + got[32:64]) + got[0:32]
        finish(q, full, left, bmat, sides)
    for r in range(TILES):
        for yh in range(4):
            wide[r * 4 + yh] = bmat[:, r * 128 : r * 128 + 128]
            for x in range(4):
                kind = x * 4 + yh
                other = (r + kind // 2 + 1) % TILES
                thin[((r // 2 * 4 + x) * 2 + r % 2) * 4 + yh] = sides[other * 2 + kind % 2]


def transform(recv, c_vir):
    return pl.pallas_call(
        transform_kernel,
        out_shape=(
            jax.ShapeDtypeStruct((64, 32, 128), BF16),
            jax.ShapeDtypeStruct((256, 16, 128), BF16),
        ),
        in_specs=[VMEM, VMEM],
        out_specs=(VMEM, VMEM),
        scratch_shapes=[
            pltpu.VMEM((32, c_vir.shape[1]), BF16),
            pltpu.VMEM((96, c_vir.shape[0]), BF16),
            pltpu.VMEM((32, 16, 128), BF16),
        ],
        compiler_params=grant(16),
        name="transform",
    )(recv, c_vir)


def onward_kernel(below, above, low, high):
    low[...] = above[0:32]
    high[...] = below[32:64]


def onward(below, above):
    half = jax.ShapeDtypeStruct((32,) + below.shape[1:], BF16)
    return pl.pallas_call(
        onward_kernel,
        out_shape=(half, half),
        in_specs=[VMEM, VMEM],
        out_specs=(VMEM, VMEM),
        compiler_params=grant(4),
        cost_estimate=pl.CostEstimate(flops=1 << 35, bytes_accessed=1 << 21, transcendentals=0),
        name="onward",
    )(below, above)


def panel_kernel(place, here, below, above, low, high, thin, keep, give, mine, wide, all_s, held, sem):
    core, side, own = place[4], place[3], place[5]
    copies = []
    for piece in range(2 * TILES):
        r = (piece // 2 - 1) % TILES
        at = (r // 2 * 8 + r % 2) * 4 + piece % 2
        copies.append(pltpu.make_async_copy(thin.at[at], held.at[piece], sem.at[piece]))
        copies[piece].start()
    first = 0
    for tiles in (here, below, above, low, high):
        count = tiles.shape[0] * 16
        for i in range(8):
            wide[first : first + count, i * 128 : i * 128 + 128] = tiles[:, i].reshape(count, 128)
        first += count
    first = wide[:, pl.ds(pl.multiple_of(own * 128, 128), 128)]
    others = wide[:, pl.ds(pl.multiple_of(side * 512, 512), 512)]
    all_s[...] = lax.dot_general(first, others, TRANSPOSED, preferred_element_type=F32)
    for which, target in ((core, keep), (1 - core, give)):
        at = pl.multiple_of(which * 256, 256)
        for q in range(4):
            target[0:32, q * 256 : q * 256 + 256] = all_s[q * 32 : q * 32 + 32, pl.ds(at, 256)]
    for copy in copies:
        copy.wait()
    left = lanes((16, 128)) < SHELL
    for t in range(TILES):
        one, two = held[t * 2].astype(F32), held[t * 2 + 1].astype(F32)
        even = jnp.where(left, one, pltpu.roll(two, SHELL, 1))
        odd = jnp.where(left, pltpu.roll(one, SHELL, 1), two)
        mine[:, t * 128 : t * 128 + 128] = jnp.where(core == 0, even, odd).astype(BF16)
        q, at = t // 8, t % 8 * 128
        give[32 + q * 16 : 48 + q * 16, at : at + 128] = jnp.where(core == 0, odd, even)


def panel(place, blocks, thin):
    tiles = (block.reshape(-1, 8, 16, 128) for block in blocks)
    return pl.pallas_call(
        panel_kernel,
        out_shape=(
            jax.ShapeDtypeStruct((32, 1024), F32),
            jax.ShapeDtypeStruct((64, 1024), F32),
            jax.ShapeDtypeStruct((16, 128 * TILES), BF16),
        ),
        in_specs=[SMEM] + [VMEM] * 5 + [HBM],
        out_specs=(VMEM, VMEM, VMEM),
        scratch_shapes=[
            pltpu.VMEM((1024, 1024), BF16),
            pltpu.VMEM((128, 512), F32),
            pltpu.VMEM((2 * TILES, 16, 128), BF16),
            pltpu.SemaphoreType.DMA((2 * TILES,)),
        ],
        compiler_params=grant(8),
        cost_estimate=pl.CostEstimate(flops=1 << 29, bytes_accessed=1 << 22, transcendentals=0),
        name="panel",
    )(place, *tiles, thin)


def settle_kernel(place, eps_occ, keep, got, eps_vir, mine, out, bmat):
    tile, side, core, own = (place[n] for n in (0, 3, 4, 5))
    row_a = eps_vir[pl.ds(tile, 1), :]
    square = (128, 128)
    col_a = jnp.sum(jnp.where(lanes(square) == rows(square), row_a, 0.0), axis=1, keepdims=True)
    for m in range(2):
        j = side * 4 + core * 2 + m
        block = jnp.concatenate(
            [
                keep[0:32, q * 256 + m * 128 : q * 256 + m * 128 + 128]
                + got[0:32, q * 256 + m * 128 : q * 256 + m * 128 + 128]
                for q in range(4)
            ],
            axis=0,
        )
        denominators = (eps_occ[own] + eps_occ[j] - row_a) - col_a
        terms = block * (2.0 * block - block.T) / denominators
        out[m : m + 1, :] = jnp.sum(terms, axis=0, keepdims=True)
    here = pl.ds(pl.multiple_of(core * 16, 16), 16)
    bmat[here, :] = mine[...]
    there = pl.ds(pl.multiple_of((1 - core) * 16, 16), 16)
    for q in range(2):
        bmat[there, q * 1024 : q * 1024 + 1024] = got[32 + q * 16 : 48 + q * 16, :].astype(BF16)


def settle(place, eps_occ, keep, got, eps_vir, mine):
    return pl.pallas_call(
        settle_kernel,
        out_shape=(jax.ShapeDtypeStruct((8, 128), F32), jax.ShapeDtypeStruct((32, mine.shape[1]), BF16)),
        in_specs=[SMEM, SMEM, VMEM, VMEM, VMEM, VMEM],
        out_specs=(VMEM, VMEM),
        compiler_params=grant(4),
        cost_estimate=pl.CostEstimate(flops=1 << 28, bytes_accessed=1 << 20, transcendentals=0),
        name="settle",
    )(place, eps_occ, keep, got, eps_vir.reshape(-1, 128), mine)


def gram_kernel(place, here, below, above, low, high, sides, _, keep, give, wide, thin, all_t):
    core, x = place[4], place[6]
    first = 0
    for away, tiles in ((0, here), (3, below), (1, above), (2, low), (2, high)):
        count = tiles.shape[0] * 16
        for i in range(8):
            wide[first : first + count, i * 128 : i * 128 + 128] = tiles[:, i].reshape(count, 128)
        z = 4 if tiles is high else 0
        for p in range(4):
            rows_z = sides[z : z + count // 32, (x + away) & 3, :, p]
            thin[first : first + count, p * 128 : p * 128 + 128] = rows_z.reshape(count, 128)
        first += count
    for p in range(4):
        part = lax.dot_general(thin[:, p * 128 : p * 128 + 128], wide[...], TRANSPOSED, preferred_element_type=F32)
        all_t[p * 128 : p * 128 + 128, :] = part
    for which, target in ((core, keep), (1 - core, give)):
        for j in range(8):
            at = pl.multiple_of(j * 64 + which * 32, 32)
            target[j * 32 : j * 32 + 32, :] = all_t[pl.ds(at, 32), :]


def gram(place, blocks, sides, after):
    tiles = (block.reshape(-1, 8, 16, 128) for block in blocks)
    shape = jax.ShapeDtypeStruct((256, 1024), F32)
    return pl.pallas_call(
        gram_kernel,
        out_shape=(shape, shape),
        in_specs=[SMEM] + [VMEM] * 6 + [HBM],
        out_specs=(VMEM, VMEM),
        scratch_shapes=[
            pltpu.VMEM((1024, 1024), BF16),
            pltpu.VMEM((1024, 512), BF16),
            pltpu.VMEM((512, 1024), F32),
        ],
        compiler_params=grant(16),
        name="gram",
    )(place, *tiles, sides.reshape(8, 4, 2, 4, 16, 128), after)


def energy_kernel(scale, place, eps_occ, keep, got, eps_vir, selfs, out, parts):
    tile, other, step, side, core, own = (place[n] for n in range(6))
    row_a = eps_vir[pl.ds(tile, 1), :]
    row_b = eps_vir[pl.ds(other, 1), :]
    first = side * 64 + core * 32
    col_b = jnp.sum(jnp.where(lanes((32, 128)) == rows((32, 128)) + first, row_b, 0.0), axis=1, keepdims=True)
    weight = jnp.where(step == 8, 1.0, 2.0)
    for i in range(8):
        for j in range(i, 8):
            there = slice(j * 32, j * 32 + 32), slice(i * 128, i * 128 + 128)
            here = slice(i * 32, i * 32 + 32), slice(j * 128, j * 128 + 128)
            one = keep[there] + got[there]
            two = keep[here] + got[here]
            denominators = (eps_occ[i] + eps_occ[j] - row_a) - col_b
            terms = (one * one + two * two - one * two) / denominators
            part = jnp.sum(terms, axis=0, keepdims=True) * weight
            parts[i * 8 + j : i * 8 + j + 1, :] = part
            parts[j * 8 + i : j * 8 + i + 1, :] = part
    for m in range(2):
        at = pl.ds(own * 8 + side * 4 + core * 2 + m, 1)
        parts[at, :] = parts[at, :] + selfs[m : m + 1, :]
    column = jnp.sum(parts[...], axis=1, keepdims=True) * scale
    row = jnp.sum(jnp.where(lanes((64, 128)) == rows((64, 128)), column, 0.0), axis=0, keepdims=True)
    out[...] = jnp.broadcast_to(row[None], out.shape)


def energies(scale, place, eps_occ, keep, got, eps_vir, selfs):
    return pl.pallas_call(
        functools.partial(energy_kernel, scale),
        out_shape=jax.ShapeDtypeStruct((32, 1, 128), F32),
        in_specs=[SMEM, SMEM, VMEM, VMEM, VMEM, VMEM],
        out_specs=VMEM,
        scratch_shapes=[pltpu.VMEM((64, 128), F32)],
        compiler_params=grant(6),
        name="energies",
    )(place, eps_occ, keep, got, eps_vir.reshape(-1, 128), selfs)


def position():
    zh, zl, x, yl, yh, core = (lax.axis_index(axis) for axis in AXES)
    tile, kind = zh * 4 + zl * 2 + yl, x * 4 + yh
    step, side = lax.shift_right_logical(kind, 1) + 1, kind & 1
    return jnp.stack([tile, (tile + step) & (TILES - 1), step, side, core, lax.shift_right_logical(kind, 1), x])


def again_kernel(got, out):
    out[...] = jnp.broadcast_to(jnp.sum(got[...], axis=0)[None], out.shape)


def last_kernel(got, out):
    row = jnp.broadcast_to(jnp.sum(got[...], axis=0), (8, 128))
    place = rows((8, 128))
    square = row
    for i in range(1, 8):
        square = jnp.where(place == i, pltpu.roll(row, 128 - 8 * i, 1), square)
    out[...] = square[:, :8]


def small(kernel, shape, name):
    return pl.pallas_call(
        kernel,
        out_shape=jax.ShapeDtypeStruct(shape, F32),
        in_specs=[VMEM],
        out_specs=VMEM,
        compiler_params=grant(2),
        name=name,
    )


def body(c_occ, c_vir, ints, blocks, screen, eps_occ, eps_vir):
    vir, occ = c_vir.shape[1], c_occ.shape[1]
    place = position()
    sent = half_transform(c_occ, ints, blocks, screen)
    recv = lax.all_to_all(sent, GRP, 0, 0, tiled=True)
    wide, thin = transform(recv, hold(c_vir))
    here = lax.all_to_all(wide, ("zh", "zl", "yl", "yh"), 0, 0, tiled=True)
    up = [(i, (i + 1) % 4) for i in range(4)]
    down = [(i, (i + 3) % 4) for i in range(4)]
    below, above = lax.ppermute(here, "x", up), lax.ppermute(here, "x", down)
    low, high = onward(below, above)
    low, high = lax.ppermute(low, "x", down), lax.ppermute(high, "x", up)
    sides = lax.all_to_all(thin, CHIPS, 0, 0, tiled=True)

    swap = [(0, 1), (1, 0)]
    blocks = (here, below, above, low, high)
    keep, give, mine = panel(place, blocks, thin)
    selfs, bmat = settle(place, eps_occ, keep, lax.ppermute(give, "core", swap), eps_vir, mine)
    keep, give = gram(place, blocks, sides, selfs)
    got = lax.ppermute(give, "core", swap)
    scale = 1.0 / (float(vir) * float(vir) * 2048.0)
    energy = energies(scale, place, eps_occ, keep, got, eps_vir, selfs)
    energy = lax.all_to_all(energy, NEAR, 0, 0, tiled=True)
    energy = lax.all_to_all(small(again_kernel, (16, 1, 128), "again")(energy), FAR, 0, 0, tiled=True)
    energy = small(last_kernel, (occ, occ), "last")(energy)
    return bmat.reshape(1, 32, vir), energy


def solution(mesh):
    fine = Mesh(mesh.devices.reshape(4, 2, 4, 2, 4, 2), AXES)
    return jax.shard_map(
        body,
        mesh=fine,
        in_specs=(P(), P(), P(GRP, PAIR, None), P(GRP, None), P(GRP), P(), P()),
        out_specs=(P(GRP, PAIR, None), P()),
        check_vma=False,
    )
```

```python
import functools

import jax
import jax.numpy as jnp
from jax import lax
from jax.experimental import pallas as pl
from jax.experimental.pallas import tpu as pltpu
from jax.sharding import Mesh, PartitionSpec as P

SHELL = 64
SHELLS = 12
TILES = 16
AXES = ("zh", "zl", "x", "yl", "yh", "core")
CHIPS = ("zh", "zl", "x", "yl", "yh")
PAIR = ("zh", "zl", "x", "yl")
NEAR = ("zl", "x", "yl", "core")
FAR = ("zh", "yh")
GRP = ("yh", "core")
F32 = jnp.float32
BF16 = jnp.bfloat16
VMEM = pl.BlockSpec(memory_space=pltpu.VMEM)
SMEM = pl.BlockSpec(memory_space=pltpu.SMEM)
HBM = pl.BlockSpec(memory_space=pltpu.HBM)
TRANSPOSED = (((0,), (0,)), ((), ()))


def lanes(shape):
    return lax.broadcasted_iota(jnp.int32, shape, 1)


def grant(mib):
    return pltpu.CompilerParams(vmem_limit_bytes=mib * 1024 * 1024)


def rows(shape):
    return lax.broadcasted_iota(jnp.int32, shape, 0)


def half_kernel(blocks_at, screen_at, c_occ_at, ints, out, blocks, screen, c_occ, held, spread, coef, sems):
    count = held.shape[0]
    first = [
        pltpu.make_async_copy(blocks_at, blocks, sems.at[count]),
        pltpu.make_async_copy(screen_at, screen, sems.at[count + 1]),
        pltpu.make_async_copy(c_occ_at, c_occ, sems.at[count + 2]),
    ]
    for copy in first:
        copy.start()
    for b in range(count):
        pltpu.make_async_copy(ints.at[b], held.at[b], sems.at[b]).start()
    shape = (SHELL, 4096)
    spread[...] = (lanes(shape) // SHELL == rows(shape)).astype(F32).astype(BF16)
    for copy in first:
        copy.wait()
    own = []
    for b in range(count):
        first = blocks[0, b]
        at = pl.multiple_of((first // 2) * 128, 128)
        shell = pltpu.roll(c_occ[:, pl.ds(at, 128)].astype(F32), (first % 2) * SHELL, 1)[:, :SHELL]
        own.append(shell * screen[b].astype(F32))
    own = jnp.concatenate(own, axis=0).astype(BF16)
    coef[...] = jnp.dot(own, spread[...], preferred_element_type=F32).reshape(count, 8, 4096)
    left = lanes((32, 128)) < SHELL

    @pl.loop(0, count)
    def _(block):
        pltpu.make_async_copy(ints.at[block], held.at[block], sems.at[block]).wait()

        def step(t, sums):
            at = pl.multiple_of(t * 128, 128)
            tile = held[block, :, pl.ds(at, 128)].astype(F32)
            weights = coef[block, :, pl.ds(at, 128)]
            return tuple(sums[i] + tile * weights[i : i + 1] for i in range(8))

        sums = lax.fori_loop(0, 32, step, (jnp.zeros((32, 128), F32),) * 8, unroll=8)
        full = [s + pltpu.roll(s, SHELL, 1) for s in sums]
        shell = blocks[1, block].astype(F32)
        put = pl.multiple_of(block * 16, 16)
        for yh in range(4):
            both = jnp.where(left, full[2 * yh], full[2 * yh + 1])
            for core in range(2):
                d = yh * 2 + core
                out[d, pl.ds(put, 16), :] = both[core * 16 : core * 16 + 16]
                out[d, 64:72, :] = jnp.where(rows((8, 128)) == block, shell, out[d, 64:72, :])


def half_transform(c_occ, ints, blocks, screen):
    return pl.pallas_call(
        half_kernel,
        out_shape=jax.ShapeDtypeStruct((8, 72, 128), F32),
        in_specs=[HBM, HBM, HBM, HBM],
        out_specs=VMEM,
        scratch_shapes=[
            pltpu.SMEM((2, ints.shape[0]), jnp.int32),
            pltpu.SMEM(screen.shape, jnp.int32),
            pltpu.VMEM((8, c_occ.shape[0]), BF16),
            pltpu.VMEM(ints.shape, BF16),
            pltpu.VMEM((SHELL, 4096), BF16),
            pltpu.VMEM((ints.shape[0], 8, 4096), F32),
            pltpu.SemaphoreType.DMA((ints.shape[0] + 3,)),
        ],
        compiler_params=grant(54),
        name="half",
    )(blocks.T, screen, c_occ.T, ints)


def hold_kernel(c_vir, out, sem):
    copy = pltpu.make_async_copy(c_vir, out, sem)
    copy.start()
    copy.wait()


def hold(c_vir):
    return pl.pallas_call(
        hold_kernel,
        out_shape=jax.ShapeDtypeStruct(c_vir.shape, BF16),
        in_specs=[HBM],
        out_specs=VMEM,
        scratch_shapes=[pltpu.SemaphoreType.DMA],
        compiler_params=grant(50),
        cost_estimate=pl.CostEstimate(flops=1 << 33, bytes_accessed=1 << 22, transcendentals=0),
        name="hold",
    )(c_vir)


def rounded(x):
    return x.astype(BF16).astype(F32)


def finish(q, full, left, bmat, sides):
    bmat[:, q * 256 : q * 256 + 256] = full.astype(BF16)
    for t in range(2):
        one, two = full[0:16, t * 128 : t * 128 + 128], full[16:32, t * 128 : t * 128 + 128]
        tile = q * 2 + t
        sides[tile * 2] = jnp.where(left, one, pltpu.roll(two, SHELL, 1)).astype(BF16)
        sides[tile * 2 + 1] = jnp.where(left, pltpu.roll(one, SHELL, 1), two).astype(BF16)


def transform_kernel(recv, c_vir, bmat, wide, thin, terms, sides):
    left = lanes((16, 128)) < SHELL
    sums = [jnp.zeros((16, 128), F32) for _ in range(SHELLS)]
    for source in range(8):
        for b in range(4):
            data = recv[source, b * 16 : b * 16 + 16, :]
            shell = recv[source, 64 + b : 65 + b, :]
            for n in range(SHELLS):
                sums[n] = sums[n] + jnp.where(shell == float(n), data, 0.0)
    for m in range(SHELLS // 2):
        one, two = sums[2 * m], sums[2 * m + 1]
        pair = (
            jnp.where(left, one, pltpu.roll(two, SHELL, 1)),
            jnp.where(left, pltpu.roll(one, SHELL, 1), two),
        )
        for i in range(2):
            value = pair[i]
            for term in range(3):
                part = rounded(value)
                terms[term * 32 + i * 16 : term * 32 + i * 16 + 16, m * 128 : m * 128 + 128] = part.astype(BF16)
                value = value - part
    for q in range(TILES // 2):
        got = jnp.dot(terms[...], c_vir[:, q * 256 : q * 256 + 256], preferred_element_type=F32)
        full = (got[64:96] + got[32:64]) + got[0:32]
        finish(q, full, left, bmat, sides)
    for r in range(TILES):
        for yh in range(4):
            wide[r * 4 + yh] = bmat[:, r * 128 : r * 128 + 128]
            for x in range(4):
                kind = x * 4 + yh
                other = (r + kind // 2 + 1) % TILES
                thin[((r // 2 * 4 + x) * 2 + r % 2) * 4 + yh] = sides[other * 2 + kind % 2]


def transform(recv, c_vir):
    return pl.pallas_call(
        transform_kernel,
        out_shape=(
            jax.ShapeDtypeStruct((32, c_vir.shape[1]), BF16),
            jax.ShapeDtypeStruct((64, 32, 128), BF16),
            jax.ShapeDtypeStruct((256, 16, 128), BF16),
        ),
        in_specs=[VMEM, VMEM],
        out_specs=(VMEM, VMEM, VMEM),
        scratch_shapes=[pltpu.VMEM((96, c_vir.shape[0]), BF16), pltpu.VMEM((32, 16, 128), BF16)],
        compiler_params=grant(16),
        name="transform",
    )(recv, c_vir)


def onward_kernel(below, above, low, high):
    low[...] = above[0:32]
    high[...] = below[32:64]


def onward(below, above):
    half = jax.ShapeDtypeStruct((32,) + below.shape[1:], BF16)
    return pl.pallas_call(
        onward_kernel,
        out_shape=(half, half),
        in_specs=[VMEM, VMEM],
        out_specs=(VMEM, VMEM),
        compiler_params=grant(4),
        cost_estimate=pl.CostEstimate(flops=1 << 35, bytes_accessed=1 << 21, transcendentals=0),
        name="onward",
    )(below, above)


def panel_kernel(place, here, below, above, low, high, two, keep, give, wide, all_s):
    core, side, own = place[4], place[3], place[5]
    first = 0
    for tiles in (here, below, above, low, high):
        count = tiles.shape[0] * 16
        wide[first : first + count, 512:640] = tiles[:, own].reshape(count, 128)
        for m in range(4):
            wide[first : first + count, m * 128 : m * 128 + 128] = tiles[:, side * 4 + m].reshape(count, 128)
        first += count
    mine, others = wide[:, 512:640], wide[:, 0:512]
    all_s[...] = lax.dot_general(mine, others, TRANSPOSED, preferred_element_type=F32)
    for which, target in ((core, keep), (1 - core, give)):
        at = pl.multiple_of(which * 256, 256)
        for q in range(4):
            target[0:32, q * 256 : q * 256 + 256] = all_s[q * 32 : q * 32 + 32, pl.ds(at, 256)]
    at = pl.multiple_of((1 - core) * 16, 16)
    for q in range(2):
        give[32 + q * 16 : 48 + q * 16, :] = two[pl.ds(at, 16), q * 1024 : q * 1024 + 1024].astype(F32)


def panel(place, blocks, two):
    tiles = (block.reshape(-1, 8, 16, 128) for block in blocks)
    return pl.pallas_call(
        panel_kernel,
        out_shape=(
            jax.ShapeDtypeStruct((32, 1024), F32),
            jax.ShapeDtypeStruct((64, 1024), F32),
        ),
        in_specs=[SMEM] + [VMEM] * 6,
        out_specs=(VMEM, VMEM),
        scratch_shapes=[pltpu.VMEM((1024, 640), BF16), pltpu.VMEM((128, 512), F32)],
        compiler_params=grant(8),
        cost_estimate=pl.CostEstimate(flops=1 << 29, bytes_accessed=1 << 22, transcendentals=0),
        name="panel",
    )(place, *tiles, two)


def settle_kernel(place, eps_occ, keep, got, eps_vir, mine, out, bmat):
    tile, side, core, own = (place[n] for n in (0, 3, 4, 5))
    row_a = eps_vir[pl.ds(tile, 1), :]
    square = (128, 128)
    col_a = jnp.sum(jnp.where(lanes(square) == rows(square), row_a, 0.0), axis=1, keepdims=True)
    for m in range(2):
        j = side * 4 + core * 2 + m
        block = jnp.concatenate(
            [
                keep[0:32, q * 256 + m * 128 : q * 256 + m * 128 + 128]
                + got[0:32, q * 256 + m * 128 : q * 256 + m * 128 + 128]
                for q in range(4)
            ],
            axis=0,
        )
        denominators = (eps_occ[own] + eps_occ[j] - row_a) - col_a
        terms = block * (2.0 * block - block.T) / denominators
        out[m : m + 1, :] = jnp.sum(terms, axis=0, keepdims=True)
    here = pl.ds(pl.multiple_of(core * 16, 16), 16)
    bmat[here, :] = mine[here, :]
    there = pl.ds(pl.multiple_of((1 - core) * 16, 16), 16)
    for q in range(2):
        bmat[there, q * 1024 : q * 1024 + 1024] = got[32 + q * 16 : 48 + q * 16, :].astype(BF16)


def settle(place, eps_occ, keep, got, eps_vir, two):
    return pl.pallas_call(
        settle_kernel,
        out_shape=(jax.ShapeDtypeStruct((8, 128), F32), jax.ShapeDtypeStruct(two.shape, BF16)),
        in_specs=[SMEM, SMEM, VMEM, VMEM, VMEM, VMEM],
        out_specs=(VMEM, VMEM),
        compiler_params=grant(4),
        cost_estimate=pl.CostEstimate(flops=1 << 28, bytes_accessed=1 << 20, transcendentals=0),
        name="settle",
    )(place, eps_occ, keep, got, eps_vir.reshape(-1, 128), two)


def gram_kernel(place, here, below, above, low, high, sides, _, keep, give, wide, thin, all_t):
    core, x = place[4], place[6]
    first = 0
    for away, tiles in ((0, here), (3, below), (1, above), (2, low), (2, high)):
        count = tiles.shape[0] * 16
        for i in range(8):
            wide[first : first + count, i * 128 : i * 128 + 128] = tiles[:, i].reshape(count, 128)
        z = 4 if tiles is high else 0
        for p in range(4):
            rows_z = sides[z : z + count // 32, (x + away) & 3, :, p]
            thin[first : first + count, p * 128 : p * 128 + 128] = rows_z.reshape(count, 128)
        first += count
    for p in range(4):
        part = lax.dot_general(thin[:, p * 128 : p * 128 + 128], wide[...], TRANSPOSED, preferred_element_type=F32)
        all_t[p * 128 : p * 128 + 128, :] = part
    for which, target in ((core, keep), (1 - core, give)):
        for j in range(8):
            at = pl.multiple_of(j * 64 + which * 32, 32)
            target[j * 32 : j * 32 + 32, :] = all_t[pl.ds(at, 32), :]


def gram(place, blocks, sides, after):
    tiles = (block.reshape(-1, 8, 16, 128) for block in blocks)
    shape = jax.ShapeDtypeStruct((256, 1024), F32)
    return pl.pallas_call(
        gram_kernel,
        out_shape=(shape, shape),
        in_specs=[SMEM] + [VMEM] * 6 + [HBM],
        out_specs=(VMEM, VMEM),
        scratch_shapes=[
            pltpu.VMEM((1024, 1024), BF16),
            pltpu.VMEM((1024, 512), BF16),
            pltpu.VMEM((512, 1024), F32),
        ],
        compiler_params=grant(16),
        name="gram",
    )(place, *tiles, sides.reshape(8, 4, 2, 4, 16, 128), after)


def energy_kernel(scale, place, eps_occ, keep, got, eps_vir, selfs, out, parts):
    tile, other, step, side, core, own = (place[n] for n in range(6))
    row_a = eps_vir[pl.ds(tile, 1), :]
    row_b = eps_vir[pl.ds(other, 1), :]
    first = side * 64 + core * 32
    col_b = jnp.sum(jnp.where(lanes((32, 128)) == rows((32, 128)) + first, row_b, 0.0), axis=1, keepdims=True)
    weight = jnp.where(step == 8, 1.0, 2.0)
    for i in range(8):
        for j in range(i, 8):
            there = slice(j * 32, j * 32 + 32), slice(i * 128, i * 128 + 128)
            here = slice(i * 32, i * 32 + 32), slice(j * 128, j * 128 + 128)
            one = keep[there] + got[there]
            two = keep[here] + got[here]
            denominators = (eps_occ[i] + eps_occ[j] - row_a) - col_b
            terms = (one * one + two * two - one * two) / denominators
            part = jnp.sum(terms, axis=0, keepdims=True) * weight
            parts[i * 8 + j : i * 8 + j + 1, :] = part
            parts[j * 8 + i : j * 8 + i + 1, :] = part
    for m in range(2):
        at = pl.ds(own * 8 + side * 4 + core * 2 + m, 1)
        parts[at, :] = parts[at, :] + selfs[m : m + 1, :]
    column = jnp.sum(parts[...], axis=1, keepdims=True) * scale
    row = jnp.sum(jnp.where(lanes((64, 128)) == rows((64, 128)), column, 0.0), axis=0, keepdims=True)
    out[...] = jnp.broadcast_to(row[None], out.shape)


def energies(scale, place, eps_occ, keep, got, eps_vir, selfs):
    return pl.pallas_call(
        functools.partial(energy_kernel, scale),
        out_shape=jax.ShapeDtypeStruct((32, 1, 128), F32),
        in_specs=[SMEM, SMEM, VMEM, VMEM, VMEM, VMEM],
        out_specs=VMEM,
        scratch_shapes=[pltpu.VMEM((64, 128), F32)],
        compiler_params=grant(6),
        name="energies",
    )(place, eps_occ, keep, got, eps_vir.reshape(-1, 128), selfs)


def position():
    zh, zl, x, yl, yh, core = (lax.axis_index(axis) for axis in AXES)
    tile, kind = zh * 4 + zl * 2 + yl, x * 4 + yh
    step, side = lax.shift_right_logical(kind, 1) + 1, kind & 1
    return jnp.stack([tile, (tile + step) & (TILES - 1), step, side, core, lax.shift_right_logical(kind, 1), x])


def again_kernel(got, out):
    out[...] = jnp.broadcast_to(jnp.sum(got[...], axis=0)[None], out.shape)


def last_kernel(got, out):
    row = jnp.broadcast_to(jnp.sum(got[...], axis=0), (8, 128))
    place = rows((8, 128))
    square = row
    for i in range(1, 8):
        square = jnp.where(place == i, pltpu.roll(row, 128 - 8 * i, 1), square)
    out[...] = square[:, :8]


def small(kernel, shape, name):
    return pl.pallas_call(
        kernel,
        out_shape=jax.ShapeDtypeStruct(shape, F32),
        in_specs=[VMEM],
        out_specs=VMEM,
        compiler_params=grant(2),
        name=name,
    )


def body(c_occ, c_vir, ints, blocks, screen, eps_occ, eps_vir):
    vir, occ = c_vir.shape[1], c_occ.shape[1]
    place = position()
    sent = half_transform(c_occ, ints, blocks, screen)
    recv = lax.all_to_all(sent, GRP, 0, 0, tiled=True)
    two, wide, thin = transform(recv, hold(c_vir))
    here = lax.all_to_all(wide, ("zh", "zl", "yl", "yh"), 0, 0, tiled=True)
    up = [(i, (i + 1) % 4) for i in range(4)]
    down = [(i, (i + 3) % 4) for i in range(4)]
    below, above = lax.ppermute(here, "x", up), lax.ppermute(here, "x", down)
    low, high = onward(below, above)
    low, high = lax.ppermute(low, "x", down), lax.ppermute(high, "x", up)
    sides = lax.all_to_all(thin, CHIPS, 0, 0, tiled=True)

    swap = [(0, 1), (1, 0)]
    blocks = (here, below, above, low, high)
    keep, give = panel(place, blocks, two)
    selfs, bmat = settle(place, eps_occ, keep, lax.ppermute(give, "core", swap), eps_vir, two)
    keep, give = gram(place, blocks, sides, selfs)
    got = lax.ppermute(give, "core", swap)
    scale = 1.0 / (float(vir) * float(vir) * 2048.0)
    energy = energies(scale, place, eps_occ, keep, got, eps_vir, selfs)
    energy = lax.all_to_all(energy, NEAR, 0, 0, tiled=True)
    energy = lax.all_to_all(small(again_kernel, (16, 1, 128), "again")(energy), FAR, 0, 0, tiled=True)
    energy = small(last_kernel, (occ, occ), "last")(energy)
    return bmat.reshape(1, 32, vir), energy


def solution(mesh):
    fine = Mesh(mesh.devices.reshape(4, 2, 4, 2, 4, 2), AXES)
    return jax.shard_map(
        body,
        mesh=fine,
        in_specs=(P(), P(), P(GRP, PAIR, None), P(GRP, None), P(GRP), P(), P()),
        out_specs=(P(GRP, PAIR, None), P()),
        check_vma=False,
    )
```

```python
import functools

import jax
import jax.numpy as jnp
from jax import lax
from jax.experimental import pallas as pl
from jax.experimental.pallas import tpu as pltpu
from jax.sharding import Mesh, PartitionSpec as P

SHELL = 64
SHELLS = 12
TILES = 16
AXES = ("zh", "zl", "x", "yl", "yh", "core")
CHIPS = ("zh", "zl", "x", "yl", "yh")
PAIR = ("zh", "zl", "x", "yl")
NEAR = ("zl", "x", "yl", "core")
FAR = ("zh", "yh")
GRP = ("yh", "core")
F32 = jnp.float32
BF16 = jnp.bfloat16
VMEM = pl.BlockSpec(memory_space=pltpu.VMEM)
SMEM = pl.BlockSpec(memory_space=pltpu.SMEM)
HBM = pl.BlockSpec(memory_space=pltpu.HBM)
TRANSPOSED = (((0,), (0,)), ((), ()))


def lanes(shape):
    return lax.broadcasted_iota(jnp.int32, shape, 1)


def grant(mib):
    return pltpu.CompilerParams(vmem_limit_bytes=mib * 1024 * 1024)


def rows(shape):
    return lax.broadcasted_iota(jnp.int32, shape, 0)


def half_kernel(blocks_at, screen_at, c_occ_at, ints, out, blocks, screen, c_occ, held, spread, coef, sems):
    count = held.shape[0]
    first = [
        pltpu.make_async_copy(blocks_at, blocks, sems.at[count]),
        pltpu.make_async_copy(screen_at, screen, sems.at[count + 1]),
        pltpu.make_async_copy(c_occ_at, c_occ, sems.at[count + 2]),
    ]
    for copy in first:
        copy.start()
    for b in range(count):
        pltpu.make_async_copy(ints.at[b], held.at[b], sems.at[b]).start()
    shape = (SHELL, 4096)
    spread[...] = (lanes(shape) // SHELL == rows(shape)).astype(F32).astype(BF16)
    for copy in first:
        copy.wait()
    own = []
    for b in range(count):
        first = blocks[0, b]
        at = pl.multiple_of((first // 2) * 128, 128)
        shell = pltpu.roll(c_occ[:, pl.ds(at, 128)].astype(F32), (first % 2) * SHELL, 1)[:, :SHELL]
        own.append(shell * screen[b].astype(F32))
    own = jnp.concatenate(own, axis=0).astype(BF16)
    coef[...] = jnp.dot(own, spread[...], preferred_element_type=F32).reshape(count, 8, 4096)
    left = lanes((32, 128)) < SHELL

    @pl.loop(0, count)
    def _(block):
        pltpu.make_async_copy(ints.at[block], held.at[block], sems.at[block]).wait()

        def step(t, sums):
            at = pl.multiple_of(t * 128, 128)
            tile = held[block, :, pl.ds(at, 128)].astype(F32)
            weights = coef[block, :, pl.ds(at, 128)]
            return tuple(sums[i] + tile * weights[i : i + 1] for i in range(8))

        sums = lax.fori_loop(0, 32, step, (jnp.zeros((32, 128), F32),) * 8, unroll=8)
        full = [s + pltpu.roll(s, SHELL, 1) for s in sums]
        shell = blocks[1, block].astype(F32)
        put = pl.multiple_of(block * 16, 16)
        for yh in range(4):
            both = jnp.where(left, full[2 * yh], full[2 * yh + 1])
            for core in range(2):
                d = yh * 2 + core
                out[d, pl.ds(put, 16), :] = both[core * 16 : core * 16 + 16]
                out[d, 64:72, :] = jnp.where(rows((8, 128)) == block, shell, out[d, 64:72, :])


def half_transform(c_occ, ints, blocks, screen):
    return pl.pallas_call(
        half_kernel,
        out_shape=jax.ShapeDtypeStruct((8, 72, 128), F32),
        in_specs=[HBM, HBM, HBM, HBM],
        out_specs=VMEM,
        scratch_shapes=[
            pltpu.SMEM((2, ints.shape[0]), jnp.int32),
            pltpu.SMEM(screen.shape, jnp.int32),
            pltpu.VMEM((8, c_occ.shape[0]), BF16),
            pltpu.VMEM(ints.shape, BF16),
            pltpu.VMEM((SHELL, 4096), BF16),
            pltpu.VMEM((ints.shape[0], 8, 4096), F32),
            pltpu.SemaphoreType.DMA((ints.shape[0] + 3,)),
        ],
        compiler_params=grant(54),
        name="half",
    )(blocks.T, screen, c_occ.T, ints)


def hold_kernel(c_vir, out, sem):
    copy = pltpu.make_async_copy(c_vir, out, sem)
    copy.start()
    copy.wait()


def hold(c_vir):
    return pl.pallas_call(
        hold_kernel,
        out_shape=jax.ShapeDtypeStruct(c_vir.shape, BF16),
        in_specs=[HBM],
        out_specs=VMEM,
        scratch_shapes=[pltpu.SemaphoreType.DMA],
        compiler_params=grant(50),
        cost_estimate=pl.CostEstimate(flops=1 << 33, bytes_accessed=1 << 22, transcendentals=0),
        name="hold",
    )(c_vir)


def rounded(x):
    return x.astype(BF16).astype(F32)


def finish(q, full, left, bmat, sides):
    bmat[:, q * 256 : q * 256 + 256] = full.astype(BF16)
    for t in range(2):
        one, two = full[0:16, t * 128 : t * 128 + 128], full[16:32, t * 128 : t * 128 + 128]
        tile = q * 2 + t
        sides[tile * 2] = jnp.where(left, one, pltpu.roll(two, SHELL, 1)).astype(BF16)
        sides[tile * 2 + 1] = jnp.where(left, pltpu.roll(one, SHELL, 1), two).astype(BF16)


def transform_kernel(recv, c_vir, bmat, wide, thin, terms, sides):
    left = lanes((16, 128)) < SHELL
    sums = [jnp.zeros((16, 128), F32) for _ in range(SHELLS)]
    for source in range(8):
        for b in range(4):
            data = recv[source, b * 16 : b * 16 + 16, :]
            shell = recv[source, 64 + b : 65 + b, :]
            for n in range(SHELLS):
                sums[n] = sums[n] + jnp.where(shell == float(n), data, 0.0)
    for m in range(SHELLS // 2):
        one, two = sums[2 * m], sums[2 * m + 1]
        pair = (
            jnp.where(left, one, pltpu.roll(two, SHELL, 1)),
            jnp.where(left, pltpu.roll(one, SHELL, 1), two),
        )
        for i in range(2):
            value = pair[i]
            for term in range(3):
                part = rounded(value)
                terms[term * 32 + i * 16 : term * 32 + i * 16 + 16, m * 128 : m * 128 + 128] = part.astype(BF16)
                value = value - part
    for q in range(TILES // 2):
        got = jnp.dot(terms[...], c_vir[:, q * 256 : q * 256 + 256], preferred_element_type=F32)
        full = (got[64:96] + got[32:64]) + got[0:32]
        finish(q, full, left, bmat, sides)
    for r in range(TILES):
        for yh in range(4):
            wide[r * 4 + yh] = bmat[:, r * 128 : r * 128 + 128]
            for x in range(4):
                kind = x * 4 + yh
                other = (r + kind // 2 + 1) % TILES
                thin[((r // 2 * 4 + x) * 2 + r % 2) * 4 + yh] = sides[other * 2 + kind % 2]


def transform(recv, c_vir):
    return pl.pallas_call(
        transform_kernel,
        out_shape=(
            jax.ShapeDtypeStruct((32, c_vir.shape[1]), BF16),
            jax.ShapeDtypeStruct((64, 32, 128), BF16),
            jax.ShapeDtypeStruct((256, 16, 128), BF16),
        ),
        in_specs=[VMEM, VMEM],
        out_specs=(VMEM, VMEM, VMEM),
        scratch_shapes=[pltpu.VMEM((96, c_vir.shape[0]), BF16), pltpu.VMEM((32, 16, 128), BF16)],
        compiler_params=grant(16),
        name="transform",
    )(recv, c_vir)


def onward_kernel(below, above, low, high):
    low[...] = above[0:32]
    high[...] = below[32:64]


def onward(below, above):
    half = jax.ShapeDtypeStruct((32,) + below.shape[1:], BF16)
    return pl.pallas_call(
        onward_kernel,
        out_shape=(half, half),
        in_specs=[VMEM, VMEM],
        out_specs=(VMEM, VMEM),
        compiler_params=grant(4),
        cost_estimate=pl.CostEstimate(flops=1 << 35, bytes_accessed=1 << 21, transcendentals=0),
        name="onward",
    )(below, above)


def panel_kernel(place, here, below, above, low, high, two, keep, give, wide, all_s):
    core, side, own = place[4], place[3], place[5]
    first = 0
    for tiles in (here, below, above, low, high):
        count = tiles.shape[0] * 16
        wide[first : first + count, 512:640] = tiles[:, own].reshape(count, 128)
        for m in range(4):
            wide[first : first + count, m * 128 : m * 128 + 128] = tiles[:, side * 4 + m].reshape(count, 128)
        first += count
    mine, others = wide[:, 512:640], wide[:, 0:512]
    all_s[...] = lax.dot_general(mine, others, TRANSPOSED, preferred_element_type=F32)
    for which, target in ((core, keep), (1 - core, give)):
        at = pl.multiple_of(which * 256, 256)
        for q in range(4):
            target[0:32, q * 256 : q * 256 + 256] = all_s[q * 32 : q * 32 + 32, pl.ds(at, 256)]
    at = pl.multiple_of((1 - core) * 16, 16)
    for q in range(2):
        give[32 + q * 16 : 48 + q * 16, :] = two[pl.ds(at, 16), q * 1024 : q * 1024 + 1024].astype(F32)


def panel(place, blocks, two):
    tiles = (block.reshape(-1, 8, 16, 128) for block in blocks)
    return pl.pallas_call(
        panel_kernel,
        out_shape=(
            jax.ShapeDtypeStruct((32, 1024), F32),
            jax.ShapeDtypeStruct((64, 1024), F32),
        ),
        in_specs=[SMEM] + [VMEM] * 6,
        out_specs=(VMEM, VMEM),
        scratch_shapes=[pltpu.VMEM((1024, 640), BF16), pltpu.VMEM((128, 512), F32)],
        compiler_params=grant(8),
        cost_estimate=pl.CostEstimate(flops=1 << 29, bytes_accessed=1 << 22, transcendentals=0),
        name="panel",
    )(place, *tiles, two)


def settle_kernel(place, eps_occ, keep, got, eps_vir, mine, out, bmat):
    tile, side, core, own = (place[n] for n in (0, 3, 4, 5))
    row_a = eps_vir[pl.ds(tile, 1), :]
    square = (128, 128)
    col_a = jnp.sum(jnp.where(lanes(square) == rows(square), row_a, 0.0), axis=1, keepdims=True)
    for m in range(2):
        j = side * 4 + core * 2 + m
        block = jnp.concatenate(
            [
                keep[0:32, q * 256 + m * 128 : q * 256 + m * 128 + 128]
                + got[0:32, q * 256 + m * 128 : q * 256 + m * 128 + 128]
                for q in range(4)
            ],
            axis=0,
        )
        denominators = (eps_occ[own] + eps_occ[j] - row_a) - col_a
        terms = block * (2.0 * block - block.T) / denominators
        out[m : m + 1, :] = jnp.sum(terms, axis=0, keepdims=True)
    here = pl.ds(pl.multiple_of(core * 16, 16), 16)
    bmat[here, :] = mine[here, :]
    there = pl.ds(pl.multiple_of((1 - core) * 16, 16), 16)
    for q in range(2):
        bmat[there, q * 1024 : q * 1024 + 1024] = got[32 + q * 16 : 48 + q * 16, :].astype(BF16)


def settle(place, eps_occ, keep, got, eps_vir, two):
    return pl.pallas_call(
        settle_kernel,
        out_shape=(jax.ShapeDtypeStruct((8, 128), F32), jax.ShapeDtypeStruct(two.shape, BF16)),
        in_specs=[SMEM, SMEM, VMEM, VMEM, VMEM, VMEM],
        out_specs=(VMEM, VMEM),
        compiler_params=grant(4),
        cost_estimate=pl.CostEstimate(flops=1 << 28, bytes_accessed=1 << 20, transcendentals=0),
        name="settle",
    )(place, eps_occ, keep, got, eps_vir.reshape(-1, 128), two)


def gram_kernel(place, here, below, above, low, high, sides, _, keep, give, wide, thin, all_t):
    core, x = place[4], place[6]
    first = 0
    for away, tiles in ((0, here), (3, below), (1, above), (2, low), (2, high)):
        count = tiles.shape[0] * 16
        for i in range(8):
            wide[first : first + count, i * 128 : i * 128 + 128] = tiles[:, i].reshape(count, 128)
        z = 4 if tiles is high else 0
        for p in range(4):
            rows_z = sides[z : z + count // 32, (x + away) & 3, :, p]
            thin[first : first + count, p * 128 : p * 128 + 128] = rows_z.reshape(count, 128)
        first += count
    for p in range(4):
        part = lax.dot_general(thin[:, p * 128 : p * 128 + 128], wide[...], TRANSPOSED, preferred_element_type=F32)
        all_t[p * 128 : p * 128 + 128, :] = part
    for which, target in ((core, keep), (1 - core, give)):
        for j in range(8):
            at = pl.multiple_of(j * 64 + which * 32, 32)
            target[j * 32 : j * 32 + 32, :] = all_t[pl.ds(at, 32), :]


def gram(place, blocks, sides, after):
    tiles = (block.reshape(-1, 8, 16, 128) for block in blocks)
    shape = jax.ShapeDtypeStruct((256, 1024), F32)
    return pl.pallas_call(
        gram_kernel,
        out_shape=(shape, shape),
        in_specs=[SMEM] + [VMEM] * 6 + [HBM],
        out_specs=(VMEM, VMEM),
        scratch_shapes=[
            pltpu.VMEM((1024, 1024), BF16),
            pltpu.VMEM((1024, 512), BF16),
            pltpu.VMEM((512, 1024), F32),
        ],
        compiler_params=grant(16),
        name="gram",
    )(place, *tiles, sides.reshape(8, 4, 2, 4, 16, 128), after)


def energy_kernel(scale, place, eps_occ, keep, got, eps_vir, selfs, out, parts):
    tile, other, step, side, core, own = (place[n] for n in range(6))
    row_a = eps_vir[pl.ds(tile, 1), :]
    row_b = eps_vir[pl.ds(other, 1), :]
    first = side * 64 + core * 32
    col_b = jnp.sum(jnp.where(lanes((32, 128)) == rows((32, 128)) + first, row_b, 0.0), axis=1, keepdims=True)
    weight = jnp.where(step == 8, 1.0, 2.0)
    for i in range(8):
        for j in range(i, 8):
            there = slice(j * 32, j * 32 + 32), slice(i * 128, i * 128 + 128)
            here = slice(i * 32, i * 32 + 32), slice(j * 128, j * 128 + 128)
            one = keep[there] + got[there]
            two = keep[here] + got[here]
            denominators = (eps_occ[i] + eps_occ[j] - row_a) - col_b
            terms = (one * one + two * two - one * two) / denominators
            part = jnp.sum(terms, axis=0, keepdims=True) * weight
            parts[i * 8 + j : i * 8 + j + 1, :] = part
            parts[j * 8 + i : j * 8 + i + 1, :] = part
    for m in range(2):
        at = pl.ds(own * 8 + side * 4 + core * 2 + m, 1)
        parts[at, :] = parts[at, :] + selfs[m : m + 1, :]
    column = jnp.sum(parts[...], axis=1, keepdims=True) * scale
    row = jnp.sum(jnp.where(lanes((64, 128)) == rows((64, 128)), column, 0.0), axis=0, keepdims=True)
    out[...] = jnp.broadcast_to(row[None], out.shape)


def energies(scale, place, eps_occ, keep, got, eps_vir, selfs):
    return pl.pallas_call(
        functools.partial(energy_kernel, scale),
        out_shape=jax.ShapeDtypeStruct((32, 1, 128), F32),
        in_specs=[SMEM, SMEM, VMEM, VMEM, VMEM, VMEM],
        out_specs=VMEM,
        scratch_shapes=[pltpu.VMEM((64, 128), F32)],
        compiler_params=grant(6),
        name="energies",
    )(place, eps_occ, keep, got, eps_vir.reshape(-1, 128), selfs)


def position():
    zh, zl, x, yl, yh, core = (lax.axis_index(axis) for axis in AXES)
    tile, kind = zh * 4 + zl * 2 + yl, x * 4 + yh
    step, side = lax.shift_right_logical(kind, 1) + 1, kind & 1
    return jnp.stack([tile, (tile + step) & (TILES - 1), step, side, core, lax.shift_right_logical(kind, 1), x])


def again_kernel(got, out):
    out[...] = jnp.broadcast_to(jnp.sum(got[...], axis=0)[None], out.shape)


def last_kernel(got, out):
    row = jnp.broadcast_to(jnp.sum(got[...], axis=0), (8, 128))
    place = rows((8, 128))
    square = row
    for i in range(1, 8):
        square = jnp.where(place == i, pltpu.roll(row, 128 - 8 * i, 1), square)
    out[...] = square[:, :8]


def small(kernel, shape, name):
    return pl.pallas_call(
        kernel,
        out_shape=jax.ShapeDtypeStruct(shape, F32),
        in_specs=[VMEM],
        out_specs=VMEM,
        compiler_params=grant(2),
        name=name,
    )


def body(c_occ, c_vir, ints, blocks, screen, eps_occ, eps_vir):
    vir, occ = c_vir.shape[1], c_occ.shape[1]
    place = position()
    sent = half_transform(c_occ, ints, blocks, screen)
    recv = lax.all_to_all(sent, GRP, 0, 0, tiled=True)
    two, wide, thin = transform(recv, hold(c_vir))
    here = lax.all_to_all(wide, ("zh", "zl", "yl", "yh"), 0, 0, tiled=True)
    up = [(i, (i + 1) % 4) for i in range(4)]
    down = [(i, (i + 3) % 4) for i in range(4)]
    below, above = lax.ppermute(here, "x", up), lax.ppermute(here, "x", down)
    low, high = onward(below, above)
    low, high = lax.ppermute(low, "x", down), lax.ppermute(high, "x", up)
    sides = lax.all_to_all(thin, CHIPS, 0, 0, tiled=True)

    swap = [(0, 1), (1, 0)]
    blocks = (here, below, above, low, high)
    keep, give = panel(place, blocks, two)
    other = lax.ppermute(give, "core", swap)
    selfs, bmat = settle(place, eps_occ, keep, other, eps_vir, two)
    keep, give = gram(place, blocks, sides, other)
    got = lax.ppermute(give, "core", swap)
    scale = 1.0 / (float(vir) * float(vir) * 2048.0)
    energy = energies(scale, place, eps_occ, keep, got, eps_vir, selfs)
    energy = lax.all_to_all(energy, NEAR, 0, 0, tiled=True)
    energy = lax.all_to_all(small(again_kernel, (16, 1, 128), "again")(energy), FAR, 0, 0, tiled=True)
    energy = small(last_kernel, (occ, occ), "last")(energy)
    return bmat.reshape(1, 32, vir), energy


def solution(mesh):
    fine = Mesh(mesh.devices.reshape(4, 2, 4, 2, 4, 2), AXES)
    return jax.shard_map(
        body,
        mesh=fine,
        in_specs=(P(), P(), P(GRP, PAIR, None), P(GRP, None), P(GRP), P(), P()),
        out_specs=(P(GRP, PAIR, None), P()),
        check_vma=False,
    )
```
